32 devices in a mesh: rows: 16 (over z, y, x), blk: 2 (over core).
Axes of the slice: x: 2, y: 2, z: 4, core: 2. Of those that a mesh axis runs over, the one named last changes fastest.
Arguments:
- tokens: bfloat16 [64, 512, 768], P(('rows', 'blk')), may hold values from -6 to 6
- lengths: int32 [64, 8], P(('rows', 'blk')), may hold values from 1 to 505, as said below
- attn_gain: bfloat16 [768], replicated, may hold values from 0.5 to 1.5
- w_query: bfloat16 [768, 768], replicated, may hold values from -0.0546875 to 0.0546875
- w_key: bfloat16 [768, 768], replicated, may hold values from -0.21875 to 0.21875
- w_value: bfloat16 [768, 768], replicated, may hold values from -0.21875 to 0.21875
- w_output: bfloat16 [768, 768], replicated, may hold values from -0.625 to 0.625
- bucket_bias_table: bfloat16 [32, 12], replicated, may hold values from -4 to 4
- ffn_gain: bfloat16 [768], replicated, may hold values from 0.5 to 1.5
- w_in: bfloat16 [768, 3072], replicated, may hold values from -0.21875 to 0.21875
- w_out: bfloat16 [3072, 768], replicated, may hold values from -0.15625 to 0.15625
- out_grad: bfloat16 [64, 512, 768], P(('rows', 'blk')), may hold values from -6 to 6
Outputs:
- mixed: bfloat16 [64, 512, 768], P(('rows', 'blk'))
- tokens_grad: bfloat16 [64, 512, 768], P(('rows', 'blk'))
- attn_gain_grad: float32 [768], replicated
- w_query_grad: float32 [768, 768], replicated
- w_key_grad: float32 [768, 768], replicated
- w_value_grad: float32 [768, 768], replicated
- w_output_grad: float32 [768, 768], replicated
- bias_table_grad: float32 [32, 12], replicated
- ffn_gain_grad: float32 [768], replicated
- w_in_grad: float32 [768, 3072], replicated
- w_out_grad: float32 [3072, 768], replicated
The draws below stay inside these ranges and needn't reach their ends.
Inputs may be any that keep to these rules, and one draw needn't show every extreme that they name: `lengths`: each row's 8 entries are positive and sum to 512; the first 7 are query-passage pairs, the last is a padding run of at most 25 tokens (row 1 has exactly that many).
All inputs are finite; a program needn't handle non-finite values.
Results may differ from the reference program's by a relative error of at most 0.014.
The reference program's roundings to bfloat16 on the way count: a program that leaves them out, or rounds other values in their place, can miss the bound.
Values sent between devices are 32-bit elements; how exact they have to be, the bound alone decides.
No kernel may reach another device: no remote copies, remote signals or barrier semaphores. Data moves between devices by JAX's collectives and lax.ppermute only.
A program may use at most 320 MiB of HBM per device.

```python
import math
import jax
import jax.numpy as jnp
import numpy as np
from jax import lax

D = 768
HEADS = 12
FF = 3072
BUCKETS = 32
SEQ = 512
SEGS = 8
ROWS = 64


def draw_lengths(key, part):
    key = jax.random.fold_in(key, 7)
    cut_key, pad_key = jax.random.split(key, 2)
    spare = SEQ // 20
    count = SEQ - spare - 2

    def one_row(row_key):
        order = jax.random.permutation(row_key, count)[:SEGS - 2] + 1
        cuts = jnp.where(order >= SEQ // 2, order + 1, order)
        return jnp.sort(cuts).astype(jnp.int32)
    cut_rows = jax.vmap(one_row)(jax.random.split(cut_key, ROWS))
    row_ids = jnp.arange(ROWS, dtype=jnp.int32)
    fixed_cuts = jnp.arange(1, SEGS - 1, dtype=jnp.int32)[None, :]
    cut_rows = jnp.where((row_ids == 0)[:, None], fixed_cuts, cut_rows).astype(jnp.int32)
    padding = jax.random.randint(pad_key, (ROWS,), 1, spare + 1)
    padding = jnp.where(row_ids == 1, spare, padding)
    padding = jnp.where(row_ids == 0, 1, padding).astype(jnp.int32)
    bounds = jnp.concatenate([jnp.zeros((ROWS, 1), jnp.int32), cut_rows, (SEQ - padding)[:, None]], axis=1)
    pairs = bounds[:, 1:] - bounds[:, :-1]
    return jnp.concatenate([pairs, padding[:, None]], axis=1).astype(jnp.int32)


def levels(stream_key, extent, shards, smallest, largest):
    level, own = 1.0, jax.random.fold_in(stream_key, 6)
    for axis_at, shards_of in shards:
        steps = jnp.exp(jax.random.uniform(jax.random.fold_in(own, axis_at), (shards_of,), jnp.float32, smallest / len(shards), largest / len(shards)))
        level = level * jnp.repeat(steps, extent[axis_at] // shards_of).reshape([-1 if axis == axis_at else 1 for axis in range(len(extent))])
    return level


def centred(rng, extent, spread, limit, shards=(), held_as=jnp.bfloat16):
    entries = jax.random.normal(rng, extent, jnp.float32) * spread
    if len(shards) > 0:
        entries = levels(rng, extent, shards, -0.22, 0.18) * entries
    return jnp.clip(entries, min=-limit, max=limit).astype(held_as)


def setup_inputs(seed: int = 0) -> dict:
    key_of = jax.random.split(jax.random.key(seed), 13)
    return {
        "tokens": centred(key_of[0], (ROWS, SEQ, D), 1.0, 6.0, ((0, 32),)),
        "lengths": draw_lengths(jax.random.fold_in(key_of[12], 71), 0),
        "attn_gain": jnp.clip(1.0 + 0.1 * jax.random.normal(key_of[2], (D,), jnp.float32), 0.5, 1.5).astype(jnp.bfloat16),
        "w_query": centred(key_of[3], (D, D), (16 * D) ** -0.5, 0.0546875),
        "w_key": centred(key_of[4], (D, D), D ** -0.5, 0.21875),
        "w_value": centred(key_of[5], (D, D), D ** -0.5, 0.21875),
        "w_output": centred(key_of[6], (D, D), (D // 8) ** -0.5, 0.625),
        "bucket_bias_table": centred(key_of[7], (BUCKETS, HEADS), 1.0, 4.0),
        "ffn_gain": jnp.clip(1.0 + 0.1 * jax.random.normal(key_of[8], (D,), jnp.float32), 0.5, 1.5).astype(jnp.bfloat16),
        "w_in": centred(key_of[9], (D, FF), D ** -0.5, 0.21875),
        "w_out": centred(key_of[10], (FF, D), (FF // 2) ** -0.5, 0.15625),
        "out_grad": centred(key_of[11], (ROWS, SEQ, D), 1.0, 6.0, ((0, 32),)),
    }


far_steps = np.array([12, 16, 23, 32, 46, 64, 91], dtype=np.int32)
highest_precision = lax.Precision.HIGHEST

@jax.custom_vjp
def low(v):
    return lax.optimization_barrier(v.astype(jnp.bfloat16)).astype(jnp.float32)

@jax.custom_vjp
def low_back(v):
    return v

def low_keep(v):
    return (low(v), None)

def low_pass(kept, grad):
    return (grad,)

def back_keep(v):
    return (v, None)

def back_low(kept, grad):
    return (low(grad),)
low.defvjp(low_keep, low_pass)
low_back.defvjp(back_keep, back_low)

def rounded_both(value):
    return low_back(low(value))

def bucket_of(relative, bucket_count):
    distance = jnp.abs(relative).astype(jnp.int32)
    beyond = lax.optimization_barrier(jnp.sum((distance[..., None] >= jnp.asarray(far_steps)).astype(jnp.int32), axis=-1)).astype(jnp.int32)
    inner = jnp.where(distance < bucket_count // 4, distance, bucket_count // 4 + beyond)
    return (jnp.where(relative > 0, bucket_count // 2, 0) + inner).astype(jnp.int32)

def segment_of(lengths, positions):
    ends = jnp.cumsum(lengths, axis=-1).astype(jnp.int32)
    return lax.optimization_barrier(jnp.sum((positions[None, :, None] >= ends[:, None, :]).astype(jnp.int32), axis=-1)).astype(jnp.int32)

def norm_rows(value, gain):
    return value * lax.rsqrt(lax.optimization_barrier(jnp.mean(value * value, axis=-1, keepdims=True)) + 1e-06) * gain

def layer(tokens, attn_gain, w_query, w_key, w_value, w_output, bucket_bias_table, ffn_gain, w_in, w_out, allowed, valid, bucket_indicator):
    group, length, width = tokens.shape
    head_count = bucket_bias_table.shape[1]
    head_size = width // head_count
    hidden_one = low(norm_rows(tokens, attn_gain))

    def project(weight):
        made = jnp.einsum('rtd,de->rte', hidden_one, weight, precision=highest_precision)
        return rounded_both(made).reshape(group, length, head_count, head_size)
    queries = project(w_query)
    keys = project(w_key)
    values = project(w_value)
    products = low_back(jnp.einsum('rqhd,rkhd->rhqk', queries, keys, precision=highest_precision))
    position_bias = jnp.einsum('ced,ci->ied', bucket_indicator, bucket_bias_table, precision=highest_precision)
    scores = products + position_bias[None] + jnp.where(allowed, 0.0, -1000000000.0)[:, None]
    exponent = jnp.exp(scores - lax.optimization_barrier(jnp.max(scores, axis=-1, keepdims=True)))
    attention = exponent / lax.optimization_barrier(jnp.sum(exponent, axis=-1, keepdims=True))
    attended = jnp.einsum('rhqk,rkhd->rqhd', low(attention), values, precision=highest_precision).reshape(group, length, width)
    attended = rounded_both(attended * valid[..., None])
    residual = tokens + low_back(jnp.einsum('rtd,de->rte', attended, w_output, precision=highest_precision))
    hidden_two = low(norm_rows(residual, ffn_gain))
    pre_act = low_back(jnp.einsum('rtd,df->rtf', hidden_two, w_in, precision=highest_precision))
    activated = low(jax.nn.gelu(pre_act, approximate=True))
    return residual + jnp.einsum('rtf,fd->rtd', activated, w_out, precision=highest_precision)

def reference(tokens, lengths, attn_gain, w_query, w_key, w_value, w_output, bucket_bias_table, ffn_gain, w_in, w_out, out_grad):
    weights = tuple((item.astype(jnp.float32) for item in (attn_gain, w_query, w_key, w_value, w_output, bucket_bias_table, ffn_gain, w_in, w_out)))
    group = math.gcd(ROWS, max(1, 4096 // SEQ))
    step_count = ROWS // group
    positions = jnp.arange(SEQ, dtype=jnp.int32)
    buckets = bucket_of(positions[None, :] - positions[:, None], BUCKETS)
    bucket_indicator = (buckets[None] == jnp.arange(BUCKETS, dtype=jnp.int32)[:, None, None]).astype(jnp.float32)

    def advance(totals, pieces):
        block_tokens, block_lengths, block_grad = pieces
        segment = segment_of(block_lengths, positions)
        valid_key = segment < SEGS - 1
        allowed = (segment[:, :, None] == segment[:, None, :]) & valid_key[:, None, :]
        valid = valid_key.astype(jnp.float32)

        def forward(inputs, *params):
            return layer(inputs, *params, allowed, valid, bucket_indicator)
        output, pull = jax.vjp(forward, block_tokens.astype(jnp.float32), *weights)
        grads = pull(block_grad.astype(jnp.float32))
        totals = tuple((total + grad for total, grad in zip(totals, grads[1:])))
        return (totals, (output.astype(jnp.bfloat16), grads[0].astype(jnp.bfloat16)))
    start = tuple((jnp.zeros(item.shape, jnp.float32) for item in weights))
    totals, (outputs, input_grads) = lax.scan(advance, start, (tokens.reshape(step_count, group, SEQ, D), lengths.reshape(step_count, group, SEGS), out_grad.reshape(step_count, group, SEQ, D)))
    return (outputs.reshape(ROWS, SEQ, D), input_grads.reshape(ROWS, SEQ, D), totals[0], totals[1], totals[2], totals[3], totals[4], totals[5], totals[6], totals[7], totals[8])
```

```python
import functools
import jax
import jax.numpy as jnp
import numpy as np
from jax import lax
from jax.experimental import pallas as pl
from jax.experimental.pallas import tpu as pltpu
from jax.sharding import PartitionSpec as P

NT = (((1,), (1,)), ((), ()))
TN = (((0,), (0,)), ((), ()))
F32, BF16 = jnp.float32, jnp.bfloat16
TILE = 128
MASKED = -1000000000.0
EPS = 1e-06
far_steps = np.array([12, 16, 23, 32, 46, 64, 91], dtype=np.int32)


def dot(a, b, dims=None):
    if dims is None:
        return jnp.dot(a, b, preferred_element_type=F32)
    return lax.dot_general(a, b, dims, preferred_element_type=F32)


def bucket_of(relative, bucket_count):
    distance = np.abs(relative)
    beyond = np.sum(distance[..., None] >= far_steps, axis=-1)
    inner = np.where(distance < bucket_count // 4, distance, bucket_count // 4 + beyond)
    return np.where(relative > 0, bucket_count // 2, 0) + inner


def band_buckets(bucket_count):
    lanes = np.arange(4 * TILE)
    offsets = np.where(lanes < 2 * TILE, lanes, lanes - 4 * TILE)
    return bucket_of(-offsets, bucket_count)


def segments_along(len_ref, row, shape, axis):
    at = lax.broadcasted_iota(jnp.int32, shape, axis)
    total = jnp.zeros(shape, jnp.int32)
    end = jnp.int32(0)
    for j in range(len_ref.shape[1]):
        end = end + len_ref[row, j]
        total = total + jnp.where(at >= end, 1, 0)
    return total


def fill_mask(len_ref, row, mask_ref, last):
    seq = mask_ref.shape[0]
    of_q = segments_along(len_ref, row, (1, seq), 1)
    of_k = segments_along(len_ref, row, (seq, TILE), 0)
    of_k = jnp.where(of_k < last, of_k, -1)
    for j in range(seq // TILE):
        same = of_k == of_q[:, j * TILE : (j + 1) * TILE]
        mask_ref[:, j * TILE : (j + 1) * TILE] = jnp.where(same, 0.0, MASKED)
    return of_q < last


def band_of(vector):
    wide = jnp.broadcast_to(vector, (TILE, 4 * TILE))
    return pltpu.roll(wide, 0, 1, stride=1, stride_axis=0)


def bias_row(band, vector, ki, count):
    shape = (TILE, TILE)
    tiles = []
    for qi in range(count):
        step = ki - qi
        if step == 0:
            tiles.append(band[:, 0:TILE])
        elif step == -1:
            tiles.append(band[:, TILE : 2 * TILE])
        elif step == 1:
            tiles.append(band[:, 3 * TILE : 4 * TILE])
        elif step < 0:
            tiles.append(jnp.broadcast_to(vector[:, 2 * TILE - 1 : 2 * TILE], shape))
        else:
            tiles.append(jnp.broadcast_to(vector[:, 2 * TILE : 2 * TILE + 1], shape))
    return jnp.concatenate(tiles, axis=1)


def norm_scale(value):
    return lax.rsqrt(jnp.mean(value * value, axis=-1, keepdims=True) + EPS)


def attn_fwd_kernel(
    len_ref, tok_ref, gain1_ref, gain2_ref, wq_ref, wk_ref, wv_ref, wo_ref, band_ref,
    h1_ref, q_ref, k_ref, v_ref, att_ref, attT_ref, lse_ref, x1_ref, h2_ref,
    mask_ref, s_ref, p_ref,
):
    seq, width = tok_ref.shape[1:]
    heads = band_ref.shape[0]
    head = width // heads
    row = pl.program_id(0)
    valid = fill_mask(len_ref, row, mask_ref, len_ref.shape[1] - 1)
    tok = tok_ref[0].astype(F32)
    h1 = (tok * norm_scale(tok) * gain1_ref[...].astype(F32)).astype(BF16)
    h1_ref[0] = h1
    q_ref[0] = dot(h1, wq_ref[...]).astype(BF16)
    k_ref[0] = dot(h1, wk_ref[...]).astype(BF16)
    v_ref[0] = dot(h1, wv_ref[...]).astype(BF16)
    count = seq // TILE
    low_half = lax.broadcasted_iota(jnp.int32, (1, TILE), 1) < head

    def pair(p, carry):
        lanes = pl.ds(pl.multiple_of(p * TILE, TILE), TILE)
        qp, kp, vp = q_ref[0, :, lanes], k_ref[0, :, lanes], v_ref[0, :, lanes]
        vT = vp.T
        outs = []
        for a in range(2):
            qm = jnp.where(low_half if a == 0 else ~low_half, qp, jnp.zeros_like(qp))
            vector = band_ref[pl.ds(2 * p + a, 1), :]
            band = band_of(vector)
            top = None
            for ki in range(count):
                rows = slice(ki * TILE, (ki + 1) * TILE)
                s = dot(kp[rows], qm, NT) + bias_row(band, vector, ki, count) + mask_ref[rows, :]
                s_ref[a, rows, :] = s
                most = jnp.max(s, axis=0, keepdims=True)
                top = most if top is None else jnp.maximum(top, most)
            total = jnp.zeros_like(top)
            for ki in range(count):
                rows = slice(ki * TILE, (ki + 1) * TILE)
                e = jnp.exp(s_ref[a, rows, :] - top)
                total = total + jnp.sum(e, axis=0, keepdims=True)
                p_ref[a, rows, :] = e.astype(BF16)
            o = dot(vT[a * head : (a + 1) * head], p_ref[a])
            o = jnp.where(valid, o / total, 0.0)
            outs.append(o)
            lse_ref[0, pl.ds(2 * p + a, 1), :] = top + jnp.log(total)
        both = jnp.concatenate(outs, axis=0)
        attT_ref[0, lanes, :] = both.astype(BF16)
        att_ref[0, :, lanes] = both.T.astype(BF16)
        return carry

    lax.fori_loop(0, heads // 2, pair, 0)
    x1 = tok_ref[0].astype(F32) + dot(att_ref[0], wo_ref[...])
    x1_ref[0] = x1
    h2_ref[0] = (x1 * norm_scale(x1) * gain2_ref[...].astype(F32)).astype(BF16)


VMEM = 60 * 2**20


def params(**kw):
    return pltpu.CompilerParams(vmem_limit_bytes=VMEM, **kw)


def attn_fwd(tokens, lengths, gain1, gain2, wq, wk, wv, wo, band):
    rows, seq, width = tokens.shape
    heads = band.shape[0]
    full = lambda a: pl.BlockSpec(a.shape, lambda r, l: (0,) * a.ndim)
    per_row = lambda *s: pl.BlockSpec((1,) + s, lambda r, l: (r,) + (0,) * len(s))
    tall = jax.ShapeDtypeStruct((rows, seq, width), BF16)
    outs = [tall] * 5 + [
        jax.ShapeDtypeStruct((rows, width, seq), BF16),
        jax.ShapeDtypeStruct((rows, heads, seq), F32),
        jax.ShapeDtypeStruct((rows, seq, width), F32),
        tall,
    ]
    return pl.pallas_call(
        attn_fwd_kernel,
        grid_spec=pltpu.PrefetchScalarGridSpec(
            num_scalar_prefetch=1,
            grid=(rows,),
            in_specs=[per_row(seq, width), full(gain1), full(gain2), full(wq), full(wk), full(wv), full(wo), full(band)],
            out_specs=[per_row(seq, width)] * 5 + [per_row(width, seq), per_row(heads, seq), per_row(seq, width), per_row(seq, width)],
            scratch_shapes=[
                pltpu.VMEM((seq, seq), F32),
                pltpu.VMEM((2, seq, seq), F32),
                pltpu.VMEM((2, seq, seq), BF16),
            ],
        ),
        out_shape=outs,
        compiler_params=params(),
        name="attn_fwd",
    )(lengths, tokens, gain1, gain2, wq, wk, wv, wo, band)


GELU_C = float(np.sqrt(2.0 / np.pi))


def gelu_pair(v):
    v2 = v * v
    t = jnp.tanh(GELU_C * v * (1.0 + 0.044715 * v2))
    half = 0.5 * (1.0 + t)
    slope = half + (0.5 * GELU_C) * v * (1.0 - t * t) * (1.0 + (3 * 0.044715) * v2)
    return v * half, slope


def place(core, mine, other, keep, send, sems):
    return [
        (core == 0, [pltpu.make_async_copy(mine, keep, sems.at[0]), pltpu.make_async_copy(other, send, sems.at[1])]),
        (core != 0, [pltpu.make_async_copy(mine, send, sems.at[0]), pltpu.make_async_copy(other, keep, sems.at[1])]),
    ]


def start_all(cases):
    for condition, copies in cases:

        @pl.when(condition)
        def _():
            for copy in copies:
                copy.start()


def wait_all(cases):
    for condition, copies in cases:

        @pl.when(condition)
        def _():
            for copy in copies:
                copy.wait()


def ffn_kernel(first, steps, core_ref, h2_ref, dy_ref, win_ref, wout_ref, *refs):
    if first:
        keep_ref, send_ref, mix_ref, dtwo_ref, h2T_ref, gin_ref, gout_ref, sems = refs
    else:
        mix0_ref, dtwo0_ref, keep_ref, send_ref, mix_ref, dtwo_ref, h2T_ref, gin_ref, gout_ref, sems = refs
    step = pl.program_id(0)
    h2, dy = h2_ref[...], dy_ref[...]
    width = h2.shape[1]
    sub = win_ref.shape[1]
    size = gin_ref.shape[1]

    def moves(at):
        rows = pl.ds(pl.multiple_of(at * size, size), size)
        return place(core_ref[0], gin_ref.at[at], gout_ref.at[at], keep_ref.at[rows, :], send_ref.at[rows, :], sems.at[at])

    @pl.when(step == 0)
    def _():
        h2T_ref[...] = h2_ref[...].T

    pre = dot(h2, win_ref[...])
    act, slope = gelu_pair(pre)
    act = act.astype(BF16)
    gout = dot(act, dy, TN)
    for j in range(width // 256):
        gout_ref[step, j * sub : (j + 1) * sub, :] = gout[:, j * 256 : (j + 1) * 256]
    dpre = (dot(dy, wout_ref[...], NT) * slope).astype(BF16)
    gin = dot(h2T_ref[...], dpre)
    for j in range(sub // 256):
        gin_ref[step, j * width : (j + 1) * width, :] = gin[:, j * 256 : (j + 1) * 256]
    start_all(moves(step))
    mix = dot(act, wout_ref[...])
    dtwo = dot(dpre, win_ref[...], NT)

    @pl.when(step == 0)
    def _():
        mix_ref[...] = mix if first else mix0_ref[...] + mix
        dtwo_ref[...] = dtwo if first else dtwo0_ref[...] + dtwo

    @pl.when(step > 0)
    def _():
        mix_ref[...] += mix
        dtwo_ref[...] += dtwo

    @pl.when(step == steps - 1)
    def _():
        for at in range(steps):
            wait_all(moves(at))


def ffn_chunk(core, h2, dy, w_in, w_out, start, size, sub, acc=None):
    toks, width = h2.shape
    first = acc is None
    base = start // sub
    steps = size // sub
    piece = width * (sub // 256)
    full = lambda a: pl.BlockSpec(a.shape, lambda s, c: (0,) * a.ndim)
    in_specs = [full(h2), full(dy), pl.BlockSpec((width, sub), lambda s, c: (0, base + s)), pl.BlockSpec((sub, width), lambda s, c: (base + s, 0))]
    args = [core, h2, dy, w_in, w_out]
    aliases = {}
    if not first:
        in_specs += [full(acc[0]), full(acc[1])]
        args += list(acc)
        aliases = {5: 2, 6: 3}
    return pl.pallas_call(
        functools.partial(ffn_kernel, first, steps),
        grid_spec=pltpu.PrefetchScalarGridSpec(
            num_scalar_prefetch=1,
            grid=(steps,),
            in_specs=in_specs,
            out_specs=[
                pl.BlockSpec(memory_space=pl.ANY),
                pl.BlockSpec(memory_space=pl.ANY),
                pl.BlockSpec((toks, width), lambda s, c: (0, 0)),
                pl.BlockSpec((toks, width), lambda s, c: (0, 0)),
            ],
            scratch_shapes=[
                pltpu.VMEM((width, toks), BF16),
                pltpu.VMEM((steps, piece, 256), F32),
                pltpu.VMEM((steps, piece, 256), F32),
                pltpu.SemaphoreType.DMA((steps, 2)),
            ],
        ),
        out_shape=[jax.ShapeDtypeStruct((steps * piece, 256), F32)] * 2 + [jax.ShapeDtypeStruct((toks, width), F32)] * 2,
        input_output_aliases=aliases,
        compiler_params=params(),
        name="ffn",
    )(*args)


def resid_kernel(len_ref, x1_ref, mix_ref, dtwo_ref, dy_ref, gain_ref, attT_ref, wo_ref,
                 mixed_ref, dres_ref, datt_ref, gwo_ref, ggain_ref):
    step = pl.program_id(0)
    x1, dtwo = x1_ref[0], dtwo_ref[0]
    mixed_ref[0] = (x1 + mix_ref[0]).astype(BF16)
    s = norm_scale(x1)
    g = gain_ref[...].astype(F32) * dtwo
    dres = dy_ref[0].astype(F32) + s * g - x1 * (s * s * s * jnp.mean(x1 * g, axis=-1, keepdims=True))
    dres_ref[0] = dres
    dbranch = dres.astype(BF16)
    ggain = jnp.sum(dtwo * x1 * s, axis=0, keepdims=True)
    gwo = dot(attT_ref[0], dbranch)
    stripes = gwo_ref.shape[0]
    seq = x1.shape[0]
    seg = segments_along(len_ref, step, (seq, TILE), 0)[:, :1]
    datt = dot(dbranch, wo_ref[...], NT)
    datt_ref[0] = jnp.where(seg < len_ref.shape[1] - 1, datt, 0.0).astype(BF16)

    @pl.when(step == 0)
    def _():
        ggain_ref[...] = ggain
        for j in range(stripes):
            gwo_ref[j] = gwo[:, j * 256 : (j + 1) * 256]

    @pl.when(step > 0)
    def _():
        ggain_ref[...] += ggain
        for j in range(stripes):
            gwo_ref[j] += gwo[:, j * 256 : (j + 1) * 256]


def resid_bwd(lengths, x1, mix, dtwo, dy, gain, attT, wo):
    rows, seq, width = x1.shape
    full = lambda a: pl.BlockSpec(a.shape, lambda r, l: (0,) * a.ndim)
    tall = pl.BlockSpec((1, seq, width), lambda r, l: (r, 0, 0))
    return pl.pallas_call(
        resid_kernel,
        grid_spec=pltpu.PrefetchScalarGridSpec(
            num_scalar_prefetch=1,
            grid=(rows,),
            in_specs=[tall, tall, tall, tall, full(gain), pl.BlockSpec((1, width, seq), lambda r, l: (r, 0, 0)), full(wo)],
            out_specs=[tall, tall, tall, pl.BlockSpec((width // 256, width, 256), lambda r, l: (0, 0, 0)), pl.BlockSpec((1, width), lambda r, l: (0, 0))],
        ),
        out_shape=[
            jax.ShapeDtypeStruct((rows, seq, width), BF16),
            jax.ShapeDtypeStruct((rows, seq, width), F32),
            jax.ShapeDtypeStruct((rows, seq, width), BF16),
            jax.ShapeDtypeStruct((width // 256, width, 256), F32),
            jax.ShapeDtypeStruct((1, width), F32),
        ],
        compiler_params=params(),
        name="resid_bwd",
    )(lengths, x1, mix, dtwo, dy, gain, attT, wo)


def diagonal_sums(x):
    depth, lanes = x.shape
    total = x[0:8]
    for g in range(8, depth, 8):
        total = total + pltpu.roll(x[g : g + 8], lanes - g, 1)
    at = lax.broadcasted_iota(jnp.int32, (8, lanes), 0)
    for bit in (1, 2, 4):
        total = jnp.where((at & bit) != 0, pltpu.roll(total, lanes - bit, 1), total)
    return jnp.sum(total, axis=0, keepdims=True)


def attn_bwd_kernel(len_ref, q_ref, k_ref, v_ref, do_ref, lse_ref, band_ref,
                    dq_ref, dk_ref, dv_ref, diag_ref,
                    mask_ref, p_ref, pl_ref, dp_ref, ds_ref, near_ref, far_ref):
    pair, row = pl.program_id(0), pl.program_id(1)
    seq = q_ref.shape[1]
    head = TILE // 2
    count = seq // TILE
    fill_mask(len_ref, row, mask_ref, len_ref.shape[1] - 1)
    low_half = lax.broadcasted_iota(jnp.int32, (1, TILE), 1) < head
    qp, kp, vp, dop = q_ref[0], k_ref[0], v_ref[0], do_ref[0]
    kT = kp.T

    @pl.when(row == 0)
    def _():
        near_ref[...] = jnp.zeros_like(near_ref)
        far_ref[...] = jnp.zeros_like(far_ref)

    dqT, dk, dv = [], None, None
    for a in range(2):
        own = low_half if a == 0 else ~low_half
        qm = jnp.where(own, qp, jnp.zeros_like(qp))
        dom = jnp.where(own, dop, jnp.zeros_like(dop))
        vector = band_ref[0, a : a + 1, :]
        band = band_of(vector)
        lse = lse_ref[0, 0, a : a + 1, :]
        delta = jnp.zeros((1, seq), F32)
        for ki in range(count):
            rows = slice(ki * TILE, (ki + 1) * TILE)
            s = dot(kp[rows], qm, NT) + bias_row(band, vector, ki, count) + mask_ref[rows, :]
            prob = jnp.exp(s - lse)
            dp = dot(vp[rows], dom, NT)
            delta = delta + jnp.sum(prob * dp, axis=0, keepdims=True)
            p_ref[a, rows, :] = prob
            pl_ref[a, rows, :] = prob.astype(BF16)
            dp_ref[a, rows, :] = dp
        for ki in range(count):
            rows = slice(ki * TILE, (ki + 1) * TILE)
            ds = p_ref[a, rows, :] * (dp_ref[a, rows, :] - delta)
            ds_ref[a, rows, :] = ds.astype(BF16)
            for qi in range(count):
                tile = ds[:, qi * TILE : (qi + 1) * TILE]
                step = ki - qi
                if abs(step) <= 1:
                    at = (0 if step == 0 else 1 if step == -1 else 3) * TILE
                    near_ref[a, :, at : at + TILE] += tile
                else:
                    at = 0 if step < 0 else TILE
                    far_ref[a, :, at : at + TILE] += tile
        dva = dot(pl_ref[a], dom)
        dka = dot(ds_ref[a], qm)
        dv = dva if dv is None else dv + dva
        dk = dka if dk is None else dk + dka
        dqT.append(dot(kT[a * head : (a + 1) * head], ds_ref[a]))
    dv_ref[0] = dv.astype(BF16)
    dk_ref[0] = dk.astype(BF16)
    dq_ref[0] = jnp.concatenate(dqT, axis=0).T.astype(BF16)

    @pl.when(row == pl.num_programs(1) - 1)
    def _():
        for a in range(2):
            diag_ref[0, a : a + 1, : 4 * TILE] = diagonal_sums(near_ref[a])
            diag_ref[0, a : a + 1, 4 * TILE :] = jnp.sum(far_ref[a], axis=0, keepdims=True)


def attn_bwd(lengths, q, k, v, do, lse, band):
    rows, seq, width = q.shape
    pairs = width // TILE
    lse = lse.reshape(rows, pairs, 2, seq)
    band = band.reshape(pairs, 2, band.shape[1])
    tall = pl.BlockSpec((1, seq, TILE), lambda p, r, l: (r, 0, p))
    out = jax.ShapeDtypeStruct((rows, seq, width), BF16)
    return pl.pallas_call(
        attn_bwd_kernel,
        grid_spec=pltpu.PrefetchScalarGridSpec(
            num_scalar_prefetch=1,
            grid=(pairs, rows),
            in_specs=[tall] * 4 + [pl.BlockSpec((1, 1, 2, seq), lambda p, r, l: (r, p, 0, 0)), pl.BlockSpec((1, 2, 4 * TILE), lambda p, r, l: (p, 0, 0))],
            out_specs=[tall] * 3 + [pl.BlockSpec((1, 2, 6 * TILE), lambda p, r, l: (p, 0, 0))],
            scratch_shapes=[
                pltpu.VMEM((seq, seq), F32),
                pltpu.VMEM((2, seq, seq), F32),
                pltpu.VMEM((2, seq, seq), BF16),
                pltpu.VMEM((2, seq, seq), F32),
                pltpu.VMEM((2, seq, seq), BF16),
                pltpu.VMEM((2, TILE, 4 * TILE), F32),
                pltpu.VMEM((2, TILE, 2 * TILE), F32),
            ],
        ),
        out_shape=[out] * 3 + [jax.ShapeDtypeStruct((pairs, 2, 6 * TILE), F32)],
        compiler_params=params(),
        name="attn_bwd",
    )(lengths, q, k, v, do, lse, band)


def wgrad_kernel(core_ref, h1_ref, dq_ref, dk_ref, dv_ref, gwo_ref, keep_ref, send_ref, h1T_ref, g_ref, sems):
    width = h1_ref.shape[1]
    n = width // 256
    h1T_ref[...] = h1_ref[...].T
    for i, d in enumerate((dq_ref, dk_ref, dv_ref)):
        g = dot(h1T_ref[...], d[...])
        for j in range(n):
            at = (i * n + j) * width
            g_ref[at : at + width, :] = g[:, j * 256 : (j + 1) * 256]
    for j in range(n):
        at = (3 * n + j) * width
        g_ref[at : at + width, :] = gwo_ref[j]
    half = keep_ref.shape[0]
    moves = place(core_ref[0], g_ref.at[0:half, :], g_ref.at[half : 2 * half, :], keep_ref, send_ref, sems)
    start_all(moves)
    wait_all(moves)


def wgrads(core, h1, ds, gwo):
    toks, width = h1.shape
    n = width // 256
    whole = pl.BlockSpec(memory_space=pltpu.VMEM)
    return pl.pallas_call(
        wgrad_kernel,
        in_specs=[pl.BlockSpec(memory_space=pltpu.SMEM)] + [whole] * 5,
        out_specs=[pl.BlockSpec(memory_space=pl.ANY)] * 2,
        out_shape=[jax.ShapeDtypeStruct((2 * n * width, 256), F32)] * 2,
        scratch_shapes=[pltpu.VMEM((width, toks), BF16), pltpu.VMEM((4 * n * width, 256), F32), pltpu.SemaphoreType.DMA((2,))],
        compiler_params=params(),
        name="attn_wgrad",
    )(core, h1, *ds, gwo)


def tokgrad_kernel(tok_ref, dres_ref, gain_ref, dq_ref, dk_ref, dv_ref, wq_ref, wk_ref, wv_ref, out_ref, ggain_ref):
    step = pl.program_id(0)
    done = dot(dq_ref[...], wq_ref[...], NT) + dot(dk_ref[...], wk_ref[...], NT) + dot(dv_ref[...], wv_ref[...], NT)
    tok = tok_ref[...].astype(F32)
    s = norm_scale(tok)
    g = gain_ref[...].astype(F32) * done
    out_ref[...] = (dres_ref[...] + s * g - tok * (s * s * s * jnp.mean(tok * g, axis=-1, keepdims=True))).astype(BF16)
    ggain = jnp.sum(done * tok * s, axis=0, keepdims=True)

    @pl.when(step == 0)
    def _():
        ggain_ref[...] = ggain

    @pl.when(step > 0)
    def _():
        ggain_ref[...] += ggain


def tokgrad(tok, dres, gain, dq, dk, dv, wq, wk, wv, block=512):
    toks, width = tok.shape
    full = lambda a: pl.BlockSpec(a.shape, lambda s: (0,) * a.ndim)
    tall = pl.BlockSpec((block, width), lambda s: (s, 0))
    return pl.pallas_call(
        tokgrad_kernel,
        grid=(toks // block,),
        in_specs=[tall, tall, full(gain), tall, tall, tall, full(wq), full(wk), full(wv)],
        out_specs=[tall, pl.BlockSpec((1, width), lambda s: (0, 0))],
        out_shape=[jax.ShapeDtypeStruct((toks, width), BF16), jax.ShapeDtypeStruct((1, width), F32)],
        compiler_params=params(),
        name="tokgrad",
    )(tok, dres, gain, dq, dk, dv, wq, wk, wv)


def bit_orders(size):
    bits = list(range(size.bit_length() - 1))
    swapped = bits[1::-1] + bits[2:]
    return list(zip(bits, swapped))


def exchange(x, size, cores, bits):
    moves = [
        (r * cores + c, (r ^ (1 << bits[c % 2])) * cores + c) for r in range(size) for c in range(cores)
    ]
    return lax.ppermute(x, ("rows", "blk"), moves)


def swap_cores(x):
    return lax.ppermute(x, "blk", [(0, 1), (1, 0)])


def my_bit(bits):
    r, c = lax.axis_index("rows"), lax.axis_index("blk")
    return jnp.where(c % 2 == 0, (r >> bits[0]) & 1, (r >> bits[1]) & 1)


def reduce_scatter(keep, send, size):
    got = swap_cores(send)
    for bits in bit_orders(size):
        bit = my_bit(bits)
        half = keep.shape[0] // 2
        part = lambda a, at: lax.dynamic_slice_in_dim(a, at * half, half, 0)
        out = part(keep, 1 - bit) + part(got, 1 - bit)
        coming = exchange(out, size, 2, bits)
        keep = part(keep, bit) + part(got, bit)
        got = coming
    return keep + got


def all_gather(piece, size):
    orders = list(reversed(bit_orders(size)))
    for bits in orders:
        got = exchange(piece, size, 2, bits)
        bit = my_bit(bits)
        if bits is not orders[-1]:
            wide = jnp.concatenate([piece, piece], axis=0)
            piece = lax.dynamic_update_slice_in_dim(wide, got, (1 - bit) * got.shape[0], 0)
    return piece, got


def assemble_kernel(place_of, n_outs, where_ref, *refs):
    sources, outs, sems = refs[:4], refs[-1 - n_outs : -1], refs[-1]
    core, bit, far_bit = where_ref[0], where_ref[1], where_ref[2]
    owners = (core, core, 1 - core, 1 - core)
    halves = (bit, 1 - bit, far_bit, 1 - far_bit)
    for action in ("start", "wait"):
        for n, source in enumerate(sources):
            for owner in range(2):
                for half in range(2):

                    @pl.when((owners[n] == owner) & (halves[n] == half))
                    def _():
                        for j in range(source.shape[0] // 256):
                            out, row, col = place_of(owner, half, j)
                            copy = pltpu.make_async_copy(
                                source.at[j * 256 : (j + 1) * 256, :],
                                outs[out].at[row : row + 256, col : col + 256],
                                sems.at[n, j],
                            )
                            getattr(copy, action)()


def assemble(place_of, shapes, where, sources, earlier=()):
    any_place = pl.BlockSpec(memory_space=pl.ANY)
    count = sources[0].shape[0] // 256
    return pl.pallas_call(
        functools.partial(assemble_kernel, place_of, len(shapes)),
        in_specs=[pl.BlockSpec(memory_space=pltpu.SMEM)] + [any_place] * (4 + len(earlier)),
        out_specs=[any_place] * len(shapes),
        out_shape=[jax.ShapeDtypeStruct(s, F32) for s in shapes],
        scratch_shapes=[pltpu.SemaphoreType.DMA((4, count))],
        input_output_aliases={5 + i: i for i in range(len(earlier))},
        compiler_params=params(),
        name="assemble",
    )(where, *sources, *earlier)


def ffn_place(width, start, sub, count, owner, half, j):
    i = half * count + j
    if owner == 0:
        per = width // 256
        return 0, (i % per) * 256, start + (i // per) * 256
    per = sub // 256
    block = i // per
    stripe, step = block % (width // 256), block // (width // 256)
    return 1, start + step * sub + (i % per) * 256, stripe * 256


def attn_place(width, owner, half, j):
    per = width // 256
    return 2 * owner + half, (j % per) * 256, (j // per) * 256


def on_device(tokens, lengths, attn_gain, wq, wk, wv, wo, table, ffn_gain, w_in, w_out, out_grad, *, size, chunks=2, sub=512):
    rows, seq, width = tokens.shape
    buckets, heads = table.shape
    ff = w_in.shape[1]
    core = lax.axis_index("blk")
    core_arg = core.astype(jnp.int32).reshape(1)
    last = bit_orders(size)[0]
    row_id = lax.axis_index("rows")
    ends = [(row_id >> b) & 1 for b in last]
    where = jnp.stack([core, jnp.where(core == 0, ends[0], ends[1]), jnp.where(core == 0, ends[1], ends[0])]).astype(jnp.int32)
    lane_buckets = band_buckets(buckets)
    onehot = np.arange(buckets)[:, None] == lane_buckets[None, :]
    band = jnp.einsum("bh,bm->hm", table, jnp.asarray(onehot, BF16), preferred_element_type=F32)
    gain1, gain2 = attn_gain.reshape(1, width), ffn_gain.reshape(1, width)
    flat = lambda a: a.reshape(rows * seq, width)
    tall = lambda a: a.reshape(rows, seq, width)

    def total(keep, send):
        piece, got = all_gather(reduce_scatter(keep, send, size), size)
        return piece, got, swap_cores(piece), swap_cores(got)

    h1, q, k, v, att, attT, lse, x1, h2 = attn_fwd(tokens, lengths, gain1, gain2, wq, wk, wv, wo, band)
    part = ff // chunks
    acc, ffn_grads = None, ()
    for c in range(chunks):
        keep, send, mix, dtwo = ffn_chunk(core_arg, flat(h2), flat(out_grad), w_in, w_out, c * part, part, sub, acc)
        acc = (mix, dtwo)
        sources = total(keep, send)
        place_of = functools.partial(ffn_place, width, c * part, sub, sources[0].shape[0] // 256)
        ffn_grads = assemble(place_of, [w_in.shape, w_out.shape], where, sources, ffn_grads)
    mixed, dres, datt, gwo, ggain2 = resid_bwd(lengths, x1, tall(mix), tall(dtwo), out_grad, gain2, attT, wo)
    dq, dk, dv, diag = attn_bwd(lengths, q, k, v, datt, lse, band)
    sources = total(*wgrads(core_arg, flat(h1), [flat(dq), flat(dk), flat(dv)], gwo))
    attn_grads = assemble(functools.partial(attn_place, width), [wq.shape] * 4, where, sources)
    tgrad, ggain1 = tokgrad(flat(tokens), flat(dres), gain1, flat(dq), flat(dk), flat(dv), wq, wk, wv)
    far = bucket_of(np.array([-2 * TILE] * TILE + [2 * TILE] * TILE), buckets)
    spread = (np.concatenate([lane_buckets, far])[:, None] == np.arange(buckets)[None, :]).astype(np.float32)
    gtable = jnp.einsum("hm,mb->bh", diag.reshape(heads, 6 * TILE), jnp.asarray(spread), precision=lax.Precision.HIGHEST)
    ggain1, ggain2, gtable = lax.psum((ggain1, ggain2, gtable), ("rows", "blk"))
    return (mixed, tall(tgrad), ggain1[0], *attn_grads, gtable, ggain2[0], *ffn_grads)


def solution(mesh):
    split = P(("rows", "blk"))
    return jax.shard_map(
        functools.partial(on_device, size=mesh.shape["rows"]),
        mesh=mesh,
        in_specs=(split, split) + (P(),) * 9 + (split,),
        out_specs=(split, split) + (P(),) * 9,
        check_vma=False,
    )
```

```python
import functools
import jax
import jax.numpy as jnp
import numpy as np
from jax import lax
from jax.experimental import pallas as pl
from jax.experimental.pallas import tpu as pltpu
from jax.sharding import PartitionSpec as P

NT = (((1,), (1,)), ((), ()))
TN = (((0,), (0,)), ((), ()))
F32, BF16 = jnp.float32, jnp.bfloat16
TILE = 128
MASKED = -1000000000.0
EPS = 1e-06
far_steps = np.array([12, 16, 23, 32, 46, 64, 91], dtype=np.int32)


def dot(a, b, dims=None):
    if dims is None:
        return jnp.dot(a, b, preferred_element_type=F32)
    return lax.dot_general(a, b, dims, preferred_element_type=F32)


def bucket_of(relative, bucket_count):
    distance = np.abs(relative)
    beyond = np.sum(distance[..., None] >= far_steps, axis=-1)
    inner = np.where(distance < bucket_count // 4, distance, bucket_count // 4 + beyond)
    return np.where(relative > 0, bucket_count // 2, 0) + inner


def band_buckets(bucket_count):
    lanes = np.arange(4 * TILE)
    offsets = np.where(lanes < 2 * TILE, lanes, lanes - 4 * TILE)
    return bucket_of(-offsets, bucket_count)


def segments_along(len_ref, row, shape, axis):
    at = lax.broadcasted_iota(jnp.int32, shape, axis)
    total = jnp.zeros(shape, jnp.int32)
    end = jnp.int32(0)
    for j in range(len_ref.shape[1]):
        end = end + len_ref[row, j]
        total = total + jnp.where(at >= end, 1, 0)
    return total


def fill_mask(len_ref, row, mask_ref, last):
    seq = mask_ref.shape[0]
    of_q = segments_along(len_ref, row, (1, seq), 1)
    of_k = segments_along(len_ref, row, (seq, TILE), 0)
    of_k = jnp.where(of_k < last, of_k, -1)
    for j in range(seq // TILE):
        same = of_k == of_q[:, j * TILE : (j + 1) * TILE]
        mask_ref[:, j * TILE : (j + 1) * TILE] = jnp.where(same, 0.0, MASKED)
    return of_q < last


def band_of(vector):
    wide = jnp.broadcast_to(vector, (TILE, 4 * TILE))
    return pltpu.roll(wide, 0, 1, stride=1, stride_axis=0)


def bias_row(band, vector, ki, count):
    shape = (TILE, TILE)
    tiles = []
    for qi in range(count):
        step = ki - qi
        if step == 0:
            tiles.append(band[:, 0:TILE])
        elif step == -1:
            tiles.append(band[:, TILE : 2 * TILE])
        elif step == 1:
            tiles.append(band[:, 3 * TILE : 4 * TILE])
        elif step < 0:
            tiles.append(jnp.broadcast_to(vector[:, 2 * TILE - 1 : 2 * TILE], shape))
        else:
            tiles.append(jnp.broadcast_to(vector[:, 2 * TILE : 2 * TILE + 1], shape))
    return jnp.concatenate(tiles, axis=1)


def norm_scale(value):
    return lax.rsqrt(jnp.mean(value * value, axis=-1, keepdims=True) + EPS)


def attn_fwd_kernel(
    len_ref, tok_ref, gain_ref, wq_ref, wk_ref, wv_ref, wo_ref, band_ref,
    h1_ref, q_ref, k_ref, v_ref, att_ref, attT_ref, lse_ref, x1_ref, h2_ref,
    mask_ref, s_ref, p_ref,
):
    seq, width = tok_ref.shape[1:]
    pairs = band_ref.shape[0]
    head = TILE // 2
    row = pl.program_id(0)
    valid = fill_mask(len_ref, row, mask_ref, len_ref.shape[1] - 1)
    tok = tok_ref[0].astype(F32)
    h1 = (tok * norm_scale(tok) * gain_ref[0:1, :]).astype(BF16)
    h1_ref[0] = h1
    q_ref[0] = dot(h1, wq_ref[...]).astype(BF16)
    k_ref[0] = dot(h1, wk_ref[...]).astype(BF16)
    v_ref[0] = dot(h1, wv_ref[...]).astype(BF16)
    count = seq // TILE
    low_half = lax.broadcasted_iota(jnp.int32, (1, TILE), 1) < head

    def pair(p, carry):
        lanes = pl.ds(pl.multiple_of(p * TILE, TILE), TILE)
        qp, kp, vp = q_ref[0, :, lanes], k_ref[0, :, lanes], v_ref[0, :, lanes]
        vT = vp.T
        outs = []
        for a in range(2):
            qm = jnp.where(low_half if a == 0 else ~low_half, qp, jnp.zeros_like(qp))
            vector = band_ref[p, a : a + 1, :]
            band = band_of(vector)
            top = None
            for ki in range(count):
                rows = slice(ki * TILE, (ki + 1) * TILE)
                s = dot(kp[rows], qm, NT) + bias_row(band, vector, ki, count) + mask_ref[rows, :]
                s_ref[a, rows, :] = s
                most = jnp.max(s, axis=0, keepdims=True)
                top = most if top is None else jnp.maximum(top, most)
            total = jnp.zeros_like(top)
            for ki in range(count):
                rows = slice(ki * TILE, (ki + 1) * TILE)
                e = jnp.exp(s_ref[a, rows, :] - top)
                total = total + jnp.sum(e, axis=0, keepdims=True)
                p_ref[a, rows, :] = e.astype(BF16)
            o = dot(vT[a * head : (a + 1) * head], p_ref[a])
            o = jnp.where(valid, o / total, 0.0)
            outs.append(o)
            lse_ref[0, p, a : a + 1, :] = top + jnp.log(total)
        both = jnp.concatenate(outs, axis=0)
        attT_ref[0, lanes, :] = both.astype(BF16)
        att_ref[0, :, lanes] = both.T.astype(BF16)
        return carry

    lax.fori_loop(0, pairs, pair, 0)
    x1 = tok_ref[0].astype(F32) + dot(att_ref[0], wo_ref[...])
    x1_ref[0] = x1
    h2_ref[0] = (x1 * norm_scale(x1) * gain_ref[1:2, :]).astype(BF16)


VMEM = 60 * 2**20
COST = pl.CostEstimate(flops=10**11, transcendentals=0, bytes_accessed=1)
ANYWHERE = pl.BlockSpec(memory_space=pl.ANY)


def params(limit=VMEM):
    return pltpu.CompilerParams(vmem_limit_bytes=limit)


def attn_fwd(tokens, lengths, gains, wq, wk, wv, wo, band):
    rows, seq, width = tokens.shape
    pairs = band.shape[0]
    full = lambda a: pl.BlockSpec(a.shape, lambda r, l: (0,) * a.ndim, pipeline_mode=pl.Buffered(1))
    per_row = lambda *s: pl.BlockSpec((1,) + s, lambda r, l: (r,) + (0,) * len(s))
    tall = jax.ShapeDtypeStruct((rows, seq, width), BF16)
    outs = [tall] * 5 + [
        jax.ShapeDtypeStruct((rows, width, seq), BF16),
        jax.ShapeDtypeStruct((rows, pairs, 2, seq), F32),
        jax.ShapeDtypeStruct((rows, seq, width), F32),
        tall,
    ]
    return pl.pallas_call(
        attn_fwd_kernel,
        grid_spec=pltpu.PrefetchScalarGridSpec(
            num_scalar_prefetch=1,
            grid=(rows,),
            in_specs=[per_row(seq, width), full(gains), full(wq), full(wk), full(wv), full(wo), full(band)],
            out_specs=[per_row(seq, width)] * 5 + [per_row(width, seq), per_row(pairs, 2, seq), per_row(seq, width), per_row(seq, width)],
            scratch_shapes=[
                pltpu.VMEM((seq, seq), F32),
                pltpu.VMEM((2, seq, seq), F32),
                pltpu.VMEM((2, seq, seq), BF16),
            ],
        ),
        out_shape=outs,
        cost_estimate=COST, compiler_params=params(32 * 2**20),
        name="attn_fwd",
    )(lengths, tokens, gains, wq, wk, wv, wo, band)


GELU_C = float(np.sqrt(2.0 / np.pi))


def gelu_pair(v):
    v2 = v * v
    t = jnp.tanh(GELU_C * v * (1.0 + 0.044715 * v2))
    half = 0.5 * (1.0 + t)
    slope = half + (0.5 * GELU_C) * v * (1.0 - t * t) * (1.0 + (3 * 0.044715) * v2)
    return v * half, slope


def place(core, mine, other, keep, send, sems):
    both = lambda a, b: [(src, dst, sems.at[n, i]) for n, pairs in enumerate((a, b)) for i, (src, dst) in enumerate(pairs)]
    return [(core == 0, both(mine(keep), other(send))), (core != 0, both(mine(send), other(keep)))]


def run_all(cases, action):
    for condition, copies in cases:

        @pl.when(condition)
        def _():
            for src, dst, sem in copies:
                getattr(pltpu.make_async_copy(src, dst, sem), action)()


def ffn_kernel(steps, slabs, n_acc, info_ref, h2_ref, dy_ref, win_ref, wout_ref, *refs):
    acc, refs = refs[:n_acc], refs[n_acc:]
    if slabs:
        keep_ref, send_ref, mix_ref, dtwo_ref, h2T_ref, gin_ref, gout_ref, sems = refs[-8:]
    else:
        gin_ref, gout_ref, mix_ref, dtwo_ref, h2T_ref = refs[-5:]
    step = pl.program_id(0)
    h2, dy = h2_ref[...], dy_ref[...]
    width = h2.shape[1]
    sub = win_ref.shape[1]
    wide, tall = width // 256, sub // 256
    if slabs:
        in_rows, out_rows = width // slabs, sub * steps // slabs
        piece = in_rows * tall * steps
        here = slabs // steps

    def moves(at):
        def of_in(ref):
            return [
                (
                    gin_ref.at[at, i * in_rows * tall : (i + 1) * in_rows * tall, :],
                    ref.at[pl.ds(pl.multiple_of(i * piece + at * (in_rows * tall), 8), in_rows * tall), :],
                )
                for i in range(slabs)
            ]

        def of_out(ref):
            return [(gout_ref.at[at], ref.at[pl.ds(pl.multiple_of(at * (here * piece), 8), here * piece), :])]

        return place(info_ref[0], of_in, of_out, keep_ref, send_ref, sems.at[at])

    @pl.when(step == 0)
    def _():
        h2T_ref[...] = h2_ref[...].T

    pre = dot(h2, win_ref[...])
    act, slope = gelu_pair(pre)
    act = act.astype(BF16)
    gout = dot(act, dy, TN)
    if slabs:
        for i in range(here):
            for j in range(wide):
                at = (i * wide + j) * out_rows
                gout_ref[step, at : at + out_rows, :] = gout[i * out_rows : (i + 1) * out_rows, j * 256 : (j + 1) * 256]
    else:
        gout_ref[...] = gout
    dpre = (dot(dy, wout_ref[...], NT) * slope).astype(BF16)
    gin = dot(h2T_ref[...], dpre)
    if slabs:
        for i in range(slabs):
            for j in range(tall):
                at = (i * tall + j) * in_rows
                gin_ref[step, at : at + in_rows, :] = gin[i * in_rows : (i + 1) * in_rows, j * 256 : (j + 1) * 256]
        run_all(moves(step), "start")
    else:
        gin_ref[...] = gin
    mix = dot(act, wout_ref[...])
    dtwo = dot(dpre, win_ref[...], NT)

    @pl.when(step == 0)
    def _():
        mix_ref[...] = acc[0][...] + mix if n_acc else mix
        dtwo_ref[...] = acc[1][...] + dtwo if n_acc else dtwo

    @pl.when(step > 0)
    def _():
        mix_ref[...] += mix
        dtwo_ref[...] += dtwo

    if slabs:

        @pl.when(step == steps - 1)
        def _():
            for at in range(steps):
                run_all(moves(at), "wait")


def ffn_chunk(info, slabs, h2, dy, w_in, w_out, start, size, sub, acc, after):
    toks, width = h2.shape
    base = start // sub
    steps = size // sub
    piece = width * (sub // 256)
    full = lambda a: pl.BlockSpec(a.shape, lambda s, c: (0,) * a.ndim, pipeline_mode=pl.Buffered(1))
    total = pl.BlockSpec((toks, width), lambda s, c: (0, 0))
    total_shape = jax.ShapeDtypeStruct((toks, width), F32)
    if slabs:
        out_specs = [ANYWHERE, ANYWHERE]
        out_shape = [jax.ShapeDtypeStruct((steps * piece, 256), F32)] * 2
        scratch = [
            pltpu.VMEM((steps, piece, 256), F32),
            pltpu.VMEM((steps, piece, 256), F32),
            pltpu.SemaphoreType.DMA((steps, 2, slabs)),
        ]
    else:
        out_specs = [pl.BlockSpec((width, sub), lambda s, c: (0, s)), pl.BlockSpec((sub, width), lambda s, c: (s, 0))]
        out_shape = [jax.ShapeDtypeStruct((width, size), F32), jax.ShapeDtypeStruct((size, width), F32)]
        scratch = []
    return pl.pallas_call(
        functools.partial(ffn_kernel, steps, slabs, len(acc)),
        grid_spec=pltpu.PrefetchScalarGridSpec(
            num_scalar_prefetch=1,
            grid=(steps,),
            in_specs=[full(h2), full(dy), pl.BlockSpec((width, sub), lambda s, c: (0, base + s)), pl.BlockSpec((sub, width), lambda s, c: (base + s, 0))]
            + [full(a) for a in acc]
            + [ANYWHERE] * len(after),
            out_specs=out_specs + [total, total],
            scratch_shapes=[pltpu.VMEM((width, toks), BF16)] + scratch,
        ),
        out_shape=out_shape + [total_shape, total_shape],
        cost_estimate=COST, compiler_params=params(52 * 2**20),
        name="ffn",
    )(info, h2, dy, w_in, w_out, *acc, *after)


def resid_kernel(len_ref, x1_ref, mix_ref, dtwo_ref, dy_ref, gain_ref, attT_ref, wo_ref,
                 mixed_ref, dres_ref, datt_ref, gwo_ref, ggain_ref):
    step = pl.program_id(0)
    x1, dtwo = x1_ref[0], dtwo_ref[0]
    mixed_ref[0] = (x1 + mix_ref[0]).astype(BF16)
    s = norm_scale(x1)
    g = gain_ref[1:2, :] * dtwo
    dres = dy_ref[0].astype(F32) + s * g - x1 * (s * s * s * jnp.mean(x1 * g, axis=-1, keepdims=True))
    dres_ref[0] = dres
    dbranch = dres.astype(BF16)
    ggain = jnp.sum(dtwo * x1 * s, axis=0, keepdims=True)
    gwo = dot(attT_ref[0], dbranch)
    seq = x1.shape[0]
    seg = segments_along(len_ref, step, (seq, TILE), 0)[:, :1]
    datt = dot(dbranch, wo_ref[...], NT)
    datt_ref[0] = jnp.where(seg < len_ref.shape[1] - 1, datt, 0.0).astype(BF16)

    @pl.when(step == 0)
    def _():
        ggain_ref[...] = ggain
        gwo_ref[...] = gwo

    @pl.when(step > 0)
    def _():
        ggain_ref[...] += ggain
        gwo_ref[...] += gwo


def resid_bwd(lengths, x1, mix, dtwo, dy, gain, attT, wo):
    rows, seq, width = x1.shape
    full = lambda a: pl.BlockSpec(a.shape, lambda r, l: (0,) * a.ndim)
    tall = pl.BlockSpec((1, seq, width), lambda r, l: (r, 0, 0))
    return pl.pallas_call(
        resid_kernel,
        grid_spec=pltpu.PrefetchScalarGridSpec(
            num_scalar_prefetch=1,
            grid=(rows,),
            in_specs=[tall, tall, tall, tall, full(gain), pl.BlockSpec((1, width, seq), lambda r, l: (r, 0, 0)), full(wo)],
            out_specs=[tall, tall, tall, pl.BlockSpec((width, width), lambda r, l: (0, 0)), pl.BlockSpec((1, width), lambda r, l: (0, 0))],
        ),
        out_shape=[
            jax.ShapeDtypeStruct((rows, seq, width), BF16),
            jax.ShapeDtypeStruct((rows, seq, width), F32),
            jax.ShapeDtypeStruct((rows, seq, width), BF16),
            jax.ShapeDtypeStruct((width, width), F32),
            jax.ShapeDtypeStruct((1, width), F32),
        ],
        cost_estimate=COST, compiler_params=params(40 * 2**20),
        name="resid_bwd",
    )(lengths, x1, mix, dtwo, dy, gain, attT, wo)


def diagonal_sums(x):
    depth, lanes = x.shape
    total = x[0:8]
    for g in range(8, depth, 8):
        total = total + pltpu.roll(x[g : g + 8], lanes - g, 1)
    at = lax.broadcasted_iota(jnp.int32, (8, lanes), 0)
    for bit in (1, 2, 4):
        total = jnp.where((at & bit) != 0, pltpu.roll(total, lanes - bit, 1), total)
    return jnp.sum(total, axis=0, keepdims=True)


def attn_bwd_kernel(len_ref, q_ref, k_ref, v_ref, do_ref, lse_ref, band_ref, *rest):
    (
        dq_ref, dk_ref, dv_ref, diag_ref,
        mask_ref, p_ref, pl_ref, dp_ref, ds_ref, near_ref, far_ref,
    ) = rest[-11:]
    pair, row = pl.program_id(0), pl.program_id(1)
    seq = q_ref.shape[1]
    head = TILE // 2
    count = seq // TILE
    fill_mask(len_ref, row, mask_ref, len_ref.shape[1] - 1)
    low_half = lax.broadcasted_iota(jnp.int32, (1, TILE), 1) < head
    qp, kp, vp, dop = q_ref[0], k_ref[0], v_ref[0], do_ref[0]
    kT = kp.T

    @pl.when(row == 0)
    def _():
        near_ref[...] = jnp.zeros_like(near_ref)
        far_ref[...] = jnp.zeros_like(far_ref)

    dqT, dk, dv = [], None, None
    for a in range(2):
        own = low_half if a == 0 else ~low_half
        qm = jnp.where(own, qp, jnp.zeros_like(qp))
        dom = jnp.where(own, dop, jnp.zeros_like(dop))
        vector = band_ref[0, a : a + 1, :]
        band = band_of(vector)
        lse = lse_ref[0, 0, a : a + 1, :]
        delta = jnp.zeros((1, seq), F32)
        for ki in range(count):
            rows = slice(ki * TILE, (ki + 1) * TILE)
            s = dot(kp[rows], qm, NT) + bias_row(band, vector, ki, count) + mask_ref[rows, :]
            prob = jnp.exp(s - lse)
            dp = dot(vp[rows], dom, NT)
            delta = delta + jnp.sum(prob * dp, axis=0, keepdims=True)
            p_ref[a, rows, :] = prob
            pl_ref[a, rows, :] = prob.astype(BF16)
            dp_ref[a, rows, :] = dp
        for ki in range(count):
            rows = slice(ki * TILE, (ki + 1) * TILE)
            ds = p_ref[a, rows, :] * (dp_ref[a, rows, :] - delta)
            ds_ref[a, rows, :] = ds.astype(BF16)
            for qi in range(count):
                tile = ds[:, qi * TILE : (qi + 1) * TILE]
                step = ki - qi
                if abs(step) <= 1:
                    at = (0 if step == 0 else 1 if step == -1 else 3) * TILE
                    near_ref[a, :, at : at + TILE] += tile
                else:
                    at = 0 if step < 0 else TILE
                    far_ref[a, :, at : at + TILE] += tile
        dva = dot(pl_ref[a], dom)
        dka = dot(ds_ref[a], qm)
        dv = dva if dv is None else dv + dva
        dk = dka if dk is None else dk + dka
        dqT.append(dot(kT[a * head : (a + 1) * head], ds_ref[a]))
    dv_ref[0] = dv.astype(BF16)
    dk_ref[0] = dk.astype(BF16)
    dq_ref[0] = jnp.concatenate(dqT, axis=0).T.astype(BF16)

    @pl.when(row == pl.num_programs(1) - 1)
    def _():
        for a in range(2):
            diag_ref[0, a : a + 1, : 4 * TILE] = diagonal_sums(near_ref[a])
            diag_ref[0, a : a + 1, 4 * TILE :] = jnp.sum(far_ref[a], axis=0, keepdims=True)


def attn_bwd(lengths, q, k, v, do, lse, band, first, pairs, after):
    rows, seq, width = q.shape
    tall = pl.BlockSpec((1, seq, TILE), lambda p, r, l: (r, 0, first + p))
    tall_out = pl.BlockSpec((1, seq, TILE), lambda p, r, l: (r, 0, p))
    out = jax.ShapeDtypeStruct((rows, seq, pairs * TILE), BF16)
    return pl.pallas_call(
        attn_bwd_kernel,
        grid_spec=pltpu.PrefetchScalarGridSpec(
            num_scalar_prefetch=1,
            grid=(pairs, rows),
            in_specs=[tall] * 4
            + [pl.BlockSpec((1, 1, 2, seq), lambda p, r, l: (r, first + p, 0, 0)), pl.BlockSpec((1, 2, 4 * TILE), lambda p, r, l: (first + p, 0, 0))]
            + [ANYWHERE] * len(after),
            out_specs=[tall_out] * 3 + [pl.BlockSpec((1, 2, 6 * TILE), lambda p, r, l: (p, 0, 0))],
            scratch_shapes=[
                pltpu.VMEM((seq, seq), F32),
                pltpu.VMEM((2, seq, seq), F32),
                pltpu.VMEM((2, seq, seq), BF16),
                pltpu.VMEM((2, seq, seq), F32),
                pltpu.VMEM((2, seq, seq), BF16),
                pltpu.VMEM((2, TILE, 4 * TILE), F32),
                pltpu.VMEM((2, TILE, 2 * TILE), F32),
            ],
        ),
        out_shape=[out] * 3 + [jax.ShapeDtypeStruct((pairs, 2, 6 * TILE), F32)],
        cost_estimate=COST, compiler_params=params(24 * 2**20),
        name="attn_bwd",
    )(lengths, q, k, v, do, lse, band, *after)


def wgrad_kernel(slabs, n_more, info_ref, h1_ref, dq_ref, dk_ref, dv_ref, *refs):
    more, refs = refs[:n_more], refs[n_more:]
    keep_ref, send_ref, h1T_ref, g_ref, sems = refs[-5:]
    width, cols = h1_ref.shape[1], g_ref.shape[2]
    stripes = keep_ref.shape[0] * 2 // width
    rows = width // 2 // slabs

    def put(j, block):
        for c in range(2):
            for s in range(slabs):
                at, begin = (s * stripes + j) * rows, (c * slabs + s) * rows
                g_ref[c, at : at + rows, :] = block[begin : begin + rows]

    h1T_ref[...] = h1_ref[...].T
    for j, d in enumerate((dq_ref, dk_ref, dv_ref)):
        put(j, dot(h1T_ref[...], d[...]))
    for j in range(stripes - 3):
        put(3 + j, more[0][:, j * cols : (j + 1) * cols])
    moves = place(
        info_ref[0], lambda ref: [(g_ref.at[0], ref)], lambda ref: [(g_ref.at[1], ref)], keep_ref, send_ref, sems
    )
    run_all(moves, "start")
    run_all(moves, "wait")


def wgrads(info, slabs, h1, ds, more, after):
    toks, width = h1.shape
    cols = ds[0].shape[1]
    half = width // 2 * (3 + sum(m.shape[1] // cols for m in more))
    whole = pl.BlockSpec(memory_space=pltpu.VMEM)
    return pl.pallas_call(
        functools.partial(wgrad_kernel, slabs, len(more)),
        in_specs=[pl.BlockSpec(memory_space=pltpu.SMEM)] + [whole] * (4 + len(more)) + [ANYWHERE] * len(after),
        out_specs=[ANYWHERE] * 2,
        out_shape=[jax.ShapeDtypeStruct((half, cols), F32)] * 2,
        scratch_shapes=[pltpu.VMEM((width, toks), BF16), pltpu.VMEM((2, half, cols), F32), pltpu.SemaphoreType.DMA((2, 1))],
        cost_estimate=COST, compiler_params=params(24 * 2**20),
        name="attn_wgrad",
    )(info, h1, *ds, *more, *after)


def tokgrad_kernel(halves, tok_ref, dres_ref, gain_ref, wq_ref, wk_ref, wv_ref, *refs):
    out_ref, ggain_ref = refs[-2:]
    step = pl.program_id(0)
    done = None
    for i, w in enumerate((wq_ref, wk_ref, wv_ref)):
        d = jnp.concatenate([refs[h * 3 + i][...] for h in range(halves)], axis=1)
        term = dot(d, w[...], NT)
        done = term if done is None else done + term
    tok = tok_ref[...].astype(F32)
    s = norm_scale(tok)
    g = gain_ref[0:1, :] * done
    out_ref[...] = (dres_ref[...] + s * g - tok * (s * s * s * jnp.mean(tok * g, axis=-1, keepdims=True))).astype(BF16)
    ggain = jnp.sum(done * tok * s, axis=0, keepdims=True)

    @pl.when(step == 0)
    def _():
        ggain_ref[...] = ggain

    @pl.when(step > 0)
    def _():
        ggain_ref[...] += ggain


def tokgrad(tok, dres, gains, ds, wq, wk, wv, after, block=512):
    toks, width = tok.shape
    full = lambda a: pl.BlockSpec(a.shape, lambda s: (0,) * a.ndim, pipeline_mode=pl.Buffered(1))
    tall = pl.BlockSpec((block, width), lambda s: (s, 0))
    return pl.pallas_call(
        functools.partial(tokgrad_kernel, len(ds) // 3),
        grid=(toks // block,),
        in_specs=[tall, tall, full(gains), full(wq), full(wk), full(wv)]
        + [pl.BlockSpec((block, d.shape[1]), lambda s: (s, 0)) for d in ds]
        + [ANYWHERE] * len(after),
        out_specs=[tall, pl.BlockSpec((1, width), lambda s: (0, 0))],
        out_shape=[jax.ShapeDtypeStruct((toks, width), BF16), jax.ShapeDtypeStruct((1, width), F32)],
        cost_estimate=COST, compiler_params=params(32 * 2**20),
        name="tokgrad",
    )(tok, dres, gains, wq, wk, wv, *ds, *after)


class Route:
    def __init__(self, size, even, odd):
        self.size, self.even, self.odd = size, even, odd
        self.count = len(even)
        core, row = lax.axis_index("blk"), lax.axis_index("rows")
        one = lambda group: sum(((row >> b) & 1) << (len(group) - 1 - i) for i, b in enumerate(group))
        at = lambda c, phase: jnp.where(c == 0, one(even[phase]), one(odd[phase])).astype(jnp.int32)
        self.at = [at(core, phase) for phase in range(self.count)]
        self.far = at(1 - core, 0)
        self.ways = [1 << len(group) for group in even]

    def exchange(self, x, phase, step):
        def other(r, group):
            for i, b in enumerate(group):
                r ^= ((step >> (len(group) - 1 - i)) & 1) << b
            return r

        moves = [
            (r * 2 + c, other(r, (self.even, self.odd)[c][phase]) * 2 + c) for r in range(self.size) for c in range(2)
        ]
        return lax.ppermute(x, ("rows", "blk"), moves)


def swap_cores(x):
    return lax.ppermute(x, "blk", [(0, 1), (1, 0)])


def following(values, after):
    if not after:
        return values
    return lax.optimization_barrier((tuple(values), tuple(after)))[0]


class Sum:
    def __init__(self, route, keep, send):
        self.route = route
        self.parts = [keep, swap_cores(send)]
        self.begins = [0, 0]
        self.shares = [keep.shape[0]]
        for ways in route.ways:
            if self.shares[-1] % (8 * ways):
                break
            self.shares.append(self.shares[-1] // ways)
        self.divided = len(self.shares) - 1
        self.phase = 0
        self.steps = (
            [self.send] * self.divided
            + [self.finish]
            + [self.add] * (route.count - self.divided)
            + [self.join] * (self.divided - 1)
            + [self.swap]
        )

    def advance(self, after):
        return self.steps.pop(0)(after) if self.steps else after

    def total(self, places, rows):
        out = None
        for begin, part in zip(self.begins, self.parts):
            at = 0
            for phase in range(begin, len(places)):
                at = at * self.route.ways[phase] + places[phase]
            share = lax.dynamic_slice_in_dim(part, at * rows, rows, 0) if part.shape[0] > rows else part
            out = share if out is None else out + share
        return out

    def send(self, after):
        phase = self.phase
        places = following(self.route.at[: phase + 1], after)
        outs = []
        for step in range(1, self.route.ways[phase]):
            outs.append(self.total([*places[:phase], places[phase] ^ step], self.shares[phase + 1]))
        for step, out in enumerate(outs):
            self.parts.append(self.route.exchange(out, phase, step + 1))
            self.begins.append(phase + 1)
        self.phase += 1
        return outs

    def finish(self, after):
        self.piece = self.total(following(self.route.at[: self.phase], after), self.shares[self.phase])
        return self.gather()

    def gather(self):
        if self.divided <= self.phase < self.route.count:
            phase = self.phase
        else:
            phase = self.phase = min(self.phase, self.divided) - 1
        self.got = [self.route.exchange(self.piece, phase, step) for step in range(1, self.route.ways[phase])]
        if self.phase == 0:
            self.far_piece = swap_cores(self.piece)
        return [self.piece]

    def add(self, after):
        got = following(self.got, after)
        self.piece = functools.reduce(lambda a, b: a + b, got, self.piece)
        self.phase += 1
        return self.gather()

    def join(self, after):
        (at,) = following((self.route.at[self.phase],), after)
        pieces = [self.piece, *self.got]
        rows = []
        for slot in range(len(pieces)):
            row = pieces[-1]
            for step in range(len(pieces) - 1):
                row = jnp.where(at == slot ^ step, pieces[step], row)
            rows.append(row)
        self.piece = jnp.concatenate(rows)
        return self.gather()

    def swap(self, after):
        (got,) = following(self.got, after)
        self.sources = (self.piece, got, self.far_piece, swap_cores(got))
        return [got]


class SmallSum:
    @staticmethod
    def steps_of(route, phase):
        return [1 << i for i in range(len(route.even[phase]))]

    def __init__(self, route, values):
        self.route = route
        self.shapes = [v.shape for v in values]
        flat = jnp.concatenate([v.reshape(-1) for v in values])
        self.sum = jnp.pad(flat, (0, -flat.shape[0] % 2048)).reshape(-1, 256)
        self.steps = [
            functools.partial(route.exchange, phase=p, step=step) for p in range(route.count) for step in SmallSum.steps_of(route, p)
        ] + [swap_cores]
        self.got = self.steps.pop(0)(self.sum)

    def advance(self, after):
        if self.got is None:
            return after
        mine, got = following((self.sum, self.got), after)
        self.sum = mine + got
        self.got = self.steps.pop(0)(self.sum) if self.steps else None
        return [self.sum]

    def values(self):
        while self.got is not None:
            self.advance(())
        flat, at, out = self.sum.reshape(-1), 0, []
        for shape in self.shapes:
            size = int(np.prod(shape))
            out.append(flat[at : at + size].reshape(shape))
            at += size
        return out


def assemble_kernel(spread, n_outs, info_ref, *refs):
    sources, outs = refs[:4], refs[-n_outs:]
    target, half = pl.program_id(0), pl.program_id(1)
    for n in range(4):
        for t in range(2):

            @pl.when((info_ref[2 + n] == 2 * target + half) & (target == t))
            def _():
                spread(t, sources[n], outs)


def assemble(info, slabs, spread, outs, blocks, sources, group, earlier, after):
    rows, cols = sources[0].shape
    count = slabs // 2 // group

    def source_spec(n):
        def index(t, h, j, i):
            stage, now = i[2 + n], 2 * t + h
            return jnp.where(now < stage, 0, jnp.where(now == stage, j, count - 1)), 0

        return pl.BlockSpec((rows // count, cols), index)

    def out_spec(target, block, row, column):
        def index(t, h, j, i):
            if target is None:
                return row + (2 * t + h) * count + j, column
            return row + jnp.where(t == target, h * count + j, 0 if target else 2 * count - 1), column

        return pl.BlockSpec(block, index)

    return pl.pallas_call(
        functools.partial(assemble_kernel, spread, len(outs)),
        grid_spec=pltpu.PrefetchScalarGridSpec(
            num_scalar_prefetch=1,
            grid=(2, 2, count),
            in_specs=[source_spec(n) for n in range(4)] + [ANYWHERE] * (len(earlier) + len(after)),
            out_specs=[out_spec(*b) for b in blocks],
        ),
        out_shape=[jax.ShapeDtypeStruct(s, F32) for s in outs],
        input_output_aliases={5 + i: i for i in range(len(earlier))},
        cost_estimate=COST, compiler_params=params(24 * 2**20),
        name="assemble",
    )(info, *sources, *earlier, *after)


def ffn_spread(width, size, slabs, group, target, source, outs):
    n, total = (size // 256, width) if target == 0 else (width // 256, size)
    rows = total // slabs
    for s in range(group):
        for j in range(n):
            at = (s * n + j) * rows
            outs[target][s * rows : (s + 1) * rows, j * 256 : (j + 1) * 256] = source[at : at + rows, :]


def attn_spread(columns, slabs, group, target, source, outs):
    n = len(columns)
    rows = source.shape[0] // (group * n)
    for s in range(group):
        for j, (out, column) in enumerate(columns):
            at = (s * n + j) * rows
            outs[out][s * rows : (s + 1) * rows, column : column + source.shape[1]] = source[at : at + rows, :]


ORDER = "F0 s0 F1 s0 R s1 s0 B0 W0 s0 s1 B1 s0 s1 s2 W1 T s3 s1 m s2 s0 m s2 s1 m s2 s3 m s1 s0 s3 s2 s0 s3 s2 s3 s1 s1 s3 s2 s2 s3 s3"


def on_device(tokens, lengths, attn_gain, wq, wk, wv, wo, table, ffn_gain, w_in, w_out, out_grad, *, size):
    rows, seq, width = tokens.shape
    buckets, heads = table.shape
    pairs = heads // 2
    ff = w_in.shape[1]
    slabs = 16
    bits = list(range(2, size.bit_length() - 1))
    rest = [tuple(bits[i : i + 2][::-1]) for i in range(0, len(bits), 2)]
    route = Route(size, [(0,), (1,)] + rest, [(1,), (0,)] + rest)
    core = lax.axis_index("blk")
    b, far = route.at[0], route.far
    info = jnp.stack(
        [core, lax.axis_index("rows"), 2 * core + b, 2 * core + 1 - b, 2 * (1 - core) + far, 2 * (1 - core) + 1 - far]
    ).astype(jnp.int32)
    lane_buckets = band_buckets(buckets)
    onehot = np.arange(buckets)[:, None] == lane_buckets[None, :]
    band = jnp.einsum(
        "bpa,bm->pam", table.reshape(buckets, pairs, 2), jnp.asarray(onehot, BF16), preferred_element_type=F32
    )
    gains = jnp.stack([attn_gain, ffn_gain]).astype(F32)
    flat = lambda a: a.reshape(rows * seq, a.shape[2])
    tall = lambda a: a.reshape(rows, seq, width)
    chunks, sub = 2, 768
    part = ff // chunks
    ends = bucket_of(np.array([-2 * TILE] * TILE + [2 * TILE] * TILE), buckets)
    spread = (np.concatenate([lane_buckets, ends])[:, None] == np.arange(buckets)[None, :]).astype(np.float32)

    h1, q, k, v, att, attT, lse, x1, h2 = attn_fwd(tokens, lengths, gains, wq, wk, wv, wo, band)
    acc, sums, after, ds, diags = (), [], (), [], []
    ffn_grads, attn_grads = (), ()

    def put(which, after):
        nonlocal ffn_grads, attn_grads
        group = 4
        sources = sums[which].sources
        if which < chunks:
            ffn_grads = assemble(
                info, slabs, functools.partial(ffn_spread, width, part, slabs, group), [w_in.shape, w_out.shape],
                [(0, (width // slabs * group, part), 0, which), (1, (part // slabs * group, width), which * (slabs // group), 0)],
                sources, group, tuple(ffn_grads), after,
            )
            return (ffn_grads[0],)
        half = which - chunks
        block = width // 2 // slabs * group
        columns = [(0, 0), (1, 0), (2, 0)] + [(3, 0), (3, width // 2)] * (half == 0)
        blocks = [(None, (block, width // 2), 0, half)] * 3 + [(None, (block, width), 0, 0)] * (half == 0)
        made = assemble(
            info, slabs, functools.partial(attn_spread, columns, slabs, group), [wq.shape] * len(blocks), blocks,
            sources, group, tuple(attn_grads[:3]), after,
        )
        attn_grads = list(made) + list(attn_grads[3:])
        return (made[0],)

    for at, op in enumerate(ORDER.split()):
        which = int(op[1]) if len(op) > 1 else 0
        if op[0] == "F":
            x, y, *acc = ffn_chunk(info, slabs, flat(h2), flat(out_grad), w_in, w_out, which * part, part, sub, acc, after)
            sums.append(Sum(route, x, y))
            after = (x,)
        elif op == "R":
            mixed, dres, datt, gwo, ggain2 = resid_bwd(lengths, x1, tall(acc[0]), tall(acc[1]), out_grad, gains, attT, wo)
            after = (mixed,)
        elif op[0] == "B":
            half = pairs // 2
            dq, dk, dv, diag = attn_bwd(lengths, q, k, v, datt, lse, band, which * half, half, after)
            ds += [flat(dq), flat(dk), flat(dv)]
            diags.append(diag)
            after = (dq,)
        elif op[0] == "W":
            keep, send = wgrads(info, slabs, flat(h1), ds[-3:], [] if which else [gwo], after)
            sums.append(Sum(route, keep, send))
            after = (keep,)
        elif op == "T":
            tgrad, ggain1 = tokgrad(flat(tokens), flat(dres), gains, ds, wq, wk, wv, after)
            diag = jnp.concatenate(diags).reshape(heads, 6 * TILE)
            gtable = jnp.einsum("hm,mb->bh", diag, jnp.asarray(spread), precision=lax.Precision.HIGHEST)
            small = SmallSum(route, (ggain1, ggain2, gtable))
            after = (ggain1,)
        elif op == "m":
            after = small.advance(after)
        else:
            after = sums[which].advance(after)
            if ORDER.split()[at:].count(op) == 1:
                while sums[which].steps:
                    after = sums[which].advance(after)
                after = put(which, after)
    ggain1, ggain2, gtable = small.values()
    return (mixed, tall(tgrad), ggain1[0], *attn_grads, gtable, ggain2[0], *ffn_grads)


def solution(mesh):
    split = P(("rows", "blk"))
    return jax.shard_map(
        functools.partial(on_device, size=mesh.shape["rows"]),
        mesh=mesh,
        in_specs=(split, split) + (P(),) * 9 + (split,),
        out_specs=(split, split) + (P(),) * 9,
        check_vma=False,
    )
```

```python
import functools
import jax
import jax.numpy as jnp
import numpy as np
from jax import lax
from jax.experimental import pallas as pl
from jax.experimental.pallas import tpu as pltpu
from jax.sharding import PartitionSpec as P

NT = (((1,), (1,)), ((), ()))
TN = (((0,), (0,)), ((), ()))
F32, BF16 = jnp.float32, jnp.bfloat16
TILE = 128
MASKED = -1000000000.0
EPS = 1e-06
far_steps = np.array([12, 16, 23, 32, 46, 64, 91], dtype=np.int32)


def dot(a, b, dims=None):
    if dims is None:
        return jnp.dot(a, b, preferred_element_type=F32)
    return lax.dot_general(a, b, dims, preferred_element_type=F32)


def bucket_of(relative, bucket_count):
    distance = np.abs(relative)
    beyond = np.sum(distance[..., None] >= far_steps, axis=-1)
    inner = np.where(distance < bucket_count // 4, distance, bucket_count // 4 + beyond)
    return np.where(relative > 0, bucket_count // 2, 0) + inner


def band_buckets(bucket_count):
    lanes = np.arange(4 * TILE)
    offsets = np.where(lanes < 2 * TILE, lanes, lanes - 4 * TILE)
    return bucket_of(-offsets, bucket_count)


def segments_along(len_ref, row, shape, axis, start=0):
    at = lax.broadcasted_iota(jnp.int32, shape, axis) + start
    total = jnp.zeros(shape, jnp.int32)
    end = jnp.int32(0)
    for j in range(len_ref.shape[1]):
        end = end + len_ref[row, j]
        total = total + jnp.where(at >= end, 1, 0)
    return total


def fill_mask(len_ref, row, mask_ref, last):
    seq = mask_ref.shape[0]
    of_q = segments_along(len_ref, row, (1, seq), 1)
    of_k = segments_along(len_ref, row, (seq, TILE), 0)
    of_k = jnp.where(of_k < last, of_k, -1)
    for j in range(seq // TILE):
        same = of_k == of_q[:, j * TILE : (j + 1) * TILE]
        mask_ref[:, j * TILE : (j + 1) * TILE] = jnp.where(same, 0.0, MASKED)
    return of_q < last


def band_of(vector):
    wide = jnp.broadcast_to(vector, (TILE, 4 * TILE))
    return pltpu.roll(wide, 0, 1, stride=1, stride_axis=0)


def bias_row(band, vector, ki, count):
    shape = (TILE, TILE)
    tiles = []
    for qi in range(count):
        step = ki - qi
        if step == 0:
            tiles.append(band[:, 0:TILE])
        elif step == -1:
            tiles.append(band[:, TILE : 2 * TILE])
        elif step == 1:
            tiles.append(band[:, 3 * TILE : 4 * TILE])
        elif step < 0:
            tiles.append(jnp.broadcast_to(vector[:, 2 * TILE - 1 : 2 * TILE], shape))
        else:
            tiles.append(jnp.broadcast_to(vector[:, 2 * TILE : 2 * TILE + 1], shape))
    return jnp.concatenate(tiles, axis=1)


def norm_scale(value):
    return lax.rsqrt(jnp.mean(value * value, axis=-1, keepdims=True) + EPS)


def row_of(gain_ref):
    return gain_ref[...].astype(F32).reshape(1, gain_ref.shape[0])


VMEM = 63 * 2**20
ANYWHERE = pl.BlockSpec(memory_space=pl.ANY)
FLOPS = 10**11
LITTLE = pl.CostEstimate(flops=1, transcendentals=0, bytes_accessed=1)
COST = pl.CostEstimate(flops=FLOPS, transcendentals=0, bytes_accessed=1)


def params(limit=VMEM):
    return pltpu.CompilerParams(vmem_limit_bytes=limit)


def attn_fwd_kernel(
    len_ref, tok_ref, gain1_ref, gain2_ref, wq_ref, wk_ref, wv_ref, wo_ref, band_ref,
    h1T_ref, q_ref, k_ref, v_ref, attT_ref, lse_ref, x1_ref, h2_ref,
    att_ref, mask_ref, s_ref, p_ref,
):
    seq, width = tok_ref.shape[1:]
    pairs = width // TILE
    head = TILE // 2
    row = pl.program_id(0)
    valid = fill_mask(len_ref, row, mask_ref, len_ref.shape[1] - 1)
    tok = tok_ref[0].astype(F32)
    h1 = (tok * norm_scale(tok) * row_of(gain1_ref)).astype(BF16)
    h1T_ref[0] = h1.T
    q_ref[0] = dot(h1, wq_ref[...]).astype(BF16)
    k_ref[0] = dot(h1, wk_ref[...]).astype(BF16)
    v_ref[0] = dot(h1, wv_ref[...]).astype(BF16)
    count = seq // TILE
    low_half = lax.broadcasted_iota(jnp.int32, (1, TILE), 1) < head

    def pair(p, carry):
        lanes = pl.ds(pl.multiple_of(p * TILE, TILE), TILE)
        qp, kp, vp = q_ref[0, :, lanes], k_ref[0, :, lanes], v_ref[0, :, lanes]
        vT = vp.T
        tops = []
        for a in range(2):
            qm = jnp.where(low_half if a == 0 else ~low_half, qp, jnp.zeros_like(qp))
            vector = band_ref[pl.ds(2 * p + a, 1), :]
            band = band_of(vector)
            top = None
            for ki in range(count):
                rows = slice(ki * TILE, (ki + 1) * TILE)
                s = dot(kp[rows], qm, NT) + bias_row(band, vector, ki, count) + mask_ref[rows, :]
                s_ref[a, rows, :] = s
                most = jnp.max(s, axis=0, keepdims=True)
                top = most if top is None else jnp.maximum(top, most)
            tops.append(top)
        totals = []
        for a, top in enumerate(tops):
            total = jnp.zeros_like(top)
            for ki in range(count):
                rows = slice(ki * TILE, (ki + 1) * TILE)
                e = jnp.exp(s_ref[a, rows, :] - top)
                total = total + jnp.sum(e, axis=0, keepdims=True)
                p_ref[a, rows, :] = e.astype(BF16)
            totals.append(total)
        outs = []
        for a, (top, total) in enumerate(zip(tops, totals)):
            o = dot(vT[a * head : (a + 1) * head], p_ref[a])
            outs.append(jnp.where(valid, o / total, 0.0))
            lse_ref[0, pl.ds(2 * p + a, 1), :] = top + jnp.log(total)
        both = jnp.concatenate(outs, axis=0)
        attT_ref[0, lanes, :] = both.astype(BF16)
        att_ref[:, lanes] = both.T.astype(BF16)
        return carry

    lax.fori_loop(0, pairs, pair, 0, unroll=6)
    x1 = tok_ref[0].astype(F32) + dot(att_ref[...], wo_ref[...])
    x1_ref[0] = x1
    h2_ref[0] = (x1 * norm_scale(x1) * row_of(gain2_ref)).astype(BF16)


def attn_fwd(tokens, lengths, gain1, gain2, wq, wk, wv, wo, band):
    rows, seq, width = tokens.shape
    heads = band.shape[0]
    full = lambda a: pl.BlockSpec(a.shape, lambda r, l: (0,) * a.ndim, pipeline_mode=pl.Buffered(1))
    per_row = lambda *s: pl.BlockSpec((1,) + s, lambda r, l: (r,) + (0,) * len(s))
    tall = jax.ShapeDtypeStruct((rows, seq, width), BF16)
    turned = jax.ShapeDtypeStruct((rows, width, seq), BF16)
    return pl.pallas_call(
        attn_fwd_kernel,
        grid_spec=pltpu.PrefetchScalarGridSpec(
            num_scalar_prefetch=1,
            grid=(rows,),
            in_specs=[per_row(seq, width)] + [full(a) for a in (gain1, gain2, wq, wk, wv, wo, band)],
            out_specs=[per_row(width, seq)]
            + [per_row(seq, width)] * 3
            + [per_row(width, seq), per_row(heads, seq), per_row(seq, width), per_row(seq, width)],
            scratch_shapes=[
                pltpu.VMEM((seq, width), BF16),
                pltpu.VMEM((seq, seq), F32),
                pltpu.VMEM((2, seq, seq), F32),
                pltpu.VMEM((2, seq, seq), BF16),
            ],
        ),
        out_shape=[turned, tall, tall, tall, turned]
        + [jax.ShapeDtypeStruct((rows, heads, seq), F32), jax.ShapeDtypeStruct((rows, seq, width), F32), tall],
        cost_estimate=COST,
        compiler_params=params(),
        name="attn_fwd",
    )(lengths, tokens, gain1, gain2, wq, wk, wv, wo, band)


GELU_C = float(np.sqrt(2.0 / np.pi))


def gelu_pair(v):
    v2 = v * v
    t = jnp.tanh(GELU_C * v * (1.0 + 0.044715 * v2))
    half = 0.5 * (1.0 + t)
    slope = half + (0.5 * GELU_C) * v * (1.0 - t * t) * (1.0 + (3 * 0.044715) * v2)
    return v * half, slope


def place(core, mine, other, keep, send, sems):
    both = lambda a, b: [(src, dst, sems.at[n, i]) for n, pairs in enumerate((a, b)) for i, (src, dst) in enumerate(pairs)]
    return [(core == 0, both(mine(keep), other(send))), (core != 0, both(mine(send), other(keep)))]


def run_all(cases, action):
    for condition, copies in cases:

        @pl.when(condition)
        def _():
            for src, dst, sem in copies:
                getattr(pltpu.make_async_copy(src, dst, sem), action)()


def ffn_kernel(steps, slabs, first, last, info_ref, len_ref, h2_ref, dy_ref, win_ref, wout_ref, *refs):
    refs = list(refs)
    acc_in = [] if first else [refs.pop(0), refs.pop(0)]
    if last:
        x1_ref, gain_ref, attT_ref, wo_ref = refs[:4]
        keep_ref, send_ref, mixed_out, dres_out, datt_out, gwo_ref, ggain_ref = refs[-19:-12]
        mix_ref, dtwo_ref, h2T_ref, act_ref, dpre_ref, gin_ref, gout_ref, sems, acc_sems, mixed_ref, dres_ref, datt_ref = refs[-12:]
    else:
        keep_ref, send_ref = refs[-13:-11]
        acc_out = refs[-11:-9]
        mix_ref, dtwo_ref, h2T_ref, act_ref, dpre_ref, gin_ref, gout_ref, sems, acc_sems = refs[-9:]
    step = pl.program_id(0)
    toks, width = h2_ref.shape
    sub = win_ref.shape[1]
    wide, tall = width // 256, sub // 256
    in_rows, out_rows = width // slabs, sub * steps // slabs
    piece = in_rows * tall * steps
    here = slabs // steps
    totals = (mix_ref, dtwo_ref)

    def moves(at):
        def of_in(ref):
            return [
                (
                    gin_ref.at[at, i * in_rows * tall : (i + 1) * in_rows * tall, :],
                    ref.at[pl.ds(pl.multiple_of(i * piece + at * (in_rows * tall), 8), in_rows * tall), :],
                )
                for i in range(slabs)
            ]

        def of_out(ref):
            return [(gout_ref.at[at], ref.at[pl.ds(pl.multiple_of(at * (here * piece), 8), here * piece), :])]

        return place(info_ref[0], of_in, of_out, keep_ref, send_ref, sems.at[at])

    @pl.when(step == 0)
    def _():
        for i, ref in enumerate(acc_in):
            pltpu.make_async_copy(ref, totals[i], acc_sems.at[i]).start()
        h2T_ref[...] = h2_ref[...].T

    for c in range(0, sub, 256):
        cols = slice(c, c + 256)
        pre = dot(h2_ref[...], win_ref[:, cols])
        dact = dot(dy_ref[...], wout_ref[cols, :], NT)
        act, slope = gelu_pair(pre)
        act_ref[:, cols] = act.astype(BF16)
        dpre_ref[:, cols] = (dact * slope).astype(BF16)
    mix = dot(act_ref[...], wout_ref[...])
    dtwo = dot(dpre_ref[...], win_ref[...], NT)

    @pl.when(step == 0)
    def _():
        if first:
            mix_ref[...] = mix
            dtwo_ref[...] = dtwo
        else:
            for i, ref in enumerate(acc_in):
                pltpu.make_async_copy(ref, totals[i], acc_sems.at[i]).wait()
            mix_ref[...] += mix
            dtwo_ref[...] += dtwo

    @pl.when(step > 0)
    def _():
        mix_ref[...] += mix
        dtwo_ref[...] += dtwo

    if not last:

        @pl.when(step == steps - 1)
        def _():
            for i in range(2):
                pltpu.make_async_copy(totals[i], acc_out[i], acc_sems.at[2 + i]).start()

    gout = dot(act_ref[...], dy_ref[...], TN)
    for i in range(here):
        for j in range(wide):
            at = (i * wide + j) * out_rows
            gout_ref[step, at : at + out_rows, :] = gout[i * out_rows : (i + 1) * out_rows, j * 256 : (j + 1) * 256]
    gin = dot(h2T_ref[...], dpre_ref[...])
    for i in range(slabs):
        for j in range(tall):
            at = (i * tall + j) * in_rows
            gin_ref[step, at : at + in_rows, :] = gin[i * in_rows : (i + 1) * in_rows, j * 256 : (j + 1) * 256]
    run_all(moves(step), "start")

    @pl.when(step == steps - 1)
    def _():
        if last:
            rows = len_ref.shape[0]
            seq = toks // rows
            block = 256
            copies = []
            ggain = None
            for b in range(toks // block):
                here_toks = slice(b * block, (b + 1) * block)
                x1, back = x1_ref[here_toks, :], dtwo_ref[here_toks, :]
                mixed_ref[here_toks, :] = (x1 + mix_ref[here_toks, :]).astype(BF16)
                s = norm_scale(x1)
                g = row_of(gain_ref) * back
                dres = dy_ref[here_toks, :].astype(F32) + s * g - x1 * (s * s * s * jnp.mean(x1 * g, axis=-1, keepdims=True))
                dres_ref[here_toks, :] = dres
                some = jnp.sum(back * x1 * s, axis=0, keepdims=True)
                ggain = some if ggain is None else ggain + some
                dbranch = dres.astype(BF16)
                act_ref[here_toks, :] = dbranch
                datt = dot(dbranch, wo_ref[...], NT)
                seg = segments_along(len_ref, b * block // seq, (block, TILE), 0, b * block % seq)[:, :1]
                datt_ref[here_toks, :] = jnp.where(seg < len_ref.shape[1] - 1, datt, 0.0).astype(BF16)
                for n, (src, dst) in enumerate(((mixed_ref, mixed_out), (dres_ref, dres_out), (datt_ref, datt_out))):
                    copies.append(pltpu.make_async_copy(src.at[here_toks, :], dst.at[here_toks, :], acc_sems.at[4 + 3 * b + n]))
                    copies[-1].start()
            ggain_ref[...] = ggain
            gwo = None
            for r in range(rows):
                part = dot(attT_ref[r], act_ref[r * seq : (r + 1) * seq, :])
                gwo = part if gwo is None else gwo + part
            gwo_ref[...] = gwo
            for copy in copies:
                copy.wait()
        else:
            for i in range(2):
                pltpu.make_async_copy(totals[i], acc_out[i], acc_sems.at[2 + i]).wait()
        for at in range(steps):
            run_all(moves(at), "wait")


def ffn_chunk(info, lengths, slabs, h2, dy, w_in, w_out, start, size, sub, acc, after, rest=None):
    toks, width = h2.shape
    base = start // sub
    steps = size // sub
    piece = width * (sub // 256)
    full = lambda a: pl.BlockSpec(a.shape, lambda s, *_: (0,) * a.ndim, pipeline_mode=pl.Buffered(1))
    f32 = lambda *s: jax.ShapeDtypeStruct(s, F32)
    out_specs = [ANYWHERE] * 2
    out_shape = [f32(steps * piece, 256)] * 2
    scratch = [
        pltpu.VMEM((toks, width), F32),
        pltpu.VMEM((toks, width), F32),
        pltpu.VMEM((width, toks), BF16),
        pltpu.VMEM((toks, sub), BF16),
        pltpu.VMEM((toks, sub), BF16),
        pltpu.VMEM((steps, piece, 256), F32),
        pltpu.VMEM((steps, piece, 256), F32),
        pltpu.SemaphoreType.DMA((steps, 2, slabs)),
        pltpu.SemaphoreType.DMA((4 + 3 * (toks // 256),)),
    ]
    if rest is None:
        rest = ()
        out_specs += [ANYWHERE] * 2
        out_shape += [f32(toks, width)] * 2
    else:
        low = jax.ShapeDtypeStruct((toks, width), BF16)
        whole = lambda s: pl.BlockSpec(s.shape, lambda *_: (0,) * len(s.shape), pipeline_mode=pl.Buffered(1))
        gwo, ggain = f32(width, width), f32(1, width)
        out_specs += [ANYWHERE] * 3 + [whole(gwo), whole(ggain)]
        out_shape += [low, f32(toks, width), low, gwo, ggain]
        scratch += [pltpu.VMEM((toks, width), BF16), pltpu.VMEM((toks, width), F32), pltpu.VMEM((toks, width), BF16)]
    return pl.pallas_call(
        functools.partial(ffn_kernel, steps, slabs, not acc, bool(rest)),
        grid_spec=pltpu.PrefetchScalarGridSpec(
            num_scalar_prefetch=2,
            grid=(steps,),
            in_specs=[
                full(h2),
                full(dy),
                pl.BlockSpec((width, sub), lambda s, *_: (0, base + s)),
                pl.BlockSpec((sub, width), lambda s, *_: (base + s, 0)),
            ]
            + [ANYWHERE] * len(acc)
            + [full(a) for a in rest]
            + [ANYWHERE] * len(after),
            out_specs=out_specs,
            scratch_shapes=scratch,
        ),
        out_shape=out_shape,
        cost_estimate=COST,
        compiler_params=params(),
        name="ffn",
    )(info, lengths, h2, dy, w_in, w_out, *acc, *rest, *after)


def diagonal_sums(x):
    depth, lanes = x.shape
    total = x[0:8]
    for g in range(8, depth, 8):
        total = total + pltpu.roll(x[g : g + 8], lanes - g, 1)
    at = lax.broadcasted_iota(jnp.int32, (8, lanes), 0)
    for bit in (1, 2, 4):
        total = jnp.where((at & bit) != 0, pltpu.roll(total, lanes - bit, 1), total)
    return jnp.sum(total, axis=0, keepdims=True)


def attn_bwd_kernel(slabs, first, n_more, info_ref, len_ref, q_ref, k_ref, v_ref, do_ref, lse_ref, band_ref, h1T_ref, *refs):
    more = refs[:n_more]
    dq_ref, dk_ref, dv_ref, diag_ref, keep_ref, send_ref = refs[-14:-8]
    mask_ref, p_ref, low_ref, dp_ref, ds_ref, d_ref, g_ref, sems = refs[-8:]
    pair, pairs = pl.program_id(0), pl.num_programs(0)
    rows, seq = q_ref.shape[:2]
    head = TILE // 2
    count = seq // TILE
    width, cols = h1T_ref.shape[1], g_ref.shape[2]
    stripes = keep_ref.shape[0] * 2 // width
    share = width // 2 // slabs

    def put(j, block):
        for c in range(2):
            for s in range(slabs):
                at, begin = (s * stripes + j) * share, (c * slabs + s) * share
                g_ref[c, at : at + share, :] = block[begin : begin + share]

    @pl.when(pair == 0)
    def _():
        for row in range(rows):
            fill_mask(len_ref, row, mask_ref.at[row], len_ref.shape[1] - 1)

    low_half = lax.broadcasted_iota(jnp.int32, (1, TILE), 1) < head
    bands = []
    for a in range(2):
        vector = band_ref[pl.ds(2 * (first + pair) + a, 1), :]
        bands.append((vector, band_of(vector)))
    sides = []
    for n in range(2 * rows):
        row, a = n // 2, n % 2
        qp, kp, vp, dop = q_ref[row], k_ref[row], v_ref[row], do_ref[row]
        own = low_half if a == 0 else ~low_half
        qm = jnp.where(own, qp, jnp.zeros_like(qp))
        dom = jnp.where(own, dop, jnp.zeros_like(dop))
        vector, band = bands[a]
        lse = lse_ref[row, pl.ds(2 * (first + pair) + a, 1), :]
        delta = jnp.zeros((1, seq), F32)
        for ki in range(count):
            some = slice(ki * TILE, (ki + 1) * TILE)
            s = dot(kp[some], qm, NT) + bias_row(band, vector, ki, count) + mask_ref[row, some, :]
            prob = jnp.exp(s - lse)
            dp = dot(vp[some], dom, NT)
            delta = delta + jnp.sum(prob * dp, axis=0, keepdims=True)
            p_ref[n, some, :] = prob
            low_ref[n, some, :] = prob.astype(BF16)
            dp_ref[n, some, :] = dp
        sides.append((qm, dom, delta))
    sums = [{}, {}]
    for n, (_, _, delta) in enumerate(sides):
        near = sums[n % 2]
        for ki in range(count):
            some = slice(ki * TILE, (ki + 1) * TILE)
            ds = p_ref[n, some, :] * (dp_ref[n, some, :] - delta)
            ds_ref[n, some, :] = ds.astype(BF16)
            for qi in range(count):
                step = max(-2, min(2, ki - qi))
                tile = ds[:, qi * TILE : (qi + 1) * TILE]
                near[step] = tile if step not in near else near[step] + tile
    for a, near in enumerate(sums):
        zero = jnp.zeros((TILE, TILE), F32)
        band = jnp.concatenate([near[0], near[-1], zero, near[1]], axis=1)
        diag_ref[0, a : a + 1, : 4 * TILE] = diagonal_sums(band)
        ends = jnp.concatenate([near[-2], near[2]], axis=1)
        diag_ref[0, a : a + 1, 4 * TILE :] = jnp.sum(ends, axis=0, keepdims=True)
    lanes = pl.ds(pl.multiple_of(pair * TILE, TILE), TILE)
    for row in range(rows):
        kT = k_ref[row].T
        dqT, dk, dv = [], None, None
        for a in range(2):
            n = 2 * row + a
            qm, dom, _ = sides[n]
            dva = dot(low_ref[n], dom)
            dka = dot(ds_ref[n], qm)
            dv = dva if dv is None else dv + dva
            dk = dka if dk is None else dk + dka
            dqT.append(dot(kT[a * head : (a + 1) * head], ds_ref[n]))
        dq = jnp.concatenate(dqT, axis=0).T.astype(BF16)
        dk, dv = dk.astype(BF16), dv.astype(BF16)
        dq_ref[row], dk_ref[row], dv_ref[row] = dq, dk, dv
        for j, d in enumerate((dq, dk, dv)):
            d_ref[j, row, :, lanes] = d

    @pl.when(pair == pairs - 1)
    def _():
        for j in range(3):
            g = None
            for r in range(h1T_ref.shape[0]):
                part = dot(h1T_ref[r], d_ref[j, r])
                g = part if g is None else g + part
            put(j, g)
        for j in range(stripes - 3):
            put(3 + j, more[0][:, j * cols : (j + 1) * cols])
        moves = place(
            info_ref[0], lambda ref: [(g_ref.at[0], ref)], lambda ref: [(g_ref.at[1], ref)], keep_ref, send_ref, sems
        )
        run_all(moves, "start")
        run_all(moves, "wait")


def attn_bwd(info, lengths, slabs, q, k, v, do, lse, band, h1T, first, pairs, more, after):
    rows, seq, width = q.shape
    cols = pairs * TILE
    half = width // 2 * (3 + sum(m.shape[1] // cols for m in more))
    tall = pl.BlockSpec((rows, seq, TILE), lambda p, *_: (0, 0, first + p))
    tall_out = pl.BlockSpec((rows, seq, TILE), lambda p, *_: (0, 0, p))
    full = lambda a: pl.BlockSpec(a.shape, lambda *_: (0,) * a.ndim, pipeline_mode=pl.Buffered(1))
    out = jax.ShapeDtypeStruct((rows, seq, cols), BF16)
    square = lambda dtype: pltpu.VMEM((2 * rows, seq, seq), dtype)
    return pl.pallas_call(
        functools.partial(attn_bwd_kernel, slabs, first, len(more)),
        grid_spec=pltpu.PrefetchScalarGridSpec(
            num_scalar_prefetch=2,
            grid=(pairs,),
            in_specs=[tall] * 4
            + [full(lse), full(band), full(h1T)]
            + [full(m) for m in more]
            + [ANYWHERE] * len(after),
            out_specs=[tall_out] * 3 + [pl.BlockSpec((1, 2, 6 * TILE), lambda p, *_: (p, 0, 0))] + [ANYWHERE] * 2,
            scratch_shapes=[
                pltpu.VMEM((rows, seq, seq), F32),
                square(F32),
                square(BF16),
                square(F32),
                square(BF16),
                pltpu.VMEM((3, rows, seq, cols), BF16),
                pltpu.VMEM((2, half, cols), F32),
                pltpu.SemaphoreType.DMA((2, 1)),
            ],
        ),
        out_shape=[out] * 3
        + [jax.ShapeDtypeStruct((pairs, 2, 6 * TILE), F32)]
        + [jax.ShapeDtypeStruct((half, cols), F32)] * 2,
        cost_estimate=COST,
        compiler_params=params(),
        name="attn_bwd",
    )(info, lengths, q, k, v, do, lse, band, h1T, *more, *after)


def tokgrad_kernel(halves, tok_ref, dres_ref, gain_ref, wq_ref, wk_ref, wv_ref, *refs):
    out_ref, ggain_ref = refs[-2:]
    step = pl.program_id(0)
    done = None
    for i, w in enumerate((wq_ref, wk_ref, wv_ref)):
        d = jnp.concatenate([refs[h * 3 + i][...] for h in range(halves)], axis=1)
        term = dot(d, w[...], NT)
        done = term if done is None else done + term
    tok = tok_ref[...].astype(F32)
    s = norm_scale(tok)
    g = row_of(gain_ref) * done
    out_ref[...] = (dres_ref[...] + s * g - tok * (s * s * s * jnp.mean(tok * g, axis=-1, keepdims=True))).astype(BF16)
    ggain = jnp.sum(done * tok * s, axis=0, keepdims=True)

    @pl.when(step == 0)
    def _():
        ggain_ref[...] = ggain

    @pl.when(step > 0)
    def _():
        ggain_ref[...] += ggain


def tokgrad(tok, dres, gain, ds, wq, wk, wv, after, block=256):
    toks, width = tok.shape
    full = lambda a: pl.BlockSpec(a.shape, lambda s: (0,) * a.ndim, pipeline_mode=pl.Buffered(1))
    tall = pl.BlockSpec((block, width), lambda s: (s, 0))
    return pl.pallas_call(
        functools.partial(tokgrad_kernel, len(ds) // 3),
        grid=(toks // block,),
        in_specs=[tall, tall, full(gain), full(wq), full(wk), full(wv)]
        + [pl.BlockSpec((block, d.shape[1]), lambda s: (s, 0)) for d in ds]
        + [ANYWHERE] * len(after),
        out_specs=[tall, pl.BlockSpec((1, width), lambda s: (0, 0))],
        out_shape=[jax.ShapeDtypeStruct((toks, width), BF16), jax.ShapeDtypeStruct((1, width), F32)],
        cost_estimate=COST,
        compiler_params=params(),
        name="tokgrad",
    )(tok, dres, gain, wq, wk, wv, *ds, *after)


SMALL = 16 * 2**20


class Route:
    def __init__(self, size, even, odd):
        self.size, self.even, self.odd = size, even, odd
        self.count = len(even)
        self.ways = [1 << len(group) for group in even]
        self.columns = {}
        table = [self.line(r, c) for r in range(size) for c in range(2)]
        device = lax.axis_index("rows") * 2 + lax.axis_index("blk")
        self.info = lax.dynamic_index_in_dim(jnp.asarray(np.array(table, np.int32)), device, 0, keepdims=False)

    def places(self, r, c):
        groups = (self.even, self.odd)[c]
        return [sum(((r >> b) & 1) << (len(group) - 1 - i) for i, b in enumerate(group)) for group in groups]

    def line(self, r, c):
        places, far = self.places(r, c), self.places(r, 1 - c)[0]
        line = [c, r, 2 * c + places[0], 2 * c + 1 - places[0], 2 * (1 - c) + far, 2 * (1 - c) + 1 - far, *places]
        self.place_column = 6
        for end in range(1, self.count + 1):
            for begin in range(end):
                for step in range(self.ways[end - 1]):
                    at = 0
                    for phase in range(begin, end):
                        at = at * self.ways[phase] + (places[phase] ^ (step if phase == end - 1 else 0))
                    self.columns[begin, end, step] = len(line)
                    line.append(at)
        return line

    def exchange(self, x, phase, step):
        def other(r, group):
            for i, b in enumerate(group):
                r ^= ((step >> (len(group) - 1 - i)) & 1) << b
            return r

        moves = [
            (r * 2 + c, other(r, (self.even, self.odd)[c][phase]) * 2 + c) for r in range(self.size) for c in range(2)
        ]
        return lax.ppermute(x, ("rows", "blk"), moves)


def swap_cores(x):
    return lax.ppermute(x, "blk", [(0, 1), (1, 0)])


def add_kernel(count, outs, info_ref, *refs):
    for n in range(outs):
        total = None
        for ref in refs[n * count : (n + 1) * count]:
            total = ref[...] if total is None else total + ref[...]
        refs[-outs + n][...] = total


def add_shares(info, sources, columns, rows, after, limit):
    cols = sources[0].shape[1]
    parts = 1
    while rows // parts * cols > 300000 and rows % (16 * parts) == 0:
        parts *= 2
    block = (rows // parts, cols)

    def spec(source, column):
        if column is None:
            return pl.BlockSpec(block, lambda g, i: (g, 0))
        return pl.BlockSpec(block, lambda g, i: (i[column] * parts + g, 0))

    outs = len(columns)
    return pl.pallas_call(
        functools.partial(add_kernel, len(sources), outs),
        grid_spec=pltpu.PrefetchScalarGridSpec(
            num_scalar_prefetch=1,
            grid=(parts,),
            in_specs=[spec(*pair) for line in columns for pair in zip(sources, line)] + [ANYWHERE] * len(after),
            out_specs=[pl.BlockSpec(block, lambda g, i: (g, 0))] * outs,
        ),
        out_shape=[jax.ShapeDtypeStruct((rows, cols), F32)] * outs,
        cost_estimate=LITTLE,
        compiler_params=params(limit),
        name="add_shares",
    )(info, *sources * outs, *after)


def join_kernel(column, ways, info_ref, *refs):
    pieces, out_ref, sems = refs[:ways], refs[-2], refs[-1]
    rows = pieces[0].shape[0]
    copies = []
    for step, piece in enumerate(pieces):
        at = pl.multiple_of((info_ref[column] ^ step) * rows, 8)
        copies.append(pltpu.make_async_copy(piece, out_ref.at[pl.ds(at, rows), :], sems.at[step]))
        copies[-1].start()
    for copy in copies:
        copy.wait()


def join(info, column, pieces, after):
    rows, cols = pieces[0].shape
    ways = len(pieces)
    return pl.pallas_call(
        functools.partial(join_kernel, column, ways),
        in_specs=[pl.BlockSpec(memory_space=pltpu.SMEM)] + [ANYWHERE] * (ways + len(after)),
        out_specs=pl.BlockSpec(memory_space=pltpu.VMEM),
        out_shape=jax.ShapeDtypeStruct((ways * rows, cols), F32),
        scratch_shapes=[pltpu.SemaphoreType.DMA((ways,))],
        cost_estimate=LITTLE,
        compiler_params=params(SMALL),
        name="join",
    )(info, *pieces, *after)


class Sum:
    def __init__(self, route, keep, send):
        self.route = route
        self.parts = [keep, swap_cores(send)]
        self.begins = [0, 0]
        self.shares = [keep.shape[0]]
        for ways in route.ways:
            if self.shares[-1] % (8 * ways):
                break
            self.shares.append(self.shares[-1] // ways)
        self.divided = len(self.shares) - 1
        self.phase = 0
        self.steps = (
            [self.send] * self.divided
            + [self.finish]
            + [self.add] * (route.count - self.divided)
            + [self.join] * (self.divided - 1)
            + [self.swap]
        )

    def advance(self, after):
        return self.steps.pop(0)(after) if self.steps else after

    def send(self, after):
        phase = self.phase
        flips = (1,) if phase == 0 else (1, 0)
        columns = [[self.route.columns[begin, phase + 1, flip] for begin in self.begins] for flip in flips]
        limit = VMEM if phase < 2 else SMALL
        outs = add_shares(self.route.info, self.parts, columns, self.shares[phase + 1], after, limit)
        got = self.route.exchange(outs[0], phase, 1)
        if phase == 0:
            self.parts.append(got)
            self.begins.append(1)
        else:
            self.parts = [outs[1], got]
            self.begins = [phase + 1] * 2
        self.phase += 1
        return (outs[0],)

    def finish(self, after):
        columns = [[self.route.columns.get((begin, self.phase, 0)) for begin in self.begins]]
        (self.piece,) = add_shares(self.route.info, self.parts, columns, self.shares[self.phase], after, SMALL)
        return self.gather()

    def gather(self):
        if self.divided <= self.phase < self.route.count:
            phase = self.phase
        else:
            phase = self.phase = min(self.phase, self.divided) - 1
        self.got = self.route.exchange(self.piece, phase, 1)
        if self.phase == 0:
            self.far_piece = swap_cores(self.piece)
            return (self.piece, (self.far_piece,))
        return (self.piece,)

    def add(self, after):
        parts = [self.piece, self.got]
        (self.piece,) = add_shares(self.route.info, parts, [[None] * 2], self.piece.shape[0], after, SMALL)
        self.phase += 1
        return self.gather()

    def join(self, after):
        self.piece = join(self.route.info, self.route.place_column + self.phase, [self.piece, self.got], after)
        return self.gather()

    def swap(self, after):
        self.sources = (self.piece, self.got, self.far_piece, swap_cores(self.got))
        return (self.got,)


SPACE = 10**11


def spacer_kernel(*refs):
    refs[-1][...] = jnp.zeros_like(refs[-1])


def spacer(after):
    return pl.pallas_call(
        spacer_kernel,
        in_specs=[ANYWHERE] * len(after),
        out_specs=pl.BlockSpec(memory_space=pltpu.VMEM),
        out_shape=jax.ShapeDtypeStruct((8, 128), F32),
        cost_estimate=pl.CostEstimate(flops=SPACE, transcendentals=0, bytes_accessed=1),
        name="spacer",
    )(*after)


class SmallSum:
    def __init__(self, route, values):
        self.route = route
        self.shapes = [v.shape for v in values]
        flat = jnp.concatenate([v.reshape(-1) for v in values])
        self.sum = jnp.pad(flat, (0, -flat.shape[0] % 2048)).reshape(-1, 256)
        self.steps = [functools.partial(route.exchange, phase=p, step=1) for p in range(route.count)] + [swap_cores]
        self.got = self.steps.pop(0)(self.sum)

    def advance(self, after):
        if self.got is None:
            return after
        (self.sum,) = add_shares(self.route.info, [self.sum, self.got], [[None, None]], self.sum.shape[0], after, SMALL)
        self.got = self.steps.pop(0)(self.sum) if self.steps else None
        return (self.sum,)

    def values(self):
        while self.got is not None:
            self.advance(())
        flat, at, out = self.sum.reshape(-1), 0, []
        for shape in self.shapes:
            size = int(np.prod(shape))
            out.append(flat[at : at + size].reshape(shape))
            at += size
        return out


def assemble_kernel(spread, n_outs, info_ref, *refs):
    sources, outs = refs[:4], refs[-n_outs:]
    target, half = pl.program_id(0), pl.program_id(1)
    for n in range(4):
        for t in range(2):

            @pl.when((info_ref[2 + n] == 2 * target + half) & (target == t))
            def _():
                spread(t, sources[n], outs)


def assemble(info, slabs, spread, outs, blocks, sources, group, earlier, after):
    rows, cols = sources[0].shape
    count = slabs // 2 // group

    def source_spec(n):
        def index(t, h, j, i):
            stage, now = i[2 + n], 2 * t + h
            return jnp.where(now < stage, 0, jnp.where(now == stage, j, count - 1)), 0

        return pl.BlockSpec((rows // count, cols), index)

    def out_spec(target, block, row, column):
        def index(t, h, j, i):
            if target is None:
                return row + (2 * t + h) * count + j, column
            return row + jnp.where(t == target, h * count + j, 0 if target else 2 * count - 1), column

        return pl.BlockSpec(block, index)

    return pl.pallas_call(
        functools.partial(assemble_kernel, spread, len(outs)),
        grid_spec=pltpu.PrefetchScalarGridSpec(
            num_scalar_prefetch=1,
            grid=(2, 2, count),
            in_specs=[source_spec(n) for n in range(4)] + [ANYWHERE] * (len(earlier) + len(after)),
            out_specs=[out_spec(*b) for b in blocks],
        ),
        out_shape=[jax.ShapeDtypeStruct(s, F32) for s in outs],
        cost_estimate=COST,
        input_output_aliases={5 + i: i for i in range(len(earlier))},
        compiler_params=params(),
        name="assemble",
    )(info, *sources, *earlier, *after)


def ffn_spread(width, size, slabs, group, target, source, outs):
    n, total = (size // 256, width) if target == 0 else (width // 256, size)
    rows = total // slabs
    for s in range(group):
        for j in range(n):
            at = (s * n + j) * rows
            outs[target][s * rows : (s + 1) * rows, j * 256 : (j + 1) * 256] = source[at : at + rows, :]


def attn_spread(columns, slabs, group, target, source, outs):
    n = len(columns)
    rows = source.shape[0] // (group * n)
    for s in range(group):
        for j, (out, column) in enumerate(columns):
            at = (s * n + j) * rows
            outs[out][s * rows : (s + 1) * rows, column : column + source.shape[1]] = source[at : at + rows, :]


ORDER = ("D", "F0", "s0", "F1", "s0", "B0", "s1", "s0", "B1", "s0", "s1", "s2", "D", "s0", "s3", "s1", "s0", "T", "s3", "s1", "s0", "D", "s3", "s3", "s2", "m", "s1", "m", "s0", "D", "s3", "m", "s1", "s3", "m", "s2", "s3", "s1", "s3", "D", "m", "s2", "s2", "s3", "s0", "s1", "s0", "s2", "s2", "s2", "s3", "s1", "s1", "s2", "D", "s2")


def on_device(tokens, lengths, attn_gain, wq, wk, wv, wo, table, ffn_gain, w_in, w_out, out_grad, *, size):
    rows, seq, width = tokens.shape
    buckets, heads = table.shape
    pairs = heads // 2
    ff = w_in.shape[1]
    slabs = 16
    rest = [(bit,) for bit in range(2, size.bit_length() - 1)]
    route = Route(size, [(0,), (1,)] + rest, [(1,), (0,)] + rest)
    info = route.info
    lane_buckets = band_buckets(buckets)
    onehot = np.arange(buckets)[:, None] == lane_buckets[None, :]
    band = jnp.einsum("bh,bm->hm", table, jnp.asarray(onehot, BF16), preferred_element_type=F32)
    flat = lambda a: a.reshape(rows * seq, a.shape[2])
    tall = lambda a: a.reshape(rows, seq, width)
    chunks, sub = 2, 768
    part = ff // chunks
    ends = bucket_of(np.array([-2 * TILE] * TILE + [2 * TILE] * TILE), buckets)
    spread = (np.concatenate([lane_buckets, ends])[:, None] == np.arange(buckets)[None, :]).astype(np.float32)

    h1T, q, k, v, attT, lse, x1, h2 = attn_fwd(tokens, lengths, attn_gain, ffn_gain, wq, wk, wv, wo, band)
    acc, sums, after, ds, diags = (), [], (), [], []
    ffn_grads, attn_grads = (), ()
    def put(which, after):
        nonlocal ffn_grads, attn_grads
        group = 8
        sources = sums[which].sources
        if which < chunks:
            ffn_grads = assemble(
                info, slabs, functools.partial(ffn_spread, width, part, slabs, group), [w_in.shape, w_out.shape],
                [(0, (width // slabs * group, part), 0, which), (1, (part // slabs * group, width), which * (slabs // group), 0)],
                sources, group, tuple(ffn_grads), after,
            )
            return (ffn_grads[0],)
        half = which - chunks
        block = width // 2 // slabs * group
        columns = [(0, 0), (1, 0), (2, 0)] + [(3, 0), (3, width // 2)] * (half == 0)
        blocks = [(None, (block, width // 2), 0, half)] * 3 + [(None, (block, width), 0, 0)] * (half == 0)
        made = assemble(
            info, slabs, functools.partial(attn_spread, columns, slabs, group), [wq.shape] * len(blocks), blocks,
            sources, group, tuple(attn_grads[:3]), after,
        )
        attn_grads = list(made) + list(attn_grads[3:])
        return (made[0],)

    late = []
    for at, op in enumerate(ORDER):
        if late:
            after = (*after, *late.pop(0))
        which = int(op[1]) if len(op) > 1 else 0
        if op[0] == "F":
            end = (flat(x1), ffn_gain, attT, wo) if which == chunks - 1 else None
            keep, send, *acc = ffn_chunk(
                info, lengths, slabs, flat(h2), flat(out_grad), w_in, w_out, which * part, part, sub, acc, after, end
            )
            sums.append(Sum(route, keep, send))
            if end:
                mixed, dres, datt, gwo, ggain2 = acc
            after = (keep,)
        elif op[0] == "B":
            half = pairs // 2
            more = [] if which else [gwo]
            dq, dk, dv, diag, keep, send = attn_bwd(
                info, lengths, slabs, q, k, v, tall(datt), lse, band, h1T, which * half, half, more, after
            )
            ds += [flat(dq), flat(dk), flat(dv)]
            diags.append(diag)
            sums.append(Sum(route, keep, send))
            after = (keep,)
        elif op == "T":
            tgrad, ggain1 = tokgrad(flat(tokens), dres, attn_gain, ds, wq, wk, wv, after)
            diag = jnp.concatenate(diags).reshape(heads, 6 * TILE)
            gtable = jnp.einsum("hm,mb->bh", diag, jnp.asarray(spread), precision=lax.Precision.HIGHEST)
            small = SmallSum(route, (ggain1, ggain2, gtable))
            after = (ggain1,)
        elif op == "D":
            after = (spacer(after),)
        elif op == "m":
            after = small.advance(after)
        else:
            after = sums[which].advance(after)
            if isinstance(after[-1], tuple):
                late, after = [(), after[-1]], after[:-1]
            if ORDER[at:].count(op) == 1:
                while sums[which].steps:
                    after = sums[which].advance(after)
                after = put(which, after)
    ggain1, ggain2, gtable = small.values()
    return (tall(mixed), tall(tgrad), ggain1[0], *attn_grads, gtable, ggain2[0], *ffn_grads)


def solution(mesh):
    split = P(("rows", "blk"))
    return jax.shard_map(
        functools.partial(on_device, size=mesh.shape["rows"]),
        mesh=mesh,
        in_specs=(split, split) + (P(),) * 9 + (split,),
        out_specs=(split, split) + (P(),) * 9,
        check_vma=False,
    )
```

```python
import functools
import jax
import jax.numpy as jnp
import numpy as np
from jax import lax
from jax.experimental import pallas as pl
from jax.experimental.pallas import tpu as pltpu
from jax.sharding import PartitionSpec as P

NT = (((1,), (1,)), ((), ()))
TN = (((0,), (0,)), ((), ()))
F32, BF16 = jnp.float32, jnp.bfloat16
TILE = 128
MASKED = -1000000000.0
EPS = 1e-06
far_steps = np.array([12, 16, 23, 32, 46, 64, 91], dtype=np.int32)


def dot(a, b, dims=None):
    if dims is None:
        return jnp.dot(a, b, preferred_element_type=F32)
    return lax.dot_general(a, b, dims, preferred_element_type=F32)


def bucket_of(relative, bucket_count):
    distance = np.abs(relative)
    beyond = np.sum(distance[..., None] >= far_steps, axis=-1)
    inner = np.where(distance < bucket_count // 4, distance, bucket_count // 4 + beyond)
    return np.where(relative > 0, bucket_count // 2, 0) + inner


def band_buckets(bucket_count):
    lanes = np.arange(4 * TILE)
    offsets = np.where(lanes < 2 * TILE, lanes, lanes - 4 * TILE)
    return bucket_of(-offsets, bucket_count)


def segments_along(len_ref, row, shape, axis, start=0):
    at = lax.broadcasted_iota(jnp.int32, shape, axis) + start
    total = jnp.zeros(shape, jnp.int32)
    end = jnp.int32(0)
    for j in range(len_ref.shape[1]):
        end = end + len_ref[row, j]
        total = total + jnp.where(at >= end, 1, 0)
    return total


def fill_mask(len_ref, row, mask_ref, last):
    seq = mask_ref.shape[0]
    of_q = segments_along(len_ref, row, (1, seq), 1)
    of_k = segments_along(len_ref, row, (seq, TILE), 0)
    of_k = jnp.where(of_k < last, of_k, -1)
    for j in range(seq // TILE):
        same = of_k == of_q[:, j * TILE : (j + 1) * TILE]
        mask_ref[:, j * TILE : (j + 1) * TILE] = jnp.where(same, 0.0, MASKED)
    return of_q < last


def band_of(vector):
    wide = jnp.broadcast_to(vector, (TILE, 4 * TILE))
    return pltpu.roll(wide, 0, 1, stride=1, stride_axis=0)


def bias_row(band, vector, ki, count):
    shape = (TILE, TILE)
    tiles = []
    for qi in range(count):
        step = ki - qi
        if step == 0:
            tiles.append(band[:, 0:TILE])
        elif step == -1:
            tiles.append(band[:, TILE : 2 * TILE])
        elif step == 1:
            tiles.append(band[:, 3 * TILE : 4 * TILE])
        elif step < 0:
            tiles.append(jnp.broadcast_to(vector[:, 2 * TILE - 1 : 2 * TILE], shape))
        else:
            tiles.append(jnp.broadcast_to(vector[:, 2 * TILE : 2 * TILE + 1], shape))
    return jnp.concatenate(tiles, axis=1)


def norm_scale(value):
    return lax.rsqrt(jnp.mean(value * value, axis=-1, keepdims=True) + EPS)


def row_of(gain_ref):
    return gain_ref[...].astype(F32).reshape(1, gain_ref.shape[0])


VMEM = 63 * 2**20
ANYWHERE = pl.BlockSpec(memory_space=pl.ANY)
OUTSIDE = pl.BlockSpec(memory_space=pltpu.HBM)
FLOPS = 10**11
LITTLE = pl.CostEstimate(flops=1, transcendentals=0, bytes_accessed=1)
COST = pl.CostEstimate(flops=FLOPS, transcendentals=0, bytes_accessed=1)


def unused(arrays):
    return [OUTSIDE if a.size >= 2**18 else ANYWHERE for a in arrays]


def params(limit=VMEM):
    return pltpu.CompilerParams(vmem_limit_bytes=limit)


def attn_fwd_kernel(
    len_ref, tok_ref, gain1_ref, gain2_ref, wq_ref, wk_ref, wv_ref, wo_ref, band_ref,
    h1T_ref, q_ref, k_ref, v_ref, attT_ref, lse_ref, x1_ref, h2_ref,
    att_ref, mask_ref, s_ref, p_ref,
):
    seq, width = tok_ref.shape[1:]
    pairs = width // TILE
    head = TILE // 2
    row = pl.program_id(0)
    valid = fill_mask(len_ref, row, mask_ref, len_ref.shape[1] - 1)
    tok = tok_ref[0].astype(F32)
    h1 = (tok * norm_scale(tok) * row_of(gain1_ref)).astype(BF16)
    h1T_ref[0] = h1.T
    q_ref[0] = dot(h1, wq_ref[...]).astype(BF16)
    k_ref[0] = dot(h1, wk_ref[...]).astype(BF16)
    v_ref[0] = dot(h1, wv_ref[...]).astype(BF16)
    count = seq // TILE
    low_half = lax.broadcasted_iota(jnp.int32, (1, TILE), 1) < head

    def pair(p, carry):
        lanes = pl.ds(pl.multiple_of(p * TILE, TILE), TILE)
        qp, kp, vp = q_ref[0, :, lanes], k_ref[0, :, lanes], v_ref[0, :, lanes]
        vT = vp.T
        tops = []
        for a in range(2):
            qm = jnp.where(low_half if a == 0 else ~low_half, qp, jnp.zeros_like(qp))
            vector = band_ref[pl.ds(2 * p + a, 1), :]
            band = band_of(vector)
            top = None
            for ki in range(count):
                rows = slice(ki * TILE, (ki + 1) * TILE)
                s = dot(kp[rows], qm, NT) + bias_row(band, vector, ki, count) + mask_ref[rows, :]
                s_ref[a, rows, :] = s
                most = jnp.max(s, axis=0, keepdims=True)
                top = most if top is None else jnp.maximum(top, most)
            tops.append(top)
        totals = []
        for a, top in enumerate(tops):
            total = jnp.zeros_like(top)
            for ki in range(count):
                rows = slice(ki * TILE, (ki + 1) * TILE)
                e = jnp.exp(s_ref[a, rows, :] - top)
                total = total + jnp.sum(e, axis=0, keepdims=True)
                p_ref[a, rows, :] = e.astype(BF16)
            totals.append(total)
        outs = []
        for a, (top, total) in enumerate(zip(tops, totals)):
            o = dot(vT[a * head : (a + 1) * head], p_ref[a])
            outs.append(jnp.where(valid, o / total, 0.0))
            lse_ref[0, pl.ds(2 * p + a, 1), :] = top + jnp.log(total)
        both = jnp.concatenate(outs, axis=0)
        attT_ref[0, lanes, :] = both.astype(BF16)
        att_ref[:, lanes] = both.T.astype(BF16)
        return carry

    lax.fori_loop(0, pairs, pair, 0, unroll=6)
    x1 = tok_ref[0].astype(F32) + dot(att_ref[...], wo_ref[...])
    x1_ref[0] = x1
    h2_ref[0] = (x1 * norm_scale(x1) * row_of(gain2_ref)).astype(BF16)


def attn_fwd(tokens, lengths, gain1, gain2, wq, wk, wv, wo, band):
    rows, seq, width = tokens.shape
    heads = band.shape[0]
    full = lambda a: pl.BlockSpec(a.shape, lambda r, l: (0,) * a.ndim, pipeline_mode=pl.Buffered(1))
    per_row = lambda *s: pl.BlockSpec((1,) + s, lambda r, l: (r,) + (0,) * len(s))
    tall = jax.ShapeDtypeStruct((rows, seq, width), BF16)
    turned = jax.ShapeDtypeStruct((rows, width, seq), BF16)
    return pl.pallas_call(
        attn_fwd_kernel,
        grid_spec=pltpu.PrefetchScalarGridSpec(
            num_scalar_prefetch=1,
            grid=(rows,),
            in_specs=[per_row(seq, width)] + [full(a) for a in (gain1, gain2, wq, wk, wv, wo, band)],
            out_specs=[per_row(width, seq)]
            + [per_row(seq, width)] * 3
            + [per_row(width, seq), per_row(heads, seq), per_row(seq, width), per_row(seq, width)],
            scratch_shapes=[
                pltpu.VMEM((seq, width), BF16),
                pltpu.VMEM((seq, seq), F32),
                pltpu.VMEM((2, seq, seq), F32),
                pltpu.VMEM((2, seq, seq), BF16),
            ],
        ),
        out_shape=[turned, tall, tall, tall, turned]
        + [jax.ShapeDtypeStruct((rows, heads, seq), F32), jax.ShapeDtypeStruct((rows, seq, width), F32), tall],
        cost_estimate=COST,
        compiler_params=params(),
        name="attn_fwd",
    )(lengths, tokens, gain1, gain2, wq, wk, wv, wo, band)


GELU_C = float(np.sqrt(2.0 / np.pi))


def gelu_pair(v):
    v2 = v * v
    t = jnp.tanh(GELU_C * v * (1.0 + 0.044715 * v2))
    half = 0.5 * (1.0 + t)
    slope = half + (0.5 * GELU_C) * v * (1.0 - t * t) * (1.0 + (3 * 0.044715) * v2)
    return v * half, slope


def place(core, mine, other, keep, send, sems):
    both = lambda a, b: [(src, dst, sems.at[n, i]) for n, pairs in enumerate((a, b)) for i, (src, dst) in enumerate(pairs)]
    return [(core == 0, both(mine(keep), other(send))), (core != 0, both(mine(send), other(keep)))]


def run_all(cases, action):
    for condition, copies in cases:

        @pl.when(condition)
        def _():
            for src, dst, sem in copies:
                getattr(pltpu.make_async_copy(src, dst, sem), action)()


def ffn_kernel(steps, slabs, first, last, info_ref, len_ref, h2_ref, dy_ref, win_ref, wout_ref, *refs):
    refs = list(refs)
    acc_in = [] if first else [refs.pop(0), refs.pop(0)]
    if last:
        gain_ref, late = refs[0], refs[1:4]
        keep_ref, send_ref, mixed_out, dres_out, datt_out, gwo_ref, ggain_ref = refs[-22:-15]
        mix_ref, dtwo_ref, h2T_ref, act_ref, dpre_ref, gin_ref, gout_ref, sems, acc_sems, mixed_ref, dres_ref, datt_ref = refs[-15:-3]
        x1_ref, attT_ref, wo_ref = refs[-3:]
        first_late = acc_sems.shape[0] - 3
        late = [pltpu.make_async_copy(a, b, acc_sems.at[first_late + i]) for i, (a, b) in enumerate(zip(late, refs[-3:]))]
    else:
        keep_ref, send_ref = refs[-13:-11]
        acc_out = refs[-11:-9]
        mix_ref, dtwo_ref, h2T_ref, act_ref, dpre_ref, gin_ref, gout_ref, sems, acc_sems = refs[-9:]
    step = pl.program_id(0)
    toks, width = h2_ref.shape
    sub = win_ref.shape[1]
    wide, tall = width // 256, sub // 256
    in_rows, out_rows = width // slabs, sub * steps // slabs
    piece = in_rows * tall * steps
    here = slabs // steps
    totals = (mix_ref, dtwo_ref)

    def moves(at):
        def of_in(ref):
            return [
                (
                    gin_ref.at[at, i * in_rows * tall : (i + 1) * in_rows * tall, :],
                    ref.at[pl.ds(pl.multiple_of(i * piece + at * (in_rows * tall), 8), in_rows * tall), :],
                )
                for i in range(slabs)
            ]

        def of_out(ref):
            return [(gout_ref.at[at], ref.at[pl.ds(pl.multiple_of(at * (here * piece), 8), here * piece), :])]

        return place(info_ref[0], of_in, of_out, keep_ref, send_ref, sems.at[at])

    @pl.when(step == 0)
    def _():
        for i, ref in enumerate(acc_in):
            pltpu.make_async_copy(ref, totals[i], acc_sems.at[i]).start()
        if last:
            for copy in late:
                copy.start()
        h2T_ref[...] = h2_ref[...].T

    pre = dot(h2_ref[...], win_ref[...])
    dact = dot(dy_ref[...], wout_ref[...], NT)
    act, slope = gelu_pair(pre)
    act_ref[...] = act.astype(BF16)
    dpre_ref[...] = (dact * slope).astype(BF16)
    mix = dot(act_ref[...], wout_ref[...])
    dtwo = dot(dpre_ref[...], win_ref[...], NT)

    @pl.when(step == 0)
    def _():
        if first:
            mix_ref[...] = mix
            dtwo_ref[...] = dtwo
        else:
            for i, ref in enumerate(acc_in):
                pltpu.make_async_copy(ref, totals[i], acc_sems.at[i]).wait()
            mix_ref[...] += mix
            dtwo_ref[...] += dtwo

    @pl.when(step > 0)
    def _():
        mix_ref[...] += mix
        dtwo_ref[...] += dtwo

    if not last:

        @pl.when(step == steps - 1)
        def _():
            for i in range(2):
                pltpu.make_async_copy(totals[i], acc_out[i], acc_sems.at[2 + i]).start()

    gout = dot(act_ref[...], dy_ref[...], TN)
    for i in range(here):
        for j in range(wide):
            at = (i * wide + j) * out_rows
            gout_ref[step, at : at + out_rows, :] = gout[i * out_rows : (i + 1) * out_rows, j * 256 : (j + 1) * 256]
    gin = dot(h2T_ref[...], dpre_ref[...])
    for i in range(slabs):
        for j in range(tall):
            at = (i * tall + j) * in_rows
            gin_ref[step, at : at + in_rows, :] = gin[i * in_rows : (i + 1) * in_rows, j * 256 : (j + 1) * 256]
    run_all(moves(step), "start")

    @pl.when(step == steps - 1)
    def _():
        if last:
            for copy in late:
                copy.wait()
            rows = len_ref.shape[0]
            seq = toks // rows
            block = 256
            copies = []
            ggain = None
            for b in range(toks // block):
                here_toks = slice(b * block, (b + 1) * block)
                x1, back = x1_ref[here_toks, :], dtwo_ref[here_toks, :]
                mixed_ref[here_toks, :] = (x1 + mix_ref[here_toks, :]).astype(BF16)
                s = norm_scale(x1)
                g = row_of(gain_ref) * back
                dres = dy_ref[here_toks, :].astype(F32) + s * g - x1 * (s * s * s * jnp.mean(x1 * g, axis=-1, keepdims=True))
                dres_ref[here_toks, :] = dres
                some = jnp.sum(back * x1 * s, axis=0, keepdims=True)
                ggain = some if ggain is None else ggain + some
                dbranch = dres.astype(BF16)
                act_ref[here_toks, :] = dbranch
                datt = dot(dbranch, wo_ref[...], NT)
                seg = segments_along(len_ref, b * block // seq, (block, TILE), 0, b * block % seq)[:, :1]
                datt_ref[here_toks, :] = jnp.where(seg < len_ref.shape[1] - 1, datt, 0.0).astype(BF16)
                for n, (src, dst) in enumerate(((mixed_ref, mixed_out), (dres_ref, dres_out), (datt_ref, datt_out))):
                    copies.append(pltpu.make_async_copy(src.at[here_toks, :], dst.at[here_toks, :], acc_sems.at[4 + 3 * b + n]))
                    copies[-1].start()
            ggain_ref[...] = ggain
            gwo = None
            for r in range(rows):
                part = dot(attT_ref[r], act_ref[r * seq : (r + 1) * seq, :])
                gwo = part if gwo is None else gwo + part
            gwo_ref[...] = gwo
            for copy in copies:
                copy.wait()
        else:
            for i in range(2):
                pltpu.make_async_copy(totals[i], acc_out[i], acc_sems.at[2 + i]).wait()
        for at in range(steps):
            run_all(moves(at), "wait")


def ffn_chunk(info, lengths, slabs, h2, dy, w_in, w_out, start, size, sub, acc, after, rest=None):
    toks, width = h2.shape
    base = start // sub
    steps = size // sub
    piece = width * (sub // 256)
    full = lambda a: pl.BlockSpec(a.shape, lambda s, *_: (0,) * a.ndim, pipeline_mode=pl.Buffered(1))
    f32 = lambda *s: jax.ShapeDtypeStruct(s, F32)
    out_specs = [ANYWHERE] * 2
    out_shape = [f32(steps * piece, 256)] * 2
    scratch = [
        pltpu.VMEM((toks, width), F32),
        pltpu.VMEM((toks, width), F32),
        pltpu.VMEM((width, toks), BF16),
        pltpu.VMEM((toks, sub), BF16),
        pltpu.VMEM((toks, sub), BF16),
        pltpu.VMEM((steps, piece, 256), F32),
        pltpu.VMEM((steps, piece, 256), F32),
        pltpu.SemaphoreType.DMA((steps, 2, slabs)),
        pltpu.SemaphoreType.DMA((7 + 3 * (toks // 256),)),
    ]
    if rest is None:
        rest, gain = (), ()
        out_specs += [ANYWHERE] * 2
        out_shape += [f32(toks, width)] * 2
    else:
        gain, *rest = rest
        gain = (gain,)
        low = jax.ShapeDtypeStruct((toks, width), BF16)
        whole = lambda s: pl.BlockSpec(s.shape, lambda *_: (0,) * len(s.shape), pipeline_mode=pl.Buffered(1))
        gwo, ggain = f32(width, width), f32(1, width)
        out_specs += [ANYWHERE] * 3 + [whole(gwo), whole(ggain)]
        out_shape += [low, f32(toks, width), low, gwo, ggain]
        scratch += [pltpu.VMEM((toks, width), BF16), pltpu.VMEM((toks, width), F32), pltpu.VMEM((toks, width), BF16)]
        scratch += [pltpu.VMEM(a.shape, a.dtype) for a in rest]
    return pl.pallas_call(
        functools.partial(ffn_kernel, steps, slabs, not acc, bool(rest)),
        grid_spec=pltpu.PrefetchScalarGridSpec(
            num_scalar_prefetch=2,
            grid=(steps,),
            in_specs=[
                full(h2),
                full(dy),
                pl.BlockSpec((width, sub), lambda s, *_: (0, base + s)),
                pl.BlockSpec((sub, width), lambda s, *_: (base + s, 0)),
            ]
            + [ANYWHERE] * len(acc)
            + [full(a) for a in gain]
            + [ANYWHERE] * len(rest)
            + unused(after),
            out_specs=out_specs,
            scratch_shapes=scratch,
        ),
        out_shape=out_shape,
        cost_estimate=COST,
        compiler_params=params(),
        name="ffn",
    )(info, lengths, h2, dy, w_in, w_out, *acc, *gain, *rest, *after)


def diagonal_sums(x):
    depth, lanes = x.shape
    total = x[0:8]
    for g in range(8, depth, 8):
        total = total + pltpu.roll(x[g : g + 8], lanes - g, 1)
    at = lax.broadcasted_iota(jnp.int32, (8, lanes), 0)
    for bit in (1, 2, 4):
        total = jnp.where((at & bit) != 0, pltpu.roll(total, lanes - bit, 1), total)
    return jnp.sum(total, axis=0, keepdims=True)


def attn_bwd_kernel(slabs, first, n_more, info_ref, len_ref, q_ref, k_ref, v_ref, do_ref, lse_ref, band_ref, h1T_ref, *refs):
    more = refs[:n_more]
    dq_ref, dk_ref, dv_ref, diag_ref, keep_ref, send_ref = refs[-14:-8]
    mask_ref, p_ref, low_ref, dp_ref, ds_ref, d_ref, g_ref, sems = refs[-8:]
    pair, pairs = pl.program_id(0), pl.num_programs(0)
    rows, seq = q_ref.shape[:2]
    head = TILE // 2
    count = seq // TILE
    width, cols = h1T_ref.shape[1], g_ref.shape[2]
    stripes = keep_ref.shape[0] * 2 // width
    share = width // 2 // slabs

    def put(j, block):
        for c in range(2):
            for s in range(slabs):
                at, begin = (s * stripes + j) * share, (c * slabs + s) * share
                g_ref[c, at : at + share, :] = block[begin : begin + share]

    @pl.when(pair == 0)
    def _():
        for row in range(rows):
            fill_mask(len_ref, row, mask_ref.at[row], len_ref.shape[1] - 1)

    low_half = lax.broadcasted_iota(jnp.int32, (1, TILE), 1) < head
    bands = []
    for a in range(2):
        vector = band_ref[pl.ds(2 * (first + pair) + a, 1), :]
        bands.append((vector, band_of(vector)))
    sides = []
    for n in range(2 * rows):
        row, a = n // 2, n % 2
        qp, kp, vp, dop = q_ref[row], k_ref[row], v_ref[row], do_ref[row]
        own = low_half if a == 0 else ~low_half
        qm = jnp.where(own, qp, jnp.zeros_like(qp))
        dom = jnp.where(own, dop, jnp.zeros_like(dop))
        vector, band = bands[a]
        lse = lse_ref[row, pl.ds(2 * (first + pair) + a, 1), :]
        delta = jnp.zeros((1, seq), F32)
        for ki in range(count):
            some = slice(ki * TILE, (ki + 1) * TILE)
            s = dot(kp[some], qm, NT) + bias_row(band, vector, ki, count) + mask_ref[row, some, :]
            prob = jnp.exp(s - lse)
            dp = dot(vp[some], dom, NT)
            delta = delta + jnp.sum(prob * dp, axis=0, keepdims=True)
            p_ref[n, some, :] = prob
            low_ref[n, some, :] = prob.astype(BF16)
            dp_ref[n, some, :] = dp
        sides.append((qm, dom, delta))
    sums = [{}, {}]
    for n, (_, _, delta) in enumerate(sides):
        near = sums[n % 2]
        for ki in range(count):
            some = slice(ki * TILE, (ki + 1) * TILE)
            ds = p_ref[n, some, :] * (dp_ref[n, some, :] - delta)
            ds_ref[n, some, :] = ds.astype(BF16)
            for qi in range(count):
                step = max(-2, min(2, ki - qi))
                tile = ds[:, qi * TILE : (qi + 1) * TILE]
                near[step] = tile if step not in near else near[step] + tile
    for a, near in enumerate(sums):
        zero = jnp.zeros((TILE, TILE), F32)
        band = jnp.concatenate([near[0], near[-1], zero, near[1]], axis=1)
        diag_ref[0, a : a + 1, : 4 * TILE] = diagonal_sums(band)
        ends = jnp.concatenate([near[-2], near[2]], axis=1)
        diag_ref[0, a : a + 1, 4 * TILE :] = jnp.sum(ends, axis=0, keepdims=True)
    lanes = pl.ds(pl.multiple_of(pair * TILE, TILE), TILE)
    for row in range(rows):
        kT = k_ref[row].T
        dqT, dk, dv = [], None, None
        for a in range(2):
            n = 2 * row + a
            qm, dom, _ = sides[n]
            dva = dot(low_ref[n], dom)
            dka = dot(ds_ref[n], qm)
            dv = dva if dv is None else dv + dva
            dk = dka if dk is None else dk + dka
            dqT.append(dot(kT[a * head : (a + 1) * head], ds_ref[n]))
        dq = jnp.concatenate(dqT, axis=0).T.astype(BF16)
        dk, dv = dk.astype(BF16), dv.astype(BF16)
        dq_ref[row], dk_ref[row], dv_ref[row] = dq, dk, dv
        for j, d in enumerate((dq, dk, dv)):
            d_ref[j, row, :, lanes] = d

    @pl.when(pair == pairs - 1)
    def _():
        for j in range(3):
            g = None
            for r in range(h1T_ref.shape[0]):
                part = dot(h1T_ref[r], d_ref[j, r])
                g = part if g is None else g + part
            put(j, g)
        for j in range(stripes - 3):
            put(3 + j, more[0][:, j * cols : (j + 1) * cols])
        moves = place(
            info_ref[0], lambda ref: [(g_ref.at[0], ref)], lambda ref: [(g_ref.at[1], ref)], keep_ref, send_ref, sems
        )
        run_all(moves, "start")
        run_all(moves, "wait")


def attn_bwd(info, lengths, slabs, q, k, v, do, lse, band, h1T, first, pairs, more, after):
    rows, seq, width = q.shape
    cols = pairs * TILE
    half = width // 2 * (3 + sum(m.shape[1] // cols for m in more))
    tall = pl.BlockSpec((rows, seq, TILE), lambda p, *_: (0, 0, first + p))
    tall_out = pl.BlockSpec((rows, seq, TILE), lambda p, *_: (0, 0, p))
    full = lambda a: pl.BlockSpec(a.shape, lambda *_: (0,) * a.ndim, pipeline_mode=pl.Buffered(1))
    out = jax.ShapeDtypeStruct((rows, seq, cols), BF16)
    square = lambda dtype: pltpu.VMEM((2 * rows, seq, seq), dtype)
    return pl.pallas_call(
        functools.partial(attn_bwd_kernel, slabs, first, len(more)),
        grid_spec=pltpu.PrefetchScalarGridSpec(
            num_scalar_prefetch=2,
            grid=(pairs,),
            in_specs=[tall] * 4
            + [full(lse), full(band), full(h1T)]
            + [full(m) for m in more]
            + unused(after),
            out_specs=[tall_out] * 3 + [pl.BlockSpec((1, 2, 6 * TILE), lambda p, *_: (p, 0, 0))] + [ANYWHERE] * 2,
            scratch_shapes=[
                pltpu.VMEM((rows, seq, seq), F32),
                square(F32),
                square(BF16),
                square(F32),
                square(BF16),
                pltpu.VMEM((3, rows, seq, cols), BF16),
                pltpu.VMEM((2, half, cols), F32),
                pltpu.SemaphoreType.DMA((2, 1)),
            ],
        ),
        out_shape=[out] * 3
        + [jax.ShapeDtypeStruct((pairs, 2, 6 * TILE), F32)]
        + [jax.ShapeDtypeStruct((half, cols), F32)] * 2,
        cost_estimate=COST,
        compiler_params=params(),
        name="attn_bwd",
    )(info, lengths, q, k, v, do, lse, band, h1T, *more, *after)


def tokgrad_kernel(halves, tok_ref, dres_ref, gain_ref, wq_ref, wk_ref, wv_ref, *refs):
    out_ref, ggain_ref = refs[-2:]
    step = pl.program_id(0)
    done = None
    for i, w in enumerate((wq_ref, wk_ref, wv_ref)):
        d = jnp.concatenate([refs[h * 3 + i][...] for h in range(halves)], axis=1)
        term = dot(d, w[...], NT)
        done = term if done is None else done + term
    tok = tok_ref[...].astype(F32)
    s = norm_scale(tok)
    g = row_of(gain_ref) * done
    out_ref[...] = (dres_ref[...] + s * g - tok * (s * s * s * jnp.mean(tok * g, axis=-1, keepdims=True))).astype(BF16)
    ggain = jnp.sum(done * tok * s, axis=0, keepdims=True)

    @pl.when(step == 0)
    def _():
        ggain_ref[...] = ggain

    @pl.when(step > 0)
    def _():
        ggain_ref[...] += ggain


def tokgrad(tok, dres, gain, ds, wq, wk, wv, after, block=256):
    toks, width = tok.shape
    full = lambda a: pl.BlockSpec(a.shape, lambda s: (0,) * a.ndim, pipeline_mode=pl.Buffered(1))
    tall = pl.BlockSpec((block, width), lambda s: (s, 0))
    return pl.pallas_call(
        functools.partial(tokgrad_kernel, len(ds) // 3),
        grid=(toks // block,),
        in_specs=[tall, tall, full(gain), full(wq), full(wk), full(wv)]
        + [pl.BlockSpec((block, d.shape[1]), lambda s: (s, 0)) for d in ds]
        + unused(after),
        out_specs=[tall, pl.BlockSpec((1, width), lambda s: (0, 0))],
        out_shape=[jax.ShapeDtypeStruct((toks, width), BF16), jax.ShapeDtypeStruct((1, width), F32)],
        cost_estimate=COST,
        compiler_params=params(),
        name="tokgrad",
    )(tok, dres, gain, wq, wk, wv, *ds, *after)


SMALL = 16 * 2**20


class Route:
    def __init__(self, size, even, odd):
        self.size, self.even, self.odd = size, even, odd
        self.count = len(even)
        self.ways = [1 << len(group) for group in even]
        self.columns = {}
        table = [self.line(r, c) for r in range(size) for c in range(2)]
        device = lax.axis_index("rows") * 2 + lax.axis_index("blk")
        self.info = lax.dynamic_index_in_dim(jnp.asarray(np.array(table, np.int32)), device, 0, keepdims=False)

    def places(self, r, c):
        groups = (self.even, self.odd)[c]
        return [sum(((r >> b) & 1) << (len(group) - 1 - i) for i, b in enumerate(group)) for group in groups]

    def line(self, r, c):
        places, far = self.places(r, c), self.places(r, 1 - c)[0]
        line = [c, r, 2 * c + places[0], 2 * c + 1 - places[0], 2 * (1 - c) + far, 2 * (1 - c) + 1 - far, *places]
        self.place_column = 6
        for end in range(1, self.count + 1):
            for begin in range(end):
                for step in range(self.ways[end - 1]):
                    at = 0
                    for phase in range(begin, end):
                        at = at * self.ways[phase] + (places[phase] ^ (step if phase == end - 1 else 0))
                    self.columns[begin, end, step] = len(line)
                    line.append(at)
        return line

    def exchange(self, x, phase, step):
        def other(r, group):
            for i, b in enumerate(group):
                r ^= ((step >> (len(group) - 1 - i)) & 1) << b
            return r

        moves = [
            (r * 2 + c, other(r, (self.even, self.odd)[c][phase]) * 2 + c) for r in range(self.size) for c in range(2)
        ]
        return lax.ppermute(x, ("rows", "blk"), moves)


def swap_cores(x):
    return lax.ppermute(x, "blk", [(0, 1), (1, 0)])


def add_kernel(count, outs, info_ref, *refs):
    for n in range(outs):
        total = None
        for ref in refs[n * count : (n + 1) * count]:
            total = ref[...] if total is None else total + ref[...]
        refs[-outs + n][...] = total


def add_shares(info, sources, columns, rows, after, limit):
    cols = sources[0].shape[1]
    parts = 1
    while rows // parts * cols > 300000 and rows % (16 * parts) == 0:
        parts *= 2
    block = (rows // parts, cols)

    def spec(source, column):
        if column is None:
            return pl.BlockSpec(block, lambda g, i: (g, 0))
        return pl.BlockSpec(block, lambda g, i: (i[column] * parts + g, 0))

    outs = len(columns)
    return pl.pallas_call(
        functools.partial(add_kernel, len(sources), outs),
        grid_spec=pltpu.PrefetchScalarGridSpec(
            num_scalar_prefetch=1,
            grid=(parts,),
            in_specs=[spec(*pair) for line in columns for pair in zip(sources, line)] + unused(after),
            out_specs=[pl.BlockSpec(block, lambda g, i: (g, 0))] * outs,
        ),
        out_shape=[jax.ShapeDtypeStruct((rows, cols), F32)] * outs,
        cost_estimate=LITTLE,
        compiler_params=params(limit),
        name="add_shares",
    )(info, *sources * outs, *after)


def join_kernel(column, ways, info_ref, *refs):
    pieces, out_ref, sems = refs[:ways], refs[-2], refs[-1]
    rows = pieces[0].shape[0]
    copies = []
    for step, piece in enumerate(pieces):
        at = pl.multiple_of((info_ref[column] ^ step) * rows, 8)
        copies.append(pltpu.make_async_copy(piece, out_ref.at[pl.ds(at, rows), :], sems.at[step]))
        copies[-1].start()
    for copy in copies:
        copy.wait()


def join(info, column, pieces, after):
    rows, cols = pieces[0].shape
    ways = len(pieces)
    return pl.pallas_call(
        functools.partial(join_kernel, column, ways),
        in_specs=[pl.BlockSpec(memory_space=pltpu.SMEM)] + [ANYWHERE] * ways + unused(after),
        out_specs=pl.BlockSpec(memory_space=pltpu.VMEM),
        out_shape=jax.ShapeDtypeStruct((ways * rows, cols), F32),
        scratch_shapes=[pltpu.SemaphoreType.DMA((ways,))],
        cost_estimate=LITTLE,
        compiler_params=params(SMALL),
        name="join",
    )(info, *pieces, *after)


class Sum:
    def __init__(self, route, keep, send):
        self.route = route
        self.parts = [keep, swap_cores(send)]
        self.begins = [0, 0]
        self.shares = [keep.shape[0]]
        for ways in route.ways:
            if self.shares[-1] % (8 * ways):
                break
            self.shares.append(self.shares[-1] // ways)
        self.divided = len(self.shares) - 1
        self.phase = 0
        self.steps = (
            [self.send] * self.divided
            + [self.finish]
            + [self.add] * (route.count - self.divided)
            + [self.join] * (self.divided - 1)
            + [self.swap]
        )

    def advance(self, after):
        return self.steps.pop(0)(after) if self.steps else after

    def send(self, after):
        phase = self.phase
        flips = (1,) if phase < 2 else (1, 0)
        columns = [[self.route.columns[begin, phase + 1, flip] for begin in self.begins] for flip in flips]
        limit = VMEM if phase < 3 else SMALL
        outs = add_shares(self.route.info, self.parts, columns, self.shares[phase + 1], after, limit)
        got = self.route.exchange(outs[0], phase, 1)
        if phase < 2:
            self.parts.append(got)
            self.begins.append(phase + 1)
        else:
            self.parts = [outs[1], got]
            self.begins = [phase + 1] * 2
        self.phase += 1
        return (outs[0],)

    def finish(self, after):
        columns = [[self.route.columns.get((begin, self.phase, 0)) for begin in self.begins]]
        (self.piece,) = add_shares(self.route.info, self.parts, columns, self.shares[self.phase], after, SMALL)
        return self.gather()

    def gather(self):
        if self.divided <= self.phase < self.route.count:
            phase = self.phase
        else:
            phase = self.phase = min(self.phase, self.divided) - 1
        self.got = self.route.exchange(self.piece, phase, 1)
        if self.phase == 0:
            self.far_piece = swap_cores(self.piece)
            return (self.piece, (self.far_piece,))
        return (self.piece,)

    def add(self, after):
        parts = [self.piece, self.got]
        (self.piece,) = add_shares(self.route.info, parts, [[None] * 2], self.piece.shape[0], after, SMALL)
        self.phase += 1
        return self.gather()

    def join(self, after):
        self.piece = join(self.route.info, self.route.place_column + self.phase, [self.piece, self.got], after)
        return self.gather()

    def swap(self, after):
        self.sources = (self.piece, self.got, self.far_piece, swap_cores(self.got))
        return (self.got,)


SPACE = 10**11


def spacer_kernel(*refs):
    refs[-1][...] = jnp.zeros_like(refs[-1])


def spacer(after):
    return pl.pallas_call(
        spacer_kernel,
        in_specs=unused(after),
        out_specs=pl.BlockSpec(memory_space=pltpu.VMEM),
        out_shape=jax.ShapeDtypeStruct((8, 128), F32),
        cost_estimate=pl.CostEstimate(flops=SPACE, transcendentals=0, bytes_accessed=1),
        name="spacer",
    )(*after)


class SmallSum:
    def __init__(self, route, values):
        self.route = route
        self.shapes = [v.shape for v in values]
        flat = jnp.concatenate([v.reshape(-1) for v in values])
        self.sum = jnp.pad(flat, (0, -flat.shape[0] % 2048)).reshape(-1, 256)
        self.steps = [functools.partial(route.exchange, phase=p, step=1) for p in range(route.count)] + [swap_cores]
        self.got = self.steps.pop(0)(self.sum)

    def advance(self, after):
        if self.got is None:
            return after
        (self.sum,) = add_shares(self.route.info, [self.sum, self.got], [[None, None]], self.sum.shape[0], after, SMALL)
        self.got = self.steps.pop(0)(self.sum) if self.steps else None
        return (self.sum,)

    def values(self):
        while self.got is not None:
            self.advance(())
        flat, at, out = self.sum.reshape(-1), 0, []
        for shape in self.shapes:
            size = int(np.prod(shape))
            out.append(flat[at : at + size].reshape(shape))
            at += size
        return out


def assemble_kernel(spread, n_outs, info_ref, *refs):
    sources, outs = refs[:4], refs[-n_outs:]
    target, half = pl.program_id(0), pl.program_id(1)
    for n in range(4):
        for t in range(2):

            @pl.when((info_ref[2 + n] == 2 * target + half) & (target == t))
            def _():
                spread(t, sources[n], outs)


def assemble(info, slabs, spread, outs, blocks, sources, group, earlier, after):
    rows, cols = sources[0].shape
    count = slabs // 2 // group

    def source_spec(n):
        def index(t, h, j, i):
            stage, now = i[2 + n], 2 * t + h
            return jnp.where(now < stage, 0, jnp.where(now == stage, j, count - 1)), 0

        return pl.BlockSpec((rows // count, cols), index)

    def out_spec(target, block, row, column):
        def index(t, h, j, i):
            if target is None:
                return row + (2 * t + h) * count + j, column
            return row + jnp.where(t == target, h * count + j, 0 if target else 2 * count - 1), column

        return pl.BlockSpec(block, index)

    return pl.pallas_call(
        functools.partial(assemble_kernel, spread, len(outs)),
        grid_spec=pltpu.PrefetchScalarGridSpec(
            num_scalar_prefetch=1,
            grid=(2, 2, count),
            in_specs=[source_spec(n) for n in range(4)] + [OUTSIDE] * len(earlier) + unused(after),
            out_specs=[out_spec(*b) for b in blocks],
        ),
        out_shape=[jax.ShapeDtypeStruct(s, F32) for s in outs],
        cost_estimate=COST,
        input_output_aliases={5 + i: i for i in range(len(earlier))},
        compiler_params=params(),
        name="assemble",
    )(info, *sources, *earlier, *after)


def ffn_spread(width, size, slabs, group, target, source, outs):
    n, total = (size // 256, width) if target == 0 else (width // 256, size)
    rows = total // slabs
    for s in range(group):
        for j in range(n):
            at = (s * n + j) * rows
            outs[target][s * rows : (s + 1) * rows, j * 256 : (j + 1) * 256] = source[at : at + rows, :]


def attn_spread(columns, slabs, group, target, source, outs):
    n = len(columns)
    rows = source.shape[0] // (group * n)
    for s in range(group):
        for j, (out, column) in enumerate(columns):
            at = (s * n + j) * rows
            outs[out][s * rows : (s + 1) * rows, column : column + source.shape[1]] = source[at : at + rows, :]


ORDER = ("F0", "s0", "F1", "s0", "B0", "s1", "s0", "B1", "s0", "s1", "s2", "D", "s3", "D", "s0", "s1", "s0", "T", "s3", "s1", "s0", "D", "m", "s3", "s2", "s3", "s1", "m", "s0", "D", "s3", "s1", "m", "s3", "s2", "s3", "s1", "m", "s3", "D", "m", "s2", "s2", "s3", "s0", "s1", "s0", "s2", "s2", "s2", "s3", "s1", "s1", "s2", "D", "s2")


def on_device(tokens, lengths, attn_gain, wq, wk, wv, wo, table, ffn_gain, w_in, w_out, out_grad, *, size):
    rows, seq, width = tokens.shape
    buckets, heads = table.shape
    pairs = heads // 2
    ff = w_in.shape[1]
    slabs = 16
    bits = range(size.bit_length() - 1)
    straight = Route(size, [(b,) for b in bits], [(b,) for b in (1, 0, *bits[2:])])
    info = straight.info
    lane_buckets = band_buckets(buckets)
    onehot = np.arange(buckets)[:, None] == lane_buckets[None, :]
    band = jnp.einsum("bh,bm->hm", table, jnp.asarray(onehot, BF16), preferred_element_type=F32)
    flat = lambda a: a.reshape(rows * seq, a.shape[2])
    tall = lambda a: a.reshape(rows, seq, width)
    chunks, sub = 2, 768
    part = ff // chunks
    ends = bucket_of(np.array([-2 * TILE] * TILE + [2 * TILE] * TILE), buckets)
    spread = (np.concatenate([lane_buckets, ends])[:, None] == np.arange(buckets)[None, :]).astype(np.float32)

    h1T, q, k, v, attT, lse, x1, h2 = attn_fwd(tokens, lengths, attn_gain, ffn_gain, wq, wk, wv, wo, band)
    acc, sums, after, ds, diags = (), [], (), [], []
    ffn_grads, attn_grads = (), ()
    def put(which, after):
        nonlocal ffn_grads, attn_grads
        group = 8
        sources, info = sums[which].sources, sums[which].route.info
        if which < chunks:
            ffn_grads = assemble(
                info, slabs, functools.partial(ffn_spread, width, part, slabs, group), [w_in.shape, w_out.shape],
                [(0, (width // slabs * group, part), 0, which), (1, (part // slabs * group, width), which * (slabs // group), 0)],
                sources, group, tuple(ffn_grads), after,
            )
            return (ffn_grads[0],)
        half = which - chunks
        block = width // 2 // slabs * group
        columns = [(0, 0), (1, 0), (2, 0)] + [(3, 0), (3, width // 2)] * (half == 0)
        blocks = [(None, (block, width // 2), 0, half)] * 3 + [(None, (block, width), 0, 0)] * (half == 0)
        made = assemble(
            info, slabs, functools.partial(attn_spread, columns, slabs, group), [wq.shape] * len(blocks), blocks,
            sources, group, tuple(attn_grads[:3]), after,
        )
        attn_grads = list(made) + list(attn_grads[3:])
        return (made[0],)

    late = []
    for at, op in enumerate(ORDER):
        if late:
            after = (*after, *late.pop(0))
        which = int(op[1]) if len(op) > 1 else 0
        if op[0] == "F":
            end = (ffn_gain, flat(x1), attT, wo) if which == chunks - 1 else None
            keep, send, *acc = ffn_chunk(
                info, lengths, slabs, flat(h2), flat(out_grad), w_in, w_out, which * part, part, sub, acc, after, end
            )
            sums.append(Sum(straight, keep, send))
            if end:
                mixed, dres, datt, gwo, ggain2 = acc
            after = (keep,)
        elif op[0] == "B":
            half = pairs // 2
            more = [] if which else [gwo]
            dq, dk, dv, diag, keep, send = attn_bwd(
                info, lengths, slabs, q, k, v, tall(datt), lse, band, h1T, which * half, half, more, after
            )
            ds += [flat(dq), flat(dk), flat(dv)]
            diags.append(diag)
            sums.append(Sum(straight, keep, send))
            after = (keep,)
        elif op == "T":
            tgrad, ggain1 = tokgrad(flat(tokens), dres, attn_gain, ds, wq, wk, wv, after)
            diag = jnp.concatenate(diags).reshape(heads, 6 * TILE)
            gtable = jnp.einsum("hm,mb->bh", diag, jnp.asarray(spread), precision=lax.Precision.HIGHEST)
            small = SmallSum(straight, (ggain1, ggain2, gtable))
            after = (ggain1,)
        elif op == "D":
            after = (spacer(after),)
        elif op == "m":
            after = small.advance(after)
        else:
            after = sums[which].advance(after)
            if isinstance(after[-1], tuple):
                late, after = [(), after[-1]], after[:-1]
            if ORDER[at:].count(op) == 1:
                while sums[which].steps:
                    after = sums[which].advance(after)
                after = put(which, after)
    ggain1, ggain2, gtable = small.values()
    return (tall(mixed), tall(tgrad), ggain1[0], *attn_grads, gtable, ggain2[0], *ffn_grads)


def solution(mesh):
    split = P(("rows", "blk"))
    return jax.shard_map(
        functools.partial(on_device, size=mesh.shape["rows"]),
        mesh=mesh,
        in_specs=(split, split) + (P(),) * 9 + (split,),
        out_specs=(split, split) + (P(),) * 9,
        check_vma=False,
    )
```

```python
import functools
import jax
import jax.numpy as jnp
import numpy as np
from jax import lax
from jax.experimental import pallas as pl
from jax.experimental.pallas import tpu as pltpu
from jax.sharding import PartitionSpec as P

NT = (((1,), (1,)), ((), ()))
TN = (((0,), (0,)), ((), ()))
F32, BF16 = jnp.float32, jnp.bfloat16
TILE = 128
MASKED = -1000000000.0
EPS = 1e-06
far_steps = np.array([12, 16, 23, 32, 46, 64, 91], dtype=np.int32)


def dot(a, b, dims=None):
    if dims is None:
        return jnp.dot(a, b, preferred_element_type=F32)
    return lax.dot_general(a, b, dims, preferred_element_type=F32)


def bucket_of(relative, bucket_count):
    distance = np.abs(relative)
    beyond = np.sum(distance[..., None] >= far_steps, axis=-1)
    inner = np.where(distance < bucket_count // 4, distance, bucket_count // 4 + beyond)
    return np.where(relative > 0, bucket_count // 2, 0) + inner


def band_buckets(bucket_count):
    lanes = np.arange(4 * TILE)
    offsets = np.where(lanes < 2 * TILE, lanes, lanes - 4 * TILE)
    return bucket_of(-offsets, bucket_count)


def segments_along(len_ref, row, shape, axis, start=0):
    at = lax.broadcasted_iota(jnp.int32, shape, axis) + start
    total = jnp.zeros(shape, jnp.int32)
    end = jnp.int32(0)
    for j in range(len_ref.shape[1]):
        end = end + len_ref[row, j]
        total = total + jnp.where(at >= end, 1, 0)
    return total


def fill_mask(len_ref, row, mask_ref, last):
    seq = mask_ref.shape[0]
    of_q = segments_along(len_ref, row, (1, seq), 1)
    of_k = segments_along(len_ref, row, (seq, TILE), 0)
    of_k = jnp.where(of_k < last, of_k, -1)
    for j in range(seq // TILE):
        same = of_k == of_q[:, j * TILE : (j + 1) * TILE]
        mask_ref[:, j * TILE : (j + 1) * TILE] = jnp.where(same, 0.0, MASKED)
    return of_q < last


def band_of(vector):
    wide = jnp.broadcast_to(vector, (TILE, 4 * TILE))
    return pltpu.roll(wide, 0, 1, stride=1, stride_axis=0)


def bias_row(band, vector, ki, count):
    shape = (TILE, TILE)
    tiles = []
    for qi in range(count):
        step = ki - qi
        if step == 0:
            tiles.append(band[:, 0:TILE])
        elif step == -1:
            tiles.append(band[:, TILE : 2 * TILE])
        elif step == 1:
            tiles.append(band[:, 3 * TILE : 4 * TILE])
        elif step < 0:
            tiles.append(jnp.broadcast_to(vector[:, 2 * TILE - 1 : 2 * TILE], shape))
        else:
            tiles.append(jnp.broadcast_to(vector[:, 2 * TILE : 2 * TILE + 1], shape))
    return jnp.concatenate(tiles, axis=1)


def norm_scale(value):
    return lax.rsqrt(jnp.mean(value * value, axis=-1, keepdims=True) + EPS)


def row_of(gain_ref):
    return gain_ref[...].astype(F32).reshape(1, gain_ref.shape[0])


VMEM = 63 * 2**20
ANYWHERE = pl.BlockSpec(memory_space=pl.ANY)
OUTSIDE = pl.BlockSpec(memory_space=pltpu.HBM)
FLOPS = 10**11
LITTLE = pl.CostEstimate(flops=1, transcendentals=0, bytes_accessed=1)
COST = pl.CostEstimate(flops=FLOPS, transcendentals=0, bytes_accessed=1)


def unused(arrays):
    return [OUTSIDE if a.size >= 2**18 else ANYWHERE for a in arrays]


def params(limit=VMEM):
    return pltpu.CompilerParams(vmem_limit_bytes=limit)


def attn_fwd_kernel(
    len_ref, tok_ref, gain1_ref, gain2_ref, wq_ref, wk_ref, wv_ref, wo_ref, band_ref,
    h1T_ref, q_ref, k_ref, v_ref, attT_ref, lse_ref, x1_ref, h2_ref,
    att_ref, mask_ref, s_ref, p_ref,
):
    seq, width = tok_ref.shape[1:]
    pairs = width // TILE
    head = TILE // 2
    row = pl.program_id(0)
    valid = fill_mask(len_ref, row, mask_ref, len_ref.shape[1] - 1)
    tok = tok_ref[0].astype(F32)
    h1 = (tok * norm_scale(tok) * row_of(gain1_ref)).astype(BF16)
    h1T_ref[0] = h1.T
    q_ref[0] = dot(h1, wq_ref[...]).astype(BF16)
    k_ref[0] = dot(h1, wk_ref[...]).astype(BF16)
    v_ref[0] = dot(h1, wv_ref[...]).astype(BF16)
    count = seq // TILE
    low_half = lax.broadcasted_iota(jnp.int32, (1, TILE), 1) < head

    def pair(p, carry):
        lanes = pl.ds(pl.multiple_of(p * TILE, TILE), TILE)
        qp, kp, vp = q_ref[0, :, lanes], k_ref[0, :, lanes], v_ref[0, :, lanes]
        vT = vp.T
        tops = []
        for a in range(2):
            qm = jnp.where(low_half if a == 0 else ~low_half, qp, jnp.zeros_like(qp))
            vector = band_ref[pl.ds(2 * p + a, 1), :]
            band = band_of(vector)
            top = None
            for ki in range(count):
                rows = slice(ki * TILE, (ki + 1) * TILE)
                s = dot(kp[rows], qm, NT) + bias_row(band, vector, ki, count) + mask_ref[rows, :]
                s_ref[a, rows, :] = s
                most = jnp.max(s, axis=0, keepdims=True)
                top = most if top is None else jnp.maximum(top, most)
            tops.append(top)
        totals = []
        for a, top in enumerate(tops):
            total = jnp.zeros_like(top)
            for ki in range(count):
                rows = slice(ki * TILE, (ki + 1) * TILE)
                e = jnp.exp(s_ref[a, rows, :] - top)
                total = total + jnp.sum(e, axis=0, keepdims=True)
                p_ref[a, rows, :] = e.astype(BF16)
            totals.append(total)
        outs = []
        for a, (top, total) in enumerate(zip(tops, totals)):
            o = dot(vT[a * head : (a + 1) * head], p_ref[a])
            outs.append(jnp.where(valid, o / total, 0.0))
            lse_ref[0, pl.ds(2 * p + a, 1), :] = top + jnp.log(total)
        both = jnp.concatenate(outs, axis=0)
        attT_ref[0, lanes, :] = both.astype(BF16)
        att_ref[:, lanes] = both.T.astype(BF16)
        return carry

    lax.fori_loop(0, pairs, pair, 0, unroll=6)
    x1 = tok_ref[0].astype(F32) + dot(att_ref[...], wo_ref[...])
    x1_ref[0] = x1
    h2_ref[0] = (x1 * norm_scale(x1) * row_of(gain2_ref)).astype(BF16)


def attn_fwd(tokens, lengths, gain1, gain2, wq, wk, wv, wo, band):
    rows, seq, width = tokens.shape
    heads = band.shape[0]
    full = lambda a: pl.BlockSpec(a.shape, lambda r, l: (0,) * a.ndim, pipeline_mode=pl.Buffered(1))
    per_row = lambda *s: pl.BlockSpec((1,) + s, lambda r, l: (r,) + (0,) * len(s))
    tall = jax.ShapeDtypeStruct((rows, seq, width), BF16)
    turned = jax.ShapeDtypeStruct((rows, width, seq), BF16)
    return pl.pallas_call(
        attn_fwd_kernel,
        grid_spec=pltpu.PrefetchScalarGridSpec(
            num_scalar_prefetch=1,
            grid=(rows,),
            in_specs=[per_row(seq, width)] + [full(a) for a in (gain1, gain2, wq, wk, wv, wo, band)],
            out_specs=[per_row(width, seq)]
            + [per_row(seq, width)] * 3
            + [per_row(width, seq), per_row(heads, seq), per_row(seq, width), per_row(seq, width)],
            scratch_shapes=[
                pltpu.VMEM((seq, width), BF16),
                pltpu.VMEM((seq, seq), F32),
                pltpu.VMEM((2, seq, seq), F32),
                pltpu.VMEM((2, seq, seq), BF16),
            ],
        ),
        out_shape=[turned, tall, tall, tall, turned]
        + [jax.ShapeDtypeStruct((rows, heads, seq), F32), jax.ShapeDtypeStruct((rows, seq, width), F32), tall],
        cost_estimate=COST,
        compiler_params=params(),
        name="attn_fwd",
    )(lengths, tokens, gain1, gain2, wq, wk, wv, wo, band)


GELU_C = float(np.sqrt(2.0 / np.pi))


def gelu_pair(v):
    v2 = v * v
    t = jnp.tanh(GELU_C * v * (1.0 + 0.044715 * v2))
    half = 0.5 * (1.0 + t)
    slope = half + (0.5 * GELU_C) * v * (1.0 - t * t) * (1.0 + (3 * 0.044715) * v2)
    return v * half, slope


def place(core, mine, other, keep, send, sems):
    both = lambda a, b: [(src, dst, sems.at[n, i]) for n, pairs in enumerate((a, b)) for i, (src, dst) in enumerate(pairs)]
    return [(core == 0, both(mine(keep), other(send))), (core != 0, both(mine(send), other(keep)))]


def run_all(cases, action):
    for condition, copies in cases:

        @pl.when(condition)
        def _():
            for src, dst, sem in copies:
                getattr(pltpu.make_async_copy(src, dst, sem), action)()


def ffn_kernel(steps, slabs, first, last, info_ref, len_ref, h2_ref, dy_ref, win_ref, wout_ref, *refs):
    refs = list(refs)
    acc_in = [] if first else [refs.pop(0), refs.pop(0)]
    if last:
        gain_ref, late = refs[0], refs[1:4]
        keep_ref, *send_refs, mixed_out, dres_out, datt_out, gwo_ref, ggain_ref = refs[-23:-15]
        mix_ref, dtwo_ref, h2T_ref, act_ref, dpre_ref, gin_ref, gout_ref, sems, acc_sems, mixed_ref, dres_ref, datt_ref = refs[-15:-3]
        x1_ref, attT_ref, wo_ref = refs[-3:]
        first_late = acc_sems.shape[0] - 3
        late = [pltpu.make_async_copy(a, b, acc_sems.at[first_late + i]) for i, (a, b) in enumerate(zip(late, refs[-3:]))]
    else:
        keep_ref, *send_refs = refs[-14:-11]
        acc_out = refs[-11:-9]
        mix_ref, dtwo_ref, h2T_ref, act_ref, dpre_ref, gin_ref, gout_ref, sems, acc_sems = refs[-9:]
    step = pl.program_id(0)
    toks, width = h2_ref.shape
    sub = win_ref.shape[1]
    wide, tall = width // 256, sub // 256
    in_rows, out_rows = width // slabs, sub * steps // slabs
    piece = in_rows * tall * steps
    here = slabs // steps
    totals = (mix_ref, dtwo_ref)

    def moves(at):
        core, first_half = info_ref[0], 1 - info_ref[4] % 2
        half = slabs // 2
        block = in_rows * tall
        cases = []
        for c in range(2):
            for f in range(2):
                here_now = (core == c) & (first_half == f)
                copies = []
                for i in range(slabs):
                    src = gin_ref.at[at, i * block : (i + 1) * block, :]
                    dst, row = (keep_ref, i) if c == 0 else (send_refs[0 if i // half == f else 1], i % half)
                    dst = dst.at[pl.ds(pl.multiple_of(row * piece + at * block, 8), block), :]
                    copies.append((src, dst, sems.at[at, 0, i]))
                cases.append((here_now, copies))
                if c == 1:
                    dst = keep_ref.at[pl.ds(pl.multiple_of(at * (here * piece), 8), here * piece), :]
                    cases.append((here_now, [(gout_ref.at[at], dst, sems.at[at, 1, 0])]))
                else:
                    for now in range(2):
                        dst = send_refs[0 if now == f else 1]
                        cases.append((here_now & (at == now), [(gout_ref.at[at], dst, sems.at[at, 1, 0])]))
        return cases

    @pl.when(step == 0)
    def _():
        for i, ref in enumerate(acc_in):
            pltpu.make_async_copy(ref, totals[i], acc_sems.at[i]).start()
        if last:
            for copy in late:
                copy.start()
        h2T_ref[...] = h2_ref[...].T

    pre = dot(h2_ref[...], win_ref[...])
    dact = dot(dy_ref[...], wout_ref[...], NT)
    act, slope = gelu_pair(pre)
    act_ref[...] = act.astype(BF16)
    dpre_ref[...] = (dact * slope).astype(BF16)
    mix = dot(act_ref[...], wout_ref[...])
    dtwo = dot(dpre_ref[...], win_ref[...], NT)

    @pl.when(step == 0)
    def _():
        if first:
            mix_ref[...] = mix
            dtwo_ref[...] = dtwo
        else:
            for i, ref in enumerate(acc_in):
                pltpu.make_async_copy(ref, totals[i], acc_sems.at[i]).wait()
            mix_ref[...] += mix
            dtwo_ref[...] += dtwo

    @pl.when(step > 0)
    def _():
        mix_ref[...] += mix
        dtwo_ref[...] += dtwo

    if not last:

        @pl.when(step == steps - 1)
        def _():
            for i in range(2):
                pltpu.make_async_copy(totals[i], acc_out[i], acc_sems.at[2 + i]).start()

    gout = dot(act_ref[...], dy_ref[...], TN)
    for i in range(here):
        for j in range(wide):
            at = (i * wide + j) * out_rows
            gout_ref[step, at : at + out_rows, :] = gout[i * out_rows : (i + 1) * out_rows, j * 256 : (j + 1) * 256]
    gin = dot(h2T_ref[...], dpre_ref[...])
    for i in range(slabs):
        for j in range(tall):
            at = (i * tall + j) * in_rows
            gin_ref[step, at : at + in_rows, :] = gin[i * in_rows : (i + 1) * in_rows, j * 256 : (j + 1) * 256]
    run_all(moves(step), "start")

    @pl.when(step == steps - 1)
    def _():
        if last:
            for copy in late:
                copy.wait()
            rows = len_ref.shape[0]
            seq = toks // rows
            block = 256
            copies = []
            ggain = None
            for b in range(toks // block):
                here_toks = slice(b * block, (b + 1) * block)
                x1, back = x1_ref[here_toks, :], dtwo_ref[here_toks, :]
                mixed_ref[here_toks, :] = (x1 + mix_ref[here_toks, :]).astype(BF16)
                s = norm_scale(x1)
                g = row_of(gain_ref) * back
                dres = dy_ref[here_toks, :].astype(F32) + s * g - x1 * (s * s * s * jnp.mean(x1 * g, axis=-1, keepdims=True))
                dres_ref[here_toks, :] = dres
                some = jnp.sum(back * x1 * s, axis=0, keepdims=True)
                ggain = some if ggain is None else ggain + some
                dbranch = dres.astype(BF16)
                act_ref[here_toks, :] = dbranch
                datt = dot(dbranch, wo_ref[...], NT)
                seg = segments_along(len_ref, b * block // seq, (block, TILE), 0, b * block % seq)[:, :1]
                datt_ref[here_toks, :] = jnp.where(seg < len_ref.shape[1] - 1, datt, 0.0).astype(BF16)
                for n, (src, dst) in enumerate(((mixed_ref, mixed_out), (dres_ref, dres_out), (datt_ref, datt_out))):
                    copies.append(pltpu.make_async_copy(src.at[here_toks, :], dst.at[here_toks, :], acc_sems.at[4 + 3 * b + n]))
                    copies[-1].start()
            ggain_ref[...] = ggain
            gwo = None
            for r in range(rows):
                part = dot(attT_ref[r], act_ref[r * seq : (r + 1) * seq, :])
                gwo = part if gwo is None else gwo + part
            gwo_ref[...] = gwo
            for copy in copies:
                copy.wait()
        else:
            for i in range(2):
                pltpu.make_async_copy(totals[i], acc_out[i], acc_sems.at[2 + i]).wait()
        for at in range(steps):
            run_all(moves(at), "wait")


def ffn_chunk(info, lengths, slabs, h2, dy, w_in, w_out, start, size, sub, acc, after, rest=None):
    toks, width = h2.shape
    base = start // sub
    steps = size // sub
    piece = width * (sub // 256)
    full = lambda a: pl.BlockSpec(a.shape, lambda s, *_: (0,) * a.ndim, pipeline_mode=pl.Buffered(1))
    f32 = lambda *s: jax.ShapeDtypeStruct(s, F32)
    out_specs = [ANYWHERE] * 3
    out_shape = [f32(steps * piece, 256)] + [f32(steps * piece // 2, 256)] * 2
    scratch = [
        pltpu.VMEM((toks, width), F32),
        pltpu.VMEM((toks, width), F32),
        pltpu.VMEM((width, toks), BF16),
        pltpu.VMEM((toks, sub), BF16),
        pltpu.VMEM((toks, sub), BF16),
        pltpu.VMEM((steps, piece, 256), F32),
        pltpu.VMEM((steps, piece, 256), F32),
        pltpu.SemaphoreType.DMA((steps, 2, slabs)),
        pltpu.SemaphoreType.DMA((7 + 3 * (toks // 256),)),
    ]
    if rest is None:
        rest, gain = (), ()
        out_specs += [ANYWHERE] * 2
        out_shape += [f32(toks, width)] * 2
    else:
        gain, *rest = rest
        gain = (gain,)
        low = jax.ShapeDtypeStruct((toks, width), BF16)
        whole = lambda s: pl.BlockSpec(s.shape, lambda *_: (0,) * len(s.shape), pipeline_mode=pl.Buffered(1))
        gwo, ggain = f32(width, width), f32(1, width)
        out_specs += [ANYWHERE] * 3 + [whole(gwo), whole(ggain)]
        out_shape += [low, f32(toks, width), low, gwo, ggain]
        scratch += [pltpu.VMEM((toks, width), BF16), pltpu.VMEM((toks, width), F32), pltpu.VMEM((toks, width), BF16)]
        scratch += [pltpu.VMEM(a.shape, a.dtype) for a in rest]
    return pl.pallas_call(
        functools.partial(ffn_kernel, steps, slabs, not acc, bool(rest)),
        grid_spec=pltpu.PrefetchScalarGridSpec(
            num_scalar_prefetch=2,
            grid=(steps,),
            in_specs=[
                full(h2),
                full(dy),
                pl.BlockSpec((width, sub), lambda s, *_: (0, base + s)),
                pl.BlockSpec((sub, width), lambda s, *_: (base + s, 0)),
            ]
            + [ANYWHERE] * len(acc)
            + [full(a) for a in gain]
            + [ANYWHERE] * len(rest)
            + unused(after),
            out_specs=out_specs,
            scratch_shapes=scratch,
        ),
        out_shape=out_shape,
        cost_estimate=COST,
        compiler_params=params(),
        name="ffn",
    )(info, lengths, h2, dy, w_in, w_out, *acc, *gain, *rest, *after)


def diagonal_sums(x):
    depth, lanes = x.shape
    total = x[0:8]
    for g in range(8, depth, 8):
        total = total + pltpu.roll(x[g : g + 8], lanes - g, 1)
    at = lax.broadcasted_iota(jnp.int32, (8, lanes), 0)
    for bit in (1, 2, 4):
        total = jnp.where((at & bit) != 0, pltpu.roll(total, lanes - bit, 1), total)
    return jnp.sum(total, axis=0, keepdims=True)


def attn_bwd_kernel(slabs, first, n_more, info_ref, len_ref, q_ref, k_ref, v_ref, do_ref, lse_ref, band_ref, h1T_ref, *refs):
    more = refs[:n_more]
    dq_ref, dk_ref, dv_ref, diag_ref, keep_ref, send_ref = refs[-14:-8]
    mask_ref, p_ref, low_ref, dp_ref, ds_ref, d_ref, g_ref, sems = refs[-8:]
    pair, pairs = pl.program_id(0), pl.num_programs(0)
    rows, seq = q_ref.shape[:2]
    head = TILE // 2
    count = seq // TILE
    width, cols = h1T_ref.shape[1], g_ref.shape[2]
    stripes = keep_ref.shape[0] * 2 // width
    share = width // 2 // slabs

    def put(j, block):
        for c in range(2):
            for s in range(slabs):
                at, begin = (s * stripes + j) * share, (c * slabs + s) * share
                g_ref[c, at : at + share, :] = block[begin : begin + share]

    @pl.when(pair == 0)
    def _():
        for row in range(rows):
            fill_mask(len_ref, row, mask_ref.at[row], len_ref.shape[1] - 1)

    low_half = lax.broadcasted_iota(jnp.int32, (1, TILE), 1) < head
    bands = []
    for a in range(2):
        vector = band_ref[pl.ds(2 * (first + pair) + a, 1), :]
        bands.append((vector, band_of(vector)))
    sides = []
    for n in range(2 * rows):
        row, a = n // 2, n % 2
        qp, kp, vp, dop = q_ref[row], k_ref[row], v_ref[row], do_ref[row]
        own = low_half if a == 0 else ~low_half
        qm = jnp.where(own, qp, jnp.zeros_like(qp))
        dom = jnp.where(own, dop, jnp.zeros_like(dop))
        vector, band = bands[a]
        lse = lse_ref[row, pl.ds(2 * (first + pair) + a, 1), :]
        delta = jnp.zeros((1, seq), F32)
        for ki in range(count):
            some = slice(ki * TILE, (ki + 1) * TILE)
            s = dot(kp[some], qm, NT) + bias_row(band, vector, ki, count) + mask_ref[row, some, :]
            prob = jnp.exp(s - lse)
            dp = dot(vp[some], dom, NT)
            delta = delta + jnp.sum(prob * dp, axis=0, keepdims=True)
            p_ref[n, some, :] = prob
            low_ref[n, some, :] = prob.astype(BF16)
            dp_ref[n, some, :] = dp
        sides.append((qm, dom, delta))
    sums = [{}, {}]
    for n, (_, _, delta) in enumerate(sides):
        near = sums[n % 2]
        for ki in range(count):
            some = slice(ki * TILE, (ki + 1) * TILE)
            ds = p_ref[n, some, :] * (dp_ref[n, some, :] - delta)
            ds_ref[n, some, :] = ds.astype(BF16)
            for qi in range(count):
                step = max(-2, min(2, ki - qi))
                tile = ds[:, qi * TILE : (qi + 1) * TILE]
                near[step] = tile if step not in near else near[step] + tile
    for a, near in enumerate(sums):
        zero = jnp.zeros((TILE, TILE), F32)
        band = jnp.concatenate([near[0], near[-1], zero, near[1]], axis=1)
        diag_ref[0, a : a + 1, : 4 * TILE] = diagonal_sums(band)
        ends = jnp.concatenate([near[-2], near[2]], axis=1)
        diag_ref[0, a : a + 1, 4 * TILE :] = jnp.sum(ends, axis=0, keepdims=True)
    lanes = pl.ds(pl.multiple_of(pair * TILE, TILE), TILE)
    for row in range(rows):
        kT = k_ref[row].T
        dqT, dk, dv = [], None, None
        for a in range(2):
            n = 2 * row + a
            qm, dom, _ = sides[n]
            dva = dot(low_ref[n], dom)
            dka = dot(ds_ref[n], qm)
            dv = dva if dv is None else dv + dva
            dk = dka if dk is None else dk + dka
            dqT.append(dot(kT[a * head : (a + 1) * head], ds_ref[n]))
        dq = jnp.concatenate(dqT, axis=0).T.astype(BF16)
        dk, dv = dk.astype(BF16), dv.astype(BF16)
        dq_ref[row], dk_ref[row], dv_ref[row] = dq, dk, dv
        for j, d in enumerate((dq, dk, dv)):
            d_ref[j, row, :, lanes] = d

    @pl.when(pair == pairs - 1)
    def _():
        for j in range(3):
            g = None
            for r in range(h1T_ref.shape[0]):
                part = dot(h1T_ref[r], d_ref[j, r])
                g = part if g is None else g + part
            put(j, g)
        for j in range(stripes - 3):
            put(3 + j, more[0][:, j * cols : (j + 1) * cols])
        moves = place(
            info_ref[0], lambda ref: [(g_ref.at[0], ref)], lambda ref: [(g_ref.at[1], ref)], keep_ref, send_ref, sems
        )
        run_all(moves, "start")
        run_all(moves, "wait")


def attn_bwd(info, lengths, slabs, q, k, v, do, lse, band, h1T, first, pairs, more, after):
    rows, seq, width = q.shape
    cols = pairs * TILE
    half = width // 2 * (3 + sum(m.shape[1] // cols for m in more))
    tall = pl.BlockSpec((rows, seq, TILE), lambda p, *_: (0, 0, first + p))
    tall_out = pl.BlockSpec((rows, seq, TILE), lambda p, *_: (0, 0, p))
    full = lambda a: pl.BlockSpec(a.shape, lambda *_: (0,) * a.ndim, pipeline_mode=pl.Buffered(1))
    out = jax.ShapeDtypeStruct((rows, seq, cols), BF16)
    square = lambda dtype: pltpu.VMEM((2 * rows, seq, seq), dtype)
    return pl.pallas_call(
        functools.partial(attn_bwd_kernel, slabs, first, len(more)),
        grid_spec=pltpu.PrefetchScalarGridSpec(
            num_scalar_prefetch=2,
            grid=(pairs,),
            in_specs=[tall] * 4
            + [full(lse), full(band), full(h1T)]
            + [full(m) for m in more]
            + unused(after),
            out_specs=[tall_out] * 3 + [pl.BlockSpec((1, 2, 6 * TILE), lambda p, *_: (p, 0, 0))] + [ANYWHERE] * 2,
            scratch_shapes=[
                pltpu.VMEM((rows, seq, seq), F32),
                square(F32),
                square(BF16),
                square(F32),
                square(BF16),
                pltpu.VMEM((3, rows, seq, cols), BF16),
                pltpu.VMEM((2, half, cols), F32),
                pltpu.SemaphoreType.DMA((2, 1)),
            ],
        ),
        out_shape=[out] * 3
        + [jax.ShapeDtypeStruct((pairs, 2, 6 * TILE), F32)]
        + [jax.ShapeDtypeStruct((half, cols), F32)] * 2,
        cost_estimate=COST,
        compiler_params=params(),
        name="attn_bwd",
    )(info, lengths, q, k, v, do, lse, band, h1T, *more, *after)


def tokgrad_kernel(halves, tok_ref, dres_ref, gain_ref, wq_ref, wk_ref, wv_ref, *refs):
    out_ref, ggain_ref = refs[-2:]
    step = pl.program_id(0)
    done = None
    for i, w in enumerate((wq_ref, wk_ref, wv_ref)):
        d = jnp.concatenate([refs[h * 3 + i][...] for h in range(halves)], axis=1)
        term = dot(d, w[...], NT)
        done = term if done is None else done + term
    tok = tok_ref[...].astype(F32)
    s = norm_scale(tok)
    g = row_of(gain_ref) * done
    out_ref[...] = (dres_ref[...] + s * g - tok * (s * s * s * jnp.mean(tok * g, axis=-1, keepdims=True))).astype(BF16)
    ggain = jnp.sum(done * tok * s, axis=0, keepdims=True)

    @pl.when(step == 0)
    def _():
        ggain_ref[...] = ggain

    @pl.when(step > 0)
    def _():
        ggain_ref[...] += ggain


def tokgrad(tok, dres, gain, ds, wq, wk, wv, after, block=256):
    toks, width = tok.shape
    full = lambda a: pl.BlockSpec(a.shape, lambda s: (0,) * a.ndim, pipeline_mode=pl.Buffered(1))
    tall = pl.BlockSpec((block, width), lambda s: (s, 0))
    return pl.pallas_call(
        functools.partial(tokgrad_kernel, len(ds) // 3),
        grid=(toks // block,),
        in_specs=[tall, tall, full(gain), full(wq), full(wk), full(wv)]
        + [pl.BlockSpec((block, d.shape[1]), lambda s: (s, 0)) for d in ds]
        + unused(after),
        out_specs=[tall, pl.BlockSpec((1, width), lambda s: (0, 0))],
        out_shape=[jax.ShapeDtypeStruct((toks, width), BF16), jax.ShapeDtypeStruct((1, width), F32)],
        cost_estimate=COST,
        compiler_params=params(),
        name="tokgrad",
    )(tok, dres, gain, wq, wk, wv, *ds, *after)


SMALL = 16 * 2**20


class Route:
    def __init__(self, size, even, odd):
        self.size, self.even, self.odd = size, even, odd
        self.count = len(even)
        self.ways = [1 << len(group) for group in even]
        self.columns = {}
        table = [self.line(r, c) for r in range(size) for c in range(2)]
        device = lax.axis_index("rows") * 2 + lax.axis_index("blk")
        self.info = lax.dynamic_index_in_dim(jnp.asarray(np.array(table, np.int32)), device, 0, keepdims=False)

    def places(self, r, c):
        groups = (self.even, self.odd)[c]
        return [sum(((r >> b) & 1) << (len(group) - 1 - i) for i, b in enumerate(group)) for group in groups]

    def line(self, r, c):
        places, far = self.places(r, c), self.places(r, 1 - c)[0]
        line = [c, r, 2 * c + places[0], 2 * c + 1 - places[0], 2 * (1 - c) + far, 2 * (1 - c) + 1 - far, *places]
        self.place_column = 6
        for end in range(1, self.count + 1):
            for begin in range(end):
                for step in range(self.ways[end - 1]):
                    at = 0
                    for phase in range(begin, end):
                        at = at * self.ways[phase] + (places[phase] ^ (step if phase == end - 1 else 0))
                    self.columns[begin, end, step] = len(line)
                    line.append(at)
        return line

    def exchange(self, x, phase, step):
        def other(r, group):
            for i, b in enumerate(group):
                r ^= ((step >> (len(group) - 1 - i)) & 1) << b
            return r

        moves = [
            (r * 2 + c, other(r, (self.even, self.odd)[c][phase]) * 2 + c) for r in range(self.size) for c in range(2)
        ]
        return lax.ppermute(x, ("rows", "blk"), moves)


def swap_cores(x):
    return lax.ppermute(x, "blk", [(0, 1), (1, 0)])


def add_kernel(count, outs, info_ref, *refs):
    for n in range(outs):
        total = None
        for ref in refs[n * count : (n + 1) * count]:
            total = ref[...] if total is None else total + ref[...]
        refs[-outs + n][...] = total


def add_shares(info, sources, columns, rows, after, limit):
    cols = sources[0].shape[1]
    parts = 1
    while rows // parts * cols > 300000 and rows % (16 * parts) == 0:
        parts *= 2
    block = (rows // parts, cols)

    def spec(source, column):
        if column is None:
            return pl.BlockSpec(block, lambda g, i: (g, 0))
        return pl.BlockSpec(block, lambda g, i: (i[column] * parts + g, 0))

    outs = len(columns)
    return pl.pallas_call(
        functools.partial(add_kernel, len(sources), outs),
        grid_spec=pltpu.PrefetchScalarGridSpec(
            num_scalar_prefetch=1,
            grid=(parts,),
            in_specs=[spec(*pair) for line in columns for pair in zip(sources, line)] + unused(after),
            out_specs=[pl.BlockSpec(block, lambda g, i: (g, 0))] * outs,
        ),
        out_shape=[jax.ShapeDtypeStruct((rows, cols), F32)] * outs,
        cost_estimate=LITTLE,
        compiler_params=params(limit),
        name="add_shares",
    )(info, *sources * outs, *after)


def join_kernel(column, ways, info_ref, *refs):
    pieces, out_ref, sems = refs[:ways], refs[-2], refs[-1]
    rows = pieces[0].shape[0]
    copies = []
    for step, piece in enumerate(pieces):
        at = pl.multiple_of((info_ref[column] ^ step) * rows, 8)
        copies.append(pltpu.make_async_copy(piece, out_ref.at[pl.ds(at, rows), :], sems.at[step]))
        copies[-1].start()
    for copy in copies:
        copy.wait()


def join(info, column, pieces, after):
    rows, cols = pieces[0].shape
    ways = len(pieces)
    return pl.pallas_call(
        functools.partial(join_kernel, column, ways),
        in_specs=[pl.BlockSpec(memory_space=pltpu.SMEM)] + [ANYWHERE] * ways + unused(after),
        out_specs=pl.BlockSpec(memory_space=pltpu.VMEM),
        out_shape=jax.ShapeDtypeStruct((ways * rows, cols), F32),
        scratch_shapes=[pltpu.SemaphoreType.DMA((ways,))],
        cost_estimate=LITTLE,
        compiler_params=params(SMALL),
        name="join",
    )(info, *pieces, *after)


class Sum:
    def __init__(self, route, keep, *send):
        self.route = route
        self.parts = [keep] + [swap_cores(s) for s in send]
        self.begins = [0] * len(self.parts)
        if len(send) == 2:
            self.begins[2] = 1
        self.shares = [keep.shape[0]]
        for ways in route.ways:
            if self.shares[-1] % (8 * ways):
                break
            self.shares.append(self.shares[-1] // ways)
        self.divided = len(self.shares) - 1
        self.phase = 0
        self.steps = (
            [self.send] * self.divided
            + [self.finish]
            + [self.add] * (route.count - self.divided)
            + [self.join] * (self.divided - 1)
            + [self.swap]
        )

    def advance(self, after):
        return self.steps.pop(0)(after) if self.steps else after

    def send(self, after):
        phase = self.phase
        flips = (1,) if phase < 2 else (1, 0)
        parts = self.parts
        columns = [[self.route.columns.get((begin, phase + 1, flip)) for begin in self.begins] for flip in flips]
        if phase == 0 and len(parts) == 3:
            parts, columns = parts[:2], [[columns[0][0], None]]
            self.parts, self.begins = [self.parts[0], self.parts[2]], [0, 1]
        limit = VMEM if phase < 3 else SMALL
        outs = add_shares(self.route.info, parts, columns, self.shares[phase + 1], after, limit)
        got = self.route.exchange(outs[0], phase, 1)
        if phase < 2:
            self.parts.append(got)
            self.begins.append(phase + 1)
        else:
            self.parts = [outs[1], got]
            self.begins = [phase + 1] * 2
        self.phase += 1
        return (outs[0],)

    def finish(self, after):
        columns = [[self.route.columns.get((begin, self.phase, 0)) for begin in self.begins]]
        (self.piece,) = add_shares(self.route.info, self.parts, columns, self.shares[self.phase], after, SMALL)
        return self.gather()

    def gather(self):
        if self.divided <= self.phase < self.route.count:
            phase = self.phase
        else:
            phase = self.phase = min(self.phase, self.divided) - 1
        self.got = self.route.exchange(self.piece, phase, 1)
        if self.phase == 0:
            self.far_piece = swap_cores(self.piece)
            return (self.piece, (self.far_piece,))
        return (self.piece,)

    def add(self, after):
        parts = [self.piece, self.got]
        (self.piece,) = add_shares(self.route.info, parts, [[None] * 2], self.piece.shape[0], after, SMALL)
        self.phase += 1
        return self.gather()

    def join(self, after):
        self.piece = join(self.route.info, self.route.place_column + self.phase, [self.piece, self.got], after)
        return self.gather()

    def swap(self, after):
        self.sources = (self.piece, self.got, self.far_piece, swap_cores(self.got))
        return (self.got,)


SPACE = 10**11


def spacer_kernel(*refs):
    refs[-1][...] = jnp.zeros_like(refs[-1])


def spacer(after):
    return pl.pallas_call(
        spacer_kernel,
        in_specs=unused(after),
        out_specs=pl.BlockSpec(memory_space=pltpu.VMEM),
        out_shape=jax.ShapeDtypeStruct((8, 128), F32),
        cost_estimate=pl.CostEstimate(flops=SPACE, transcendentals=0, bytes_accessed=1),
        name="spacer",
    )(*after)


class SmallSum:
    def __init__(self, route, values):
        self.route = route
        self.shapes = [v.shape for v in values]
        flat = jnp.concatenate([v.reshape(-1) for v in values])
        self.sum = jnp.pad(flat, (0, -flat.shape[0] % 2048)).reshape(-1, 256)
        self.steps = [functools.partial(route.exchange, phase=p, step=1) for p in range(route.count)] + [swap_cores]
        self.got = self.steps.pop(0)(self.sum)

    def advance(self, after):
        if self.got is None:
            return after
        (self.sum,) = add_shares(self.route.info, [self.sum, self.got], [[None, None]], self.sum.shape[0], after, SMALL)
        self.got = self.steps.pop(0)(self.sum) if self.steps else None
        return (self.sum,)

    def values(self):
        while self.got is not None:
            self.advance(())
        flat, at, out = self.sum.reshape(-1), 0, []
        for shape in self.shapes:
            size = int(np.prod(shape))
            out.append(flat[at : at + size].reshape(shape))
            at += size
        return out


def assemble_kernel(spread, n_outs, info_ref, *refs):
    sources, outs = refs[:4], refs[-n_outs:]
    target, half = pl.program_id(0), pl.program_id(1)
    for n in range(4):
        for t in range(2):

            @pl.when((info_ref[2 + n] == 2 * target + half) & (target == t))
            def _():
                spread(t, sources[n], outs)


def assemble(info, slabs, spread, outs, blocks, sources, group, earlier, after):
    rows, cols = sources[0].shape
    count = slabs // 2 // group

    def source_spec(n):
        def index(t, h, j, i):
            stage, now = i[2 + n], 2 * t + h
            return jnp.where(now < stage, 0, jnp.where(now == stage, j, count - 1)), 0

        return pl.BlockSpec((rows // count, cols), index)

    def out_spec(target, block, row, column):
        def index(t, h, j, i):
            if target is None:
                return row + (2 * t + h) * count + j, column
            return row + jnp.where(t == target, h * count + j, 0 if target else 2 * count - 1), column

        return pl.BlockSpec(block, index)

    return pl.pallas_call(
        functools.partial(assemble_kernel, spread, len(outs)),
        grid_spec=pltpu.PrefetchScalarGridSpec(
            num_scalar_prefetch=1,
            grid=(2, 2, count),
            in_specs=[source_spec(n) for n in range(4)] + [OUTSIDE] * len(earlier) + unused(after),
            out_specs=[out_spec(*b) for b in blocks],
        ),
        out_shape=[jax.ShapeDtypeStruct(s, F32) for s in outs],
        cost_estimate=COST,
        input_output_aliases={5 + i: i for i in range(len(earlier))},
        compiler_params=params(),
        name="assemble",
    )(info, *sources, *earlier, *after)


def ffn_spread(width, size, slabs, group, target, source, outs):
    n, total = (size // 256, width) if target == 0 else (width // 256, size)
    rows = total // slabs
    for s in range(group):
        for j in range(n):
            at = (s * n + j) * rows
            outs[target][s * rows : (s + 1) * rows, j * 256 : (j + 1) * 256] = source[at : at + rows, :]


def attn_spread(columns, slabs, group, target, source, outs):
    n = len(columns)
    rows = source.shape[0] // (group * n)
    for s in range(group):
        for j, (out, column) in enumerate(columns):
            at = (s * n + j) * rows
            outs[out][s * rows : (s + 1) * rows, column : column + source.shape[1]] = source[at : at + rows, :]


ORDER = ("F0", "s0", "F1", "s0", "B0", "s1", "s0", "B1", "s0", "s1", "s2", "s0", "D", "s3", "D", "s1", "s0", "T", "s3", "s1", "s0", "D", "m", "s3", "s2", "D", "s3", "s1", "m", "s0", "D", "s3", "s1", "m", "s3", "s2", "s3", "s1", "m", "s3", "D", "m", "s2", "s2", "s3", "s0", "s1", "s0", "s2", "s2", "s2", "s3", "s1", "s1", "s2", "D", "s2")


def on_device(tokens, lengths, attn_gain, wq, wk, wv, wo, table, ffn_gain, w_in, w_out, out_grad, *, size):
    rows, seq, width = tokens.shape
    buckets, heads = table.shape
    pairs = heads // 2
    ff = w_in.shape[1]
    slabs = 16
    bits = range(size.bit_length() - 1)
    straight = Route(size, [(b,) for b in bits], [(b,) for b in (1, 0, *bits[2:])])
    info = straight.info
    lane_buckets = band_buckets(buckets)
    onehot = np.arange(buckets)[:, None] == lane_buckets[None, :]
    band = jnp.einsum("bh,bm->hm", table, jnp.asarray(onehot, BF16), preferred_element_type=F32)
    flat = lambda a: a.reshape(rows * seq, a.shape[2])
    tall = lambda a: a.reshape(rows, seq, width)
    chunks, sub = 2, 768
    part = ff // chunks
    ends = bucket_of(np.array([-2 * TILE] * TILE + [2 * TILE] * TILE), buckets)
    spread = (np.concatenate([lane_buckets, ends])[:, None] == np.arange(buckets)[None, :]).astype(np.float32)

    h1T, q, k, v, attT, lse, x1, h2 = attn_fwd(tokens, lengths, attn_gain, ffn_gain, wq, wk, wv, wo, band)
    acc, sums, after, ds, diags = (), [], (), [], []
    ffn_grads, attn_grads = (), ()
    def put(which, after):
        nonlocal ffn_grads, attn_grads
        group = 8
        sources, info = sums[which].sources, sums[which].route.info
        if which < chunks:
            ffn_grads = assemble(
                info, slabs, functools.partial(ffn_spread, width, part, slabs, group), [w_in.shape, w_out.shape],
                [(0, (width // slabs * group, part), 0, which), (1, (part // slabs * group, width), which * (slabs // group), 0)],
                sources, group, tuple(ffn_grads), after,
            )
            return (ffn_grads[0],)
        half = which - chunks
        block = width // 2 // slabs * group
        columns = [(0, 0), (1, 0), (2, 0)] + [(3, 0), (3, width // 2)] * (half == 0)
        blocks = [(None, (block, width // 2), 0, half)] * 3 + [(None, (block, width), 0, 0)] * (half == 0)
        made = assemble(
            info, slabs, functools.partial(attn_spread, columns, slabs, group), [wq.shape] * len(blocks), blocks,
            sources, group, tuple(attn_grads[:3]), after,
        )
        attn_grads = list(made) + list(attn_grads[3:])
        return (made[0],)

    late = []
    for at, op in enumerate(ORDER):
        if late:
            after = (*after, *late.pop(0))
        which = int(op[1]) if len(op) > 1 else 0
        if op[0] == "F":
            end = (ffn_gain, flat(x1), attT, wo) if which == chunks - 1 else None
            keep, send, rest, *acc = ffn_chunk(
                info, lengths, slabs, flat(h2), flat(out_grad), w_in, w_out, which * part, part, sub, acc, after, end
            )
            sums.append(Sum(straight, keep, send, rest))
            if end:
                mixed, dres, datt, gwo, ggain2 = acc
            after = (keep,)
        elif op[0] == "B":
            half = pairs // 2
            more = [] if which else [gwo]
            dq, dk, dv, diag, keep, send = attn_bwd(
                info, lengths, slabs, q, k, v, tall(datt), lse, band, h1T, which * half, half, more, after
            )
            ds += [flat(dq), flat(dk), flat(dv)]
            diags.append(diag)
            sums.append(Sum(straight, keep, send))
            after = (keep,)
        elif op == "T":
            tgrad, ggain1 = tokgrad(flat(tokens), dres, attn_gain, ds, wq, wk, wv, after)
            diag = jnp.concatenate(diags).reshape(heads, 6 * TILE)
            gtable = jnp.einsum("hm,mb->bh", diag, jnp.asarray(spread), precision=lax.Precision.HIGHEST)
            small = SmallSum(straight, (ggain1, ggain2, gtable))
            after = (ggain1,)
        elif op == "D":
            after = (spacer(after),)
        elif op == "m":
            after = small.advance(after)
        else:
            after = sums[which].advance(after)
            if isinstance(after[-1], tuple):
                late, after = [(), after[-1]], after[:-1]
            if ORDER[at:].count(op) == 1:
                while sums[which].steps:
                    after = sums[which].advance(after)
                after = put(which, after)
    ggain1, ggain2, gtable = small.values()
    return (tall(mixed), tall(tgrad), ggain1[0], *attn_grads, gtable, ggain2[0], *ffn_grads)


def solution(mesh):
    split = P(("rows", "blk"))
    return jax.shard_map(
        functools.partial(on_device, size=mesh.shape["rows"]),
        mesh=mesh,
        in_specs=(split, split) + (P(),) * 9 + (split,),
        out_specs=(split, split) + (P(),) * 9,
        check_vma=False,
    )
```

```python
import functools
import jax
import jax.numpy as jnp
import numpy as np
from jax import lax
from jax.experimental import pallas as pl
from jax.experimental.pallas import tpu as pltpu
from jax.sharding import PartitionSpec as P

NT = (((1,), (1,)), ((), ()))
TN = (((0,), (0,)), ((), ()))
F32, BF16 = jnp.float32, jnp.bfloat16
TILE = 128
MASKED = -1000000000.0
EPS = 1e-06
far_steps = np.array([12, 16, 23, 32, 46, 64, 91], dtype=np.int32)


def dot(a, b, dims=None):
    if dims is None:
        return jnp.dot(a, b, preferred_element_type=F32)
    return lax.dot_general(a, b, dims, preferred_element_type=F32)


def bucket_of(relative, bucket_count):
    distance = np.abs(relative)
    beyond = np.sum(distance[..., None] >= far_steps, axis=-1)
    inner = np.where(distance < bucket_count // 4, distance, bucket_count // 4 + beyond)
    return np.where(relative > 0, bucket_count // 2, 0) + inner


def band_buckets(bucket_count):
    lanes = np.arange(4 * TILE)
    offsets = np.where(lanes < 2 * TILE, lanes, lanes - 4 * TILE)
    return bucket_of(-offsets, bucket_count)


def segments_along(len_ref, row, shape, axis, start=0):
    at = lax.broadcasted_iota(jnp.int32, shape, axis) + start
    total = jnp.zeros(shape, jnp.int32)
    end = jnp.int32(0)
    for j in range(len_ref.shape[1]):
        end = end + len_ref[row, j]
        total = total + jnp.where(at >= end, 1, 0)
    return total


def fill_mask(len_ref, row, mask_ref, last):
    seq = mask_ref.shape[0]
    of_q = segments_along(len_ref, row, (1, seq), 1)
    of_k = segments_along(len_ref, row, (seq, TILE), 0)
    of_k = jnp.where(of_k < last, of_k, -1)
    for j in range(seq // TILE):
        same = of_k == of_q[:, j * TILE : (j + 1) * TILE]
        mask_ref[:, j * TILE : (j + 1) * TILE] = jnp.where(same, 0.0, MASKED)
    return of_q < last


def band_of(vector):
    wide = jnp.broadcast_to(vector, (TILE, 4 * TILE))
    return pltpu.roll(wide, 0, 1, stride=1, stride_axis=0)


def bias_row(band, vector, ki, count):
    shape = (TILE, TILE)
    tiles = []
    for qi in range(count):
        step = ki - qi
        if step == 0:
            tiles.append(band[:, 0:TILE])
        elif step == -1:
            tiles.append(band[:, TILE : 2 * TILE])
        elif step == 1:
            tiles.append(band[:, 3 * TILE : 4 * TILE])
        elif step < 0:
            tiles.append(jnp.broadcast_to(vector[:, 2 * TILE - 1 : 2 * TILE], shape))
        else:
            tiles.append(jnp.broadcast_to(vector[:, 2 * TILE : 2 * TILE + 1], shape))
    return jnp.concatenate(tiles, axis=1)


def norm_scale(value):
    return lax.rsqrt(jnp.mean(value * value, axis=-1, keepdims=True) + EPS)


def row_of(gain_ref):
    return gain_ref[...].astype(F32).reshape(1, gain_ref.shape[0])


VMEM = 63 * 2**20
ANYWHERE = pl.BlockSpec(memory_space=pl.ANY)
OUTSIDE = pl.BlockSpec(memory_space=pltpu.HBM)
FLOPS = 10**11
LITTLE = pl.CostEstimate(flops=1, transcendentals=0, bytes_accessed=1)
COST = pl.CostEstimate(flops=FLOPS, transcendentals=0, bytes_accessed=1)


def unused(arrays):
    return [OUTSIDE if a.size >= 2**18 else ANYWHERE for a in arrays]


def params(limit=VMEM):
    return pltpu.CompilerParams(vmem_limit_bytes=limit)


def attn_fwd_kernel(
    len_ref, tok_ref, gain1_ref, gain2_ref, wq_ref, wk_ref, wv_ref, wo_ref, band_ref,
    h1T_ref, q_ref, k_ref, v_ref, attT_ref, lse_ref, x1_ref, h2_ref,
    att_ref, mask_ref, s_ref, p_ref,
):
    seq, width = tok_ref.shape[1:]
    pairs = width // TILE
    head = TILE // 2
    row = pl.program_id(0)
    valid = fill_mask(len_ref, row, mask_ref, len_ref.shape[1] - 1)
    tok = tok_ref[0].astype(F32)
    h1 = (tok * norm_scale(tok) * row_of(gain1_ref)).astype(BF16)
    h1T_ref[0] = h1.T
    q_ref[0] = dot(h1, wq_ref[...]).astype(BF16)
    k_ref[0] = dot(h1, wk_ref[...]).astype(BF16)
    v_ref[0] = dot(h1, wv_ref[...]).astype(BF16)
    count = seq // TILE
    low_half = lax.broadcasted_iota(jnp.int32, (1, TILE), 1) < head

    def pair(p, carry):
        lanes = pl.ds(pl.multiple_of(p * TILE, TILE), TILE)
        qp, kp, vp = q_ref[0, :, lanes], k_ref[0, :, lanes], v_ref[0, :, lanes]
        vT = vp.T
        tops = []
        for a in range(2):
            qm = jnp.where(low_half if a == 0 else ~low_half, qp, jnp.zeros_like(qp))
            vector = band_ref[pl.ds(2 * p + a, 1), :]
            band = band_of(vector)
            top = None
            for ki in range(count):
                rows = slice(ki * TILE, (ki + 1) * TILE)
                s = dot(kp[rows], qm, NT) + bias_row(band, vector, ki, count) + mask_ref[rows, :]
                s_ref[a, rows, :] = s
                most = jnp.max(s, axis=0, keepdims=True)
                top = most if top is None else jnp.maximum(top, most)
            tops.append(top)
        totals = []
        for a, top in enumerate(tops):
            total = jnp.zeros_like(top)
            for ki in range(count):
                rows = slice(ki * TILE, (ki + 1) * TILE)
                e = jnp.exp(s_ref[a, rows, :] - top)
                total = total + jnp.sum(e, axis=0, keepdims=True)
                p_ref[a, rows, :] = e.astype(BF16)
            totals.append(total)
        outs = []
        for a, (top, total) in enumerate(zip(tops, totals)):
            o = dot(vT[a * head : (a + 1) * head], p_ref[a])
            outs.append(jnp.where(valid, o / total, 0.0))
            lse_ref[0, pl.ds(2 * p + a, 1), :] = top + jnp.log(total)
        both = jnp.concatenate(outs, axis=0)
        attT_ref[0, lanes, :] = both.astype(BF16)
        att_ref[:, lanes] = both.T.astype(BF16)
        return carry

    lax.fori_loop(0, pairs, pair, 0, unroll=6)
    x1 = tok_ref[0].astype(F32) + dot(att_ref[...], wo_ref[...])
    x1_ref[0] = x1
    h2_ref[0] = (x1 * norm_scale(x1) * row_of(gain2_ref)).astype(BF16)


def attn_fwd(tokens, lengths, gain1, gain2, wq, wk, wv, wo, band):
    rows, seq, width = tokens.shape
    heads = band.shape[0]
    full = lambda a: pl.BlockSpec(a.shape, lambda r, l: (0,) * a.ndim, pipeline_mode=pl.Buffered(1))
    per_row = lambda *s: pl.BlockSpec((1,) + s, lambda r, l: (r,) + (0,) * len(s))
    tall = jax.ShapeDtypeStruct((rows, seq, width), BF16)
    turned = jax.ShapeDtypeStruct((rows, width, seq), BF16)
    return pl.pallas_call(
        attn_fwd_kernel,
        grid_spec=pltpu.PrefetchScalarGridSpec(
            num_scalar_prefetch=1,
            grid=(rows,),
            in_specs=[per_row(seq, width)] + [full(a) for a in (gain1, gain2, wq, wk, wv, wo, band)],
            out_specs=[per_row(width, seq)]
            + [per_row(seq, width)] * 3
            + [per_row(width, seq), per_row(heads, seq), per_row(seq, width), per_row(seq, width)],
            scratch_shapes=[
                pltpu.VMEM((seq, width), BF16),
                pltpu.VMEM((seq, seq), F32),
                pltpu.VMEM((2, seq, seq), F32),
                pltpu.VMEM((2, seq, seq), BF16),
            ],
        ),
        out_shape=[turned, tall, tall, tall, turned]
        + [jax.ShapeDtypeStruct((rows, heads, seq), F32), jax.ShapeDtypeStruct((rows, seq, width), F32), tall],
        cost_estimate=COST,
        compiler_params=params(),
        name="attn_fwd",
    )(lengths, tokens, gain1, gain2, wq, wk, wv, wo, band)


GELU_C = float(np.sqrt(2.0 / np.pi))


def gelu_pair(v):
    v2 = v * v
    t = jnp.tanh(GELU_C * v * (1.0 + 0.044715 * v2))
    half = 0.5 * (1.0 + t)
    slope = half + (0.5 * GELU_C) * v * (1.0 - t * t) * (1.0 + (3 * 0.044715) * v2)
    return v * half, slope


def place(core, mine, other, keep, send, sems):
    both = lambda a, b: [(src, dst, sems.at[n, i]) for n, pairs in enumerate((a, b)) for i, (src, dst) in enumerate(pairs)]
    return [(core == 0, both(mine(keep), other(send))), (core != 0, both(mine(send), other(keep)))]


def run_all(cases, action):
    for condition, copies in cases:

        @pl.when(condition)
        def _():
            for src, dst, sem in copies:
                getattr(pltpu.make_async_copy(src, dst, sem), action)()


def ffn_kernel(steps, slabs, first, last, info_ref, len_ref, h2_ref, dy_ref, win_ref, wout_ref, *refs):
    refs = list(refs)
    acc_in = [] if first else [refs.pop(0), refs.pop(0)]
    if last:
        gain_ref, late = refs[0], refs[1:4]
        keep_ref, *send_refs, mixed_out, dres_out, datt_out, gwo_ref, ggain_ref = refs[-23:-15]
        mix_ref, dtwo_ref, h2T_ref, act_ref, dpre_ref, gin_ref, gout_ref, sems, acc_sems, mixed_ref, dres_ref, datt_ref = refs[-15:-3]
        x1_ref, attT_ref, wo_ref = refs[-3:]
        first_late = acc_sems.shape[0] - 3
        late = [pltpu.make_async_copy(a, b, acc_sems.at[first_late + i]) for i, (a, b) in enumerate(zip(late, refs[-3:]))]
    else:
        keep_ref, *send_refs = refs[-14:-11]
        acc_out = refs[-11:-9]
        mix_ref, dtwo_ref, h2T_ref, act_ref, dpre_ref, gin_ref, gout_ref, sems, acc_sems = refs[-9:]
    step = pl.program_id(0)
    toks, width = h2_ref.shape
    sub = win_ref.shape[1]
    wide, tall = width // 256, sub // 256
    in_rows, out_rows = width // slabs, sub * steps // slabs
    piece = in_rows * tall * steps
    here = slabs // steps
    totals = (mix_ref, dtwo_ref)

    def moves(at):
        core, first_half = info_ref[0], 1 - info_ref[4] % 2
        half = slabs // 2
        block = in_rows * tall
        cases = []
        for c in range(2):
            for f in range(2):
                here_now = (core == c) & (first_half == f)
                copies = []
                for i in range(slabs):
                    src = gin_ref.at[at, i * block : (i + 1) * block, :]
                    dst, row = (keep_ref, i) if c == 0 else (send_refs[0 if i // half == f else 1], i % half)
                    dst = dst.at[pl.ds(pl.multiple_of(row * piece + at * block, 8), block), :]
                    copies.append((src, dst, sems.at[at, 0, i]))
                cases.append((here_now, copies))
                if c == 1:
                    dst = keep_ref.at[pl.ds(pl.multiple_of(at * (here * piece), 8), here * piece), :]
                    cases.append((here_now, [(gout_ref.at[at], dst, sems.at[at, 1, 0])]))
                else:
                    for now in range(2):
                        dst = send_refs[0 if now == f else 1]
                        cases.append((here_now & (at == now), [(gout_ref.at[at], dst, sems.at[at, 1, 0])]))
        return cases

    @pl.when(step == 0)
    def _():
        for i, ref in enumerate(acc_in):
            pltpu.make_async_copy(ref, totals[i], acc_sems.at[i]).start()
        if last:
            for copy in late:
                copy.start()
        h2T_ref[...] = h2_ref[...].T

    pre = dot(h2_ref[...], win_ref[...])
    dact = dot(dy_ref[...], wout_ref[...], NT)
    act, slope = gelu_pair(pre)
    act_ref[...] = act.astype(BF16)
    dpre_ref[...] = (dact * slope).astype(BF16)
    mix = dot(act_ref[...], wout_ref[...])
    dtwo = dot(dpre_ref[...], win_ref[...], NT)

    @pl.when(step == 0)
    def _():
        if first:
            mix_ref[...] = mix
            dtwo_ref[...] = dtwo
        else:
            for i, ref in enumerate(acc_in):
                pltpu.make_async_copy(ref, totals[i], acc_sems.at[i]).wait()
            mix_ref[...] += mix
            dtwo_ref[...] += dtwo

    @pl.when(step > 0)
    def _():
        mix_ref[...] += mix
        dtwo_ref[...] += dtwo

    if not last:

        @pl.when(step == steps - 1)
        def _():
            for i in range(2):
                pltpu.make_async_copy(totals[i], acc_out[i], acc_sems.at[2 + i]).start()

    gout = dot(act_ref[...], dy_ref[...], TN)
    for i in range(here):
        for j in range(wide):
            at = (i * wide + j) * out_rows
            gout_ref[step, at : at + out_rows, :] = gout[i * out_rows : (i + 1) * out_rows, j * 256 : (j + 1) * 256]
    gin = dot(h2T_ref[...], dpre_ref[...])
    for i in range(slabs):
        for j in range(tall):
            at = (i * tall + j) * in_rows
            gin_ref[step, at : at + in_rows, :] = gin[i * in_rows : (i + 1) * in_rows, j * 256 : (j + 1) * 256]
    run_all(moves(step), "start")

    @pl.when(step == steps - 1)
    def _():
        if last:
            for copy in late:
                copy.wait()
            rows = len_ref.shape[0]
            seq = toks // rows
            block = 256
            copies = []
            ggain = None
            for b in range(toks // block):
                here_toks = slice(b * block, (b + 1) * block)
                x1, back = x1_ref[here_toks, :], dtwo_ref[here_toks, :]
                mixed_ref[here_toks, :] = (x1 + mix_ref[here_toks, :]).astype(BF16)
                s = norm_scale(x1)
                g = row_of(gain_ref) * back
                dres = dy_ref[here_toks, :].astype(F32) + s * g - x1 * (s * s * s * jnp.mean(x1 * g, axis=-1, keepdims=True))
                dres_ref[here_toks, :] = dres
                some = jnp.sum(back * x1 * s, axis=0, keepdims=True)
                ggain = some if ggain is None else ggain + some
                dbranch = dres.astype(BF16)
                act_ref[here_toks, :] = dbranch
                datt = dot(dbranch, wo_ref[...], NT)
                seg = segments_along(len_ref, b * block // seq, (block, TILE), 0, b * block % seq)[:, :1]
                datt_ref[here_toks, :] = jnp.where(seg < len_ref.shape[1] - 1, datt, 0.0).astype(BF16)
                for n, (src, dst) in enumerate(((mixed_ref, mixed_out), (dres_ref, dres_out), (datt_ref, datt_out))):
                    copies.append(pltpu.make_async_copy(src.at[here_toks, :], dst.at[here_toks, :], acc_sems.at[4 + 3 * b + n]))
                    copies[-1].start()
            ggain_ref[...] = ggain
            gwo = None
            for r in range(rows):
                part = dot(attT_ref[r], act_ref[r * seq : (r + 1) * seq, :])
                gwo = part if gwo is None else gwo + part
            gwo_ref[...] = gwo
            for copy in copies:
                copy.wait()
        else:
            for i in range(2):
                pltpu.make_async_copy(totals[i], acc_out[i], acc_sems.at[2 + i]).wait()
        for at in range(steps):
            run_all(moves(at), "wait")


def ffn_chunk(info, lengths, slabs, h2, dy, w_in, w_out, start, size, sub, acc, after, rest=None):
    toks, width = h2.shape
    base = start // sub
    steps = size // sub
    piece = width * (sub // 256)
    full = lambda a: pl.BlockSpec(a.shape, lambda s, *_: (0,) * a.ndim, pipeline_mode=pl.Buffered(1))
    f32 = lambda *s: jax.ShapeDtypeStruct(s, F32)
    out_specs = [ANYWHERE] * 3
    out_shape = [f32(steps * piece, 256)] + [f32(steps * piece // 2, 256)] * 2
    scratch = [
        pltpu.VMEM((toks, width), F32),
        pltpu.VMEM((toks, width), F32),
        pltpu.VMEM((width, toks), BF16),
        pltpu.VMEM((toks, sub), BF16),
        pltpu.VMEM((toks, sub), BF16),
        pltpu.VMEM((steps, piece, 256), F32),
        pltpu.VMEM((steps, piece, 256), F32),
        pltpu.SemaphoreType.DMA((steps, 2, slabs)),
        pltpu.SemaphoreType.DMA((7 + 3 * (toks // 256),)),
    ]
    if rest is None:
        rest, gain = (), ()
        out_specs += [ANYWHERE] * 2
        out_shape += [f32(toks, width)] * 2
    else:
        gain, *rest = rest
        gain = (gain,)
        low = jax.ShapeDtypeStruct((toks, width), BF16)
        whole = lambda s: pl.BlockSpec(s.shape, lambda *_: (0,) * len(s.shape), pipeline_mode=pl.Buffered(1))
        gwo, ggain = f32(width, width), f32(1, width)
        out_specs += [ANYWHERE] * 3 + [whole(gwo), whole(ggain)]
        out_shape += [low, f32(toks, width), low, gwo, ggain]
        scratch += [pltpu.VMEM((toks, width), BF16), pltpu.VMEM((toks, width), F32), pltpu.VMEM((toks, width), BF16)]
        scratch += [pltpu.VMEM(a.shape, a.dtype) for a in rest]
    return pl.pallas_call(
        functools.partial(ffn_kernel, steps, slabs, not acc, bool(rest)),
        grid_spec=pltpu.PrefetchScalarGridSpec(
            num_scalar_prefetch=2,
            grid=(steps,),
            in_specs=[
                full(h2),
                full(dy),
                pl.BlockSpec((width, sub), lambda s, *_: (0, base + s)),
                pl.BlockSpec((sub, width), lambda s, *_: (base + s, 0)),
            ]
            + [ANYWHERE] * len(acc)
            + [full(a) for a in gain]
            + [ANYWHERE] * len(rest)
            + unused(after),
            out_specs=out_specs,
            scratch_shapes=scratch,
        ),
        out_shape=out_shape,
        cost_estimate=COST,
        compiler_params=params(),
        name="ffn",
    )(info, lengths, h2, dy, w_in, w_out, *acc, *gain, *rest, *after)


def diagonal_sums(x):
    depth, lanes = x.shape
    total = x[0:8]
    for g in range(8, depth, 8):
        total = total + pltpu.roll(x[g : g + 8], lanes - g, 1)
    at = lax.broadcasted_iota(jnp.int32, (8, lanes), 0)
    for bit in (1, 2, 4):
        total = jnp.where((at & bit) != 0, pltpu.roll(total, lanes - bit, 1), total)
    return jnp.sum(total, axis=0, keepdims=True)


def attn_bwd_kernel(slabs, first, n_more, info_ref, len_ref, q_ref, k_ref, v_ref, do_ref, attT_ref, lse_ref, band_ref, h1T_ref, *refs):
    more = refs[:n_more]
    dq_ref, dk_ref, dv_ref, diag_ref, keep_ref, send_ref = refs[-12:-6]
    mask_ref, low_ref, ds_ref, d_ref, g_ref, sems = refs[-6:]
    pair, pairs = pl.program_id(0), pl.num_programs(0)
    rows, seq = q_ref.shape[:2]
    head = TILE // 2
    count = seq // TILE
    width, cols = h1T_ref.shape[1], g_ref.shape[2]
    stripes = keep_ref.shape[0] * 2 // width
    share = width // 2 // slabs

    def put(j, block):
        for c in range(2):
            for s in range(slabs):
                at, begin = (s * stripes + j) * share, (c * slabs + s) * share
                g_ref[c, at : at + share, :] = block[begin : begin + share]

    @pl.when(pair == 0)
    def _():
        for row in range(rows):
            fill_mask(len_ref, row, mask_ref.at[row], len_ref.shape[1] - 1)

    low_half = lax.broadcasted_iota(jnp.int32, (1, TILE), 1) < head
    bands = []
    for a in range(2):
        vector = band_ref[pl.ds(2 * (first + pair) + a, 1), :]
        bands.append((vector, band_of(vector)))
    sides, sums = [], [{}, {}]
    for n in range(2 * rows):
        row, a = n // 2, n % 2
        qp, kp, vp, dop = q_ref[row], k_ref[row], v_ref[row], do_ref[row]
        dopT = dop.T
        own = low_half if a == 0 else ~low_half
        qm = jnp.where(own, qp, jnp.zeros_like(qp))
        dom = jnp.where(own, dop, jnp.zeros_like(dop))
        vector, band = bands[a]
        lse = lse_ref[row, pl.ds(2 * (first + pair) + a, 1), :]
        part = slice(a * head, (a + 1) * head)
        delta = jnp.sum(attT_ref[row, part, :].astype(F32) * dopT[part].astype(F32), axis=0, keepdims=True)
        near = sums[a]
        for ki in range(count):
            some = slice(ki * TILE, (ki + 1) * TILE)
            s = dot(kp[some], qm, NT) + bias_row(band, vector, ki, count) + mask_ref[row, some, :]
            prob = jnp.exp(s - lse)
            ds = prob * (dot(vp[some], dom, NT) - delta)
            low_ref[n, some, :] = prob.astype(BF16)
            ds_ref[n, some, :] = ds.astype(BF16)
            for qi in range(count):
                step = max(-2, min(2, ki - qi))
                tile = ds[:, qi * TILE : (qi + 1) * TILE]
                near[step] = tile if step not in near else near[step] + tile
        sides.append((qm, dom))
    for a, near in enumerate(sums):
        zero = jnp.zeros((TILE, TILE), F32)
        band = jnp.concatenate([near[0], near[-1], zero, near[1]], axis=1)
        diag_ref[0, a : a + 1, : 4 * TILE] = diagonal_sums(band)
        ends = jnp.concatenate([near[-2], near[2]], axis=1)
        diag_ref[0, a : a + 1, 4 * TILE :] = jnp.sum(ends, axis=0, keepdims=True)
    lanes = pl.ds(pl.multiple_of(pair * TILE, TILE), TILE)
    for row in range(rows):
        kT = k_ref[row].T
        dqT, dk, dv = [], None, None
        for a in range(2):
            n = 2 * row + a
            qm, dom = sides[n]
            dva = dot(low_ref[n], dom)
            dka = dot(ds_ref[n], qm)
            dv = dva if dv is None else dv + dva
            dk = dka if dk is None else dk + dka
            dqT.append(dot(kT[a * head : (a + 1) * head], ds_ref[n]))
        dq = jnp.concatenate(dqT, axis=0).T.astype(BF16)
        dk, dv = dk.astype(BF16), dv.astype(BF16)
        dq_ref[row], dk_ref[row], dv_ref[row] = dq, dk, dv
        for j, d in enumerate((dq, dk, dv)):
            d_ref[j, row, :, lanes] = d

    @pl.when(pair == pairs - 1)
    def _():
        for j in range(3):
            g = None
            for r in range(h1T_ref.shape[0]):
                part = dot(h1T_ref[r], d_ref[j, r])
                g = part if g is None else g + part
            put(j, g)
        for j in range(stripes - 3):
            put(3 + j, more[0][:, j * cols : (j + 1) * cols])
        moves = place(
            info_ref[0], lambda ref: [(g_ref.at[0], ref)], lambda ref: [(g_ref.at[1], ref)], keep_ref, send_ref, sems
        )
        run_all(moves, "start")
        run_all(moves, "wait")


def attn_bwd(info, lengths, slabs, q, k, v, do, attT, lse, band, h1T, first, pairs, more, after):
    rows, seq, width = q.shape
    cols = pairs * TILE
    half = width // 2 * (3 + sum(m.shape[1] // cols for m in more))
    tall = pl.BlockSpec((rows, seq, TILE), lambda p, *_: (0, 0, first + p))
    tall_out = pl.BlockSpec((rows, seq, TILE), lambda p, *_: (0, 0, p))
    full = lambda a: pl.BlockSpec(a.shape, lambda *_: (0,) * a.ndim, pipeline_mode=pl.Buffered(1))
    out = jax.ShapeDtypeStruct((rows, seq, cols), BF16)
    square = lambda dtype: pltpu.VMEM((2 * rows, seq, seq), dtype)
    return pl.pallas_call(
        functools.partial(attn_bwd_kernel, slabs, first, len(more)),
        grid_spec=pltpu.PrefetchScalarGridSpec(
            num_scalar_prefetch=2,
            grid=(pairs,),
            in_specs=[tall] * 4
            + [pl.BlockSpec((rows, TILE, seq), lambda p, *_: (0, first + p, 0)), full(lse), full(band), full(h1T)]
            + [full(m) for m in more]
            + unused(after),
            out_specs=[tall_out] * 3 + [pl.BlockSpec((1, 2, 6 * TILE), lambda p, *_: (p, 0, 0))] + [ANYWHERE] * 2,
            scratch_shapes=[
                pltpu.VMEM((rows, seq, seq), F32),
                square(BF16),
                square(BF16),
                pltpu.VMEM((3, rows, seq, cols), BF16),
                pltpu.VMEM((2, half, cols), F32),
                pltpu.SemaphoreType.DMA((2, 1)),
            ],
        ),
        out_shape=[out] * 3
        + [jax.ShapeDtypeStruct((pairs, 2, 6 * TILE), F32)]
        + [jax.ShapeDtypeStruct((half, cols), F32)] * 2,
        cost_estimate=COST,
        compiler_params=params(),
        name="attn_bwd",
    )(info, lengths, q, k, v, do, attT, lse, band, h1T, *more, *after)


def tokgrad_kernel(halves, tok_ref, dres_ref, gain_ref, wq_ref, wk_ref, wv_ref, *refs):
    out_ref, ggain_ref = refs[-2:]
    step = pl.program_id(0)
    done = None
    for i, w in enumerate((wq_ref, wk_ref, wv_ref)):
        d = jnp.concatenate([refs[h * 3 + i][...] for h in range(halves)], axis=1)
        term = dot(d, w[...], NT)
        done = term if done is None else done + term
    tok = tok_ref[...].astype(F32)
    s = norm_scale(tok)
    g = row_of(gain_ref) * done
    out_ref[...] = (dres_ref[...] + s * g - tok * (s * s * s * jnp.mean(tok * g, axis=-1, keepdims=True))).astype(BF16)
    ggain = jnp.sum(done * tok * s, axis=0, keepdims=True)

    @pl.when(step == 0)
    def _():
        ggain_ref[...] = ggain

    @pl.when(step > 0)
    def _():
        ggain_ref[...] += ggain


def tokgrad(tok, dres, gain, ds, wq, wk, wv, after, block=256):
    toks, width = tok.shape
    full = lambda a: pl.BlockSpec(a.shape, lambda s: (0,) * a.ndim, pipeline_mode=pl.Buffered(1))
    tall = pl.BlockSpec((block, width), lambda s: (s, 0))
    return pl.pallas_call(
        functools.partial(tokgrad_kernel, len(ds) // 3),
        grid=(toks // block,),
        in_specs=[tall, tall, full(gain), full(wq), full(wk), full(wv)]
        + [pl.BlockSpec((block, d.shape[1]), lambda s: (s, 0)) for d in ds]
        + unused(after),
        out_specs=[tall, pl.BlockSpec((1, width), lambda s: (0, 0))],
        out_shape=[jax.ShapeDtypeStruct((toks, width), BF16), jax.ShapeDtypeStruct((1, width), F32)],
        cost_estimate=COST,
        compiler_params=params(),
        name="tokgrad",
    )(tok, dres, gain, wq, wk, wv, *ds, *after)


SMALL = 16 * 2**20


class Route:
    def __init__(self, size, even, odd):
        self.size, self.even, self.odd = size, even, odd
        self.count = len(even)
        self.ways = [1 << len(group) for group in even]
        self.columns = {}
        table = [self.line(r, c) for r in range(size) for c in range(2)]
        device = lax.axis_index("rows") * 2 + lax.axis_index("blk")
        self.info = lax.dynamic_index_in_dim(jnp.asarray(np.array(table, np.int32)), device, 0, keepdims=False)

    def places(self, r, c):
        groups = (self.even, self.odd)[c]
        return [sum(((r >> b) & 1) << (len(group) - 1 - i) for i, b in enumerate(group)) for group in groups]

    def line(self, r, c):
        places, far = self.places(r, c), self.places(r, 1 - c)[0]
        line = [c, r, 2 * c + places[0], 2 * c + 1 - places[0], 2 * (1 - c) + far, 2 * (1 - c) + 1 - far, *places]
        self.place_column = 6
        for end in range(1, self.count + 1):
            for begin in range(end):
                for step in range(self.ways[end - 1]):
                    at = 0
                    for phase in range(begin, end):
                        at = at * self.ways[phase] + (places[phase] ^ (step if phase == end - 1 else 0))
                    self.columns[begin, end, step] = len(line)
                    line.append(at)
        return line

    def exchange(self, x, phase, step):
        def other(r, group):
            for i, b in enumerate(group):
                r ^= ((step >> (len(group) - 1 - i)) & 1) << b
            return r

        moves = [
            (r * 2 + c, other(r, (self.even, self.odd)[c][phase]) * 2 + c) for r in range(self.size) for c in range(2)
        ]
        return lax.ppermute(x, ("rows", "blk"), moves)


def swap_cores(x):
    return lax.ppermute(x, "blk", [(0, 1), (1, 0)])


def add_kernel(count, outs, info_ref, *refs):
    for n in range(outs):
        total = None
        for ref in refs[n * count : (n + 1) * count]:
            total = ref[...] if total is None else total + ref[...]
        refs[-outs + n][...] = total


def add_shares(info, sources, columns, rows, after, limit):
    cols = sources[0].shape[1]
    parts = 1
    while rows // parts * cols > 300000 and rows % (16 * parts) == 0:
        parts *= 2
    block = (rows // parts, cols)

    def spec(source, column):
        if column is None:
            return pl.BlockSpec(block, lambda g, i: (g, 0))
        return pl.BlockSpec(block, lambda g, i: (i[column] * parts + g, 0))

    outs = len(columns)
    return pl.pallas_call(
        functools.partial(add_kernel, len(sources), outs),
        grid_spec=pltpu.PrefetchScalarGridSpec(
            num_scalar_prefetch=1,
            grid=(parts,),
            in_specs=[spec(*pair) for line in columns for pair in zip(sources, line)] + unused(after),
            out_specs=[pl.BlockSpec(block, lambda g, i: (g, 0))] * outs,
        ),
        out_shape=[jax.ShapeDtypeStruct((rows, cols), F32)] * outs,
        cost_estimate=LITTLE,
        compiler_params=params(limit),
        name="add_shares",
    )(info, *sources * outs, *after)


def join_kernel(column, ways, info_ref, *refs):
    pieces, out_ref, sems = refs[:ways], refs[-2], refs[-1]
    rows = pieces[0].shape[0]
    copies = []
    for step, piece in enumerate(pieces):
        at = pl.multiple_of((info_ref[column] ^ step) * rows, 8)
        copies.append(pltpu.make_async_copy(piece, out_ref.at[pl.ds(at, rows), :], sems.at[step]))
        copies[-1].start()
    for copy in copies:
        copy.wait()


def join(info, column, pieces, after):
    rows, cols = pieces[0].shape
    ways = len(pieces)
    return pl.pallas_call(
        functools.partial(join_kernel, column, ways),
        in_specs=[pl.BlockSpec(memory_space=pltpu.SMEM)] + [ANYWHERE] * ways + unused(after),
        out_specs=pl.BlockSpec(memory_space=pltpu.VMEM),
        out_shape=jax.ShapeDtypeStruct((ways * rows, cols), F32),
        scratch_shapes=[pltpu.SemaphoreType.DMA((ways,))],
        cost_estimate=LITTLE,
        compiler_params=params(SMALL),
        name="join",
    )(info, *pieces, *after)


class Sum:
    def __init__(self, route, keep, *send):
        self.route = route
        self.parts = [keep] + [swap_cores(s) for s in send]
        self.begins = [0] * len(self.parts)
        if len(send) == 2:
            self.begins[2] = 1
        self.shares = [keep.shape[0]]
        for ways in route.ways:
            if self.shares[-1] % (8 * ways):
                break
            self.shares.append(self.shares[-1] // ways)
        self.divided = len(self.shares) - 1
        self.phase = 0
        self.steps = (
            [self.send] * self.divided
            + [self.finish]
            + [self.add] * (route.count - self.divided)
            + [self.join] * (self.divided - 1)
            + [self.swap]
        )

    def advance(self, after):
        return self.steps.pop(0)(after) if self.steps else after

    def send(self, after):
        phase = self.phase
        flips = (1,) if phase < 2 else (1, 0)
        parts = self.parts
        columns = [[self.route.columns.get((begin, phase + 1, flip)) for begin in self.begins] for flip in flips]
        if phase == 0 and len(parts) == 3:
            parts, columns = parts[:2], [[columns[0][0], None]]
            self.parts, self.begins = [self.parts[0], self.parts[2]], [0, 1]
        limit = VMEM if phase < 3 else SMALL
        outs = add_shares(self.route.info, parts, columns, self.shares[phase + 1], after, limit)
        got = self.route.exchange(outs[0], phase, 1)
        if phase < 2:
            self.parts.append(got)
            self.begins.append(phase + 1)
        else:
            self.parts = [outs[1], got]
            self.begins = [phase + 1] * 2
        self.phase += 1
        return (outs[0],)

    def finish(self, after):
        columns = [[self.route.columns.get((begin, self.phase, 0)) for begin in self.begins]]
        (self.piece,) = add_shares(self.route.info, self.parts, columns, self.shares[self.phase], after, SMALL)
        return self.gather()

    def gather(self):
        if self.divided <= self.phase < self.route.count:
            phase = self.phase
        else:
            phase = self.phase = min(self.phase, self.divided) - 1
        self.got = self.route.exchange(self.piece, phase, 1)
        if self.phase == 0:
            self.far_piece = swap_cores(self.piece)
            return (self.piece, (self.far_piece,))
        return (self.piece,)

    def add(self, after):
        parts = [self.piece, self.got]
        (self.piece,) = add_shares(self.route.info, parts, [[None] * 2], self.piece.shape[0], after, SMALL)
        self.phase += 1
        return self.gather()

    def join(self, after):
        self.piece = join(self.route.info, self.route.place_column + self.phase, [self.piece, self.got], after)
        return self.gather()

    def swap(self, after):
        self.sources = (self.piece, self.got, self.far_piece, swap_cores(self.got))
        return (self.got,)


SPACE = 10**11


def spacer_kernel(*refs):
    refs[-1][...] = jnp.zeros_like(refs[-1])


def spacer(after):
    return pl.pallas_call(
        spacer_kernel,
        in_specs=unused(after),
        out_specs=pl.BlockSpec(memory_space=pltpu.VMEM),
        out_shape=jax.ShapeDtypeStruct((8, 128), F32),
        cost_estimate=pl.CostEstimate(flops=SPACE, transcendentals=0, bytes_accessed=1),
        name="spacer",
    )(*after)


class SmallSum:
    def __init__(self, route, values):
        self.route = route
        self.shapes = [v.shape for v in values]
        flat = jnp.concatenate([v.reshape(-1) for v in values])
        self.sum = jnp.pad(flat, (0, -flat.shape[0] % 2048)).reshape(-1, 256)
        self.steps = [functools.partial(route.exchange, phase=p, step=1) for p in range(route.count)] + [swap_cores]
        self.got = self.steps.pop(0)(self.sum)

    def advance(self, after):
        if self.got is None:
            return after
        (self.sum,) = add_shares(self.route.info, [self.sum, self.got], [[None, None]], self.sum.shape[0], after, SMALL)
        self.got = self.steps.pop(0)(self.sum) if self.steps else None
        return (self.sum,)

    def values(self):
        while self.got is not None:
            self.advance(())
        flat, at, out = self.sum.reshape(-1), 0, []
        for shape in self.shapes:
            size = int(np.prod(shape))
            out.append(flat[at : at + size].reshape(shape))
            at += size
        return out


def assemble_kernel(spread, n_outs, info_ref, *refs):
    sources, outs = refs[:4], refs[-n_outs:]
    target, half = pl.program_id(0), pl.program_id(1)
    for n in range(4):
        for t in range(2):

            @pl.when((info_ref[2 + n] == 2 * target + half) & (target == t))
            def _():
                spread(t, sources[n], outs)


def assemble(info, slabs, spread, outs, blocks, sources, group, earlier, after):
    rows, cols = sources[0].shape
    count = slabs // 2 // group

    def source_spec(n):
        def index(t, h, j, i):
            stage, now = i[2 + n], 2 * t + h
            return jnp.where(now < stage, 0, jnp.where(now == stage, j, count - 1)), 0

        return pl.BlockSpec((rows // count, cols), index)

    def out_spec(target, block, row, column):
        def index(t, h, j, i):
            if target is None:
                return row + (2 * t + h) * count + j, column
            return row + jnp.where(t == target, h * count + j, 0 if target else 2 * count - 1), column

        return pl.BlockSpec(block, index)

    return pl.pallas_call(
        functools.partial(assemble_kernel, spread, len(outs)),
        grid_spec=pltpu.PrefetchScalarGridSpec(
            num_scalar_prefetch=1,
            grid=(2, 2, count),
            in_specs=[source_spec(n) for n in range(4)] + [OUTSIDE] * len(earlier) + unused(after),
            out_specs=[out_spec(*b) for b in blocks],
        ),
        out_shape=[jax.ShapeDtypeStruct(s, F32) for s in outs],
        cost_estimate=COST,
        input_output_aliases={5 + i: i for i in range(len(earlier))},
        compiler_params=params(),
        name="assemble",
    )(info, *sources, *earlier, *after)


def ffn_spread(width, size, slabs, group, target, source, outs):
    n, total = (size // 256, width) if target == 0 else (width // 256, size)
    rows = total // slabs
    for s in range(group):
        for j in range(n):
            at = (s * n + j) * rows
            outs[target][s * rows : (s + 1) * rows, j * 256 : (j + 1) * 256] = source[at : at + rows, :]


def attn_spread(columns, slabs, group, target, source, outs):
    n = len(columns)
    rows = source.shape[0] // (group * n)
    for s in range(group):
        for j, (out, column) in enumerate(columns):
            at = (s * n + j) * rows
            outs[out][s * rows : (s + 1) * rows, column : column + source.shape[1]] = source[at : at + rows, :]


ORDER = ("F0", "s0", "F1", "s0", "B0", "s1", "s0", "B1", "s0", "s1", "s2", "s0", "D", "s3", "D", "s1", "s0", "T", "s1", "s3", "s0", "D", "m", "s3", "s2", "D", "s3", "s1", "m", "s0", "D", "s3", "s2", "s1", "m", "s3", "s3", "s1", "m", "s3", "D", "m", "s2", "s2", "s3", "s0", "s1", "s0", "s2", "s2", "s2", "s3", "s1", "s1", "s2", "D", "s2")


def on_device(tokens, lengths, attn_gain, wq, wk, wv, wo, table, ffn_gain, w_in, w_out, out_grad, *, size):
    rows, seq, width = tokens.shape
    buckets, heads = table.shape
    pairs = heads // 2
    ff = w_in.shape[1]
    slabs = 16
    bits = range(size.bit_length() - 1)
    straight = Route(size, [(b,) for b in bits], [(b,) for b in (1, 0, *bits[2:])])
    info = straight.info
    lane_buckets = band_buckets(buckets)
    onehot = np.arange(buckets)[:, None] == lane_buckets[None, :]
    band = jnp.einsum("bh,bm->hm", table, jnp.asarray(onehot, BF16), preferred_element_type=F32)
    flat = lambda a: a.reshape(rows * seq, a.shape[2])
    tall = lambda a: a.reshape(rows, seq, width)
    chunks, sub = 2, 768
    part = ff // chunks
    ends = bucket_of(np.array([-2 * TILE] * TILE + [2 * TILE] * TILE), buckets)
    spread = (np.concatenate([lane_buckets, ends])[:, None] == np.arange(buckets)[None, :]).astype(np.float32)

    h1T, q, k, v, attT, lse, x1, h2 = attn_fwd(tokens, lengths, attn_gain, ffn_gain, wq, wk, wv, wo, band)
    acc, sums, after, ds, diags = (), [], (), [], []
    ffn_grads, attn_grads = (), ()
    def put(which, after):
        nonlocal ffn_grads, attn_grads
        group = 8
        sources, info = sums[which].sources, sums[which].route.info
        if which < chunks:
            ffn_grads = assemble(
                info, slabs, functools.partial(ffn_spread, width, part, slabs, group), [w_in.shape, w_out.shape],
                [(0, (width // slabs * group, part), 0, which), (1, (part // slabs * group, width), which * (slabs // group), 0)],
                sources, group, tuple(ffn_grads), after,
            )
            return (ffn_grads[0],)
        half = which - chunks
        block = width // 2 // slabs * group
        columns = [(0, 0), (1, 0), (2, 0)] + [(3, 0), (3, width // 2)] * (half == 0)
        blocks = [(None, (block, width // 2), 0, half)] * 3 + [(None, (block, width), 0, 0)] * (half == 0)
        made = assemble(
            info, slabs, functools.partial(attn_spread, columns, slabs, group), [wq.shape] * len(blocks), blocks,
            sources, group, tuple(attn_grads[:3]), after,
        )
        attn_grads = list(made) + list(attn_grads[3:])
        return (made[0],)

    late = []
    for at, op in enumerate(ORDER):
        if late:
            after = (*after, *late.pop(0))
        which = int(op[1]) if len(op) > 1 else 0
        if op[0] == "F":
            end = (ffn_gain, flat(x1), attT, wo) if which == chunks - 1 else None
            keep, send, rest, *acc = ffn_chunk(
                info, lengths, slabs, flat(h2), flat(out_grad), w_in, w_out, which * part, part, sub, acc, after, end
            )
            sums.append(Sum(straight, keep, send, rest))
            if end:
                mixed, dres, datt, gwo, ggain2 = acc
            after = (keep,)
        elif op[0] == "B":
            half = pairs // 2
            more = [] if which else [gwo]
            dq, dk, dv, diag, keep, send = attn_bwd(
                info, lengths, slabs, q, k, v, tall(datt), attT, lse, band, h1T, which * half, half, more, after
            )
            ds += [flat(dq), flat(dk), flat(dv)]
            diags.append(diag)
            sums.append(Sum(straight, keep, send))
            after = (keep,)
        elif op == "T":
            tgrad, ggain1 = tokgrad(flat(tokens), dres, attn_gain, ds, wq, wk, wv, after)
            diag = jnp.concatenate(diags).reshape(heads, 6 * TILE)
            gtable = jnp.einsum("hm,mb->bh", diag, jnp.asarray(spread), precision=lax.Precision.HIGHEST)
            small = SmallSum(straight, (ggain1, ggain2, gtable))
            after = (ggain1,)
        elif op == "D":
            after = (spacer(after),)
        elif op == "m":
            after = small.advance(after)
        else:
            after = sums[which].advance(after)
            if isinstance(after[-1], tuple):
                late, after = [(), after[-1]], after[:-1]
            if ORDER[at:].count(op) == 1:
                while sums[which].steps:
                    after = sums[which].advance(after)
                after = put(which, after)
    ggain1, ggain2, gtable = small.values()
    return (tall(mixed), tall(tgrad), ggain1[0], *attn_grads, gtable, ggain2[0], *ffn_grads)


def solution(mesh):
    split = P(("rows", "blk"))
    return jax.shard_map(
        functools.partial(on_device, size=mesh.shape["rows"]),
        mesh=mesh,
        in_specs=(split, split) + (P(),) * 9 + (split,),
        out_specs=(split, split) + (P(),) * 9,
        check_vma=False,
    )
```
